32 devices in a mesh: seq: 8 (over z, y), head: 4 (over x, core).
Axes of the slice: x: 2, y: 2, z: 4, core: 2. Of those that a mesh axis runs over, the one named last changes fastest.
Arguments:
- queries: bfloat16 [1024, 8192], P('seq', 'head'), may hold values from -6 to 6
- key_vectors: bfloat16 [1024, 8192], P('seq', 'head'), may hold values from -6 to 6
- value_vectors: bfloat16 [1024, 8192], P('seq', 'head'), may hold values from -6 to 6
- log_decay: float32 [1024, 64], P('seq', 'head'), may hold values from -2 to 0
- doc_ids: int32 [1024], P('seq'), may hold values from 0 to 3, as said below
- head_gain: float32 [8192], P('head'), may hold values from 0.4 to 1.6
- output_weight: bfloat16 [8192, 3072], P('head', 'seq'), may hold values from -0.0625 to 0.0625
- residual: bfloat16 [1024, 3072], P('seq', 'head'), may hold values from -8 to 8
- norm_gain: float32 [3072], replicated, may hold values from 0.4 to 1.6
- routing: int32 [1024, 2], P('seq'), may hold values from 0 to 7, all different within a row; in each aligned block of 128 rows (0 to 127, 128 to 255, ...) at most 64 rows name the same one
- route_weights: float32 [1024, 2], P('seq'), may hold values from 0.1 to 1
- gate_weight: bfloat16 [8, 3072, 4608], P('seq', None, 'head'), may hold values from -0.109375 to 0.109375
- up_weight: bfloat16 [8, 3072, 4608], P('seq', None, 'head'), may hold values from -0.109375 to 0.109375
- down_weight: bfloat16 [8, 4608, 3072], P('seq', 'head'), may hold values from -0.09375 to 0.09375
Outputs:
- mixed: bfloat16 [1024, 3072], P('seq', 'head')
The draws below stay inside these ranges and needn't reach their ends.
Inputs may be any that keep to these rules, and one draw needn't show every extreme that they name: `doc_ids`: ids never fall along the sequence and rise by one where a document starts; every id occurs. `routing`: the two experts of a position differ; among the rows of one index of seq no expert is named more than 64 times.
All inputs are finite; a program needn't handle non-finite values.
Results may differ from the reference program's by a relative error of at most 0.014.
Values may be sent and summed in bfloat16 or wider, within the bound.
No kernel may reach another device: no remote copies, remote signals or barrier semaphores. Data moves between devices by JAX's collectives and lax.ppermute only.
A program may use at most 128 MiB of HBM per device.

```python
import math
import jax
import jax.numpy as jnp
import numpy as np
from jax import lax

D = 3072
HEADS = 64
HD = 128
FFW = 4608
NDOCS = 4
TOK_DEV = 128
EXPERTS = 8
SEQUENCE_SLOTS = 1024
CAP = 64
N_SEQ = 8
N_HEAD = 4


def draw_log_decay(key, part):
    stochastic_subseeds = jax.random.split(jax.random.fold_in(key, 11), 7)
    slow_share = 0.5
    slow_heads = jax.random.uniform(stochastic_subseeds[0], (HEADS,)) < slow_share
    slow_rate = jnp.log(10.0) * jax.random.uniform(stochastic_subseeds[1], (HEADS,), minval=0.1, maxval=0.4) / SEQUENCE_SLOTS
    fast_rate = jnp.log(10.0) / jax.random.uniform(stochastic_subseeds[2], (HEADS,), minval=30.0, maxval=50.0)
    fading_rate = jnp.where(slow_heads, slow_rate, fast_rate)
    noise_magnitude = jax.random.uniform(stochastic_subseeds[3], (SEQUENCE_SLOTS, HEADS), minval=0.5, maxval=1.5)
    block_factor = jnp.exp(jax.random.uniform(stochastic_subseeds[4], (SEQUENCE_SLOTS // TOK_DEV, 1), minval=jnp.log(0.5), maxval=jnp.log(2.0)))
    tile_multiplier = jnp.repeat(block_factor, TOK_DEV, axis=0)
    spike_locations = jax.random.randint(stochastic_subseeds[5], (2,), 0, SEQUENCE_SLOTS)
    objective_entries = jnp.log(jax.random.uniform(stochastic_subseeds[6], (2, 1), minval=0.5, maxval=0.8))
    spike_log_height = jnp.zeros((SEQUENCE_SLOTS, 1), jnp.float32).at[spike_locations].add(objective_entries)
    return (-fading_rate[None, :] * noise_magnitude * tile_multiplier + spike_log_height).astype(jnp.float32)


def draw_doc_ids(key, part):
    shuffled = jax.random.permutation(jax.random.fold_in(key, 37), SEQUENCE_SLOTS - 1)
    starts = (shuffled[:NDOCS - 1] + 1).astype(jnp.int32)
    position = jnp.arange(SEQUENCE_SLOTS, dtype=jnp.int32)
    return jnp.sum((position[:, None] >= starts[None, :]).astype(jnp.int32), axis=1).astype(jnp.int32)


def draw_residual(key, part):
    stochastic_subseeds = jax.random.split(jax.random.fold_in(key, 23), 2)
    base_draw = jax.random.normal(stochastic_subseeds[0], (SEQUENCE_SLOTS, D), jnp.float32)
    noise_magnitude = jnp.exp(jax.random.uniform(stochastic_subseeds[1], (1, D), minval=jnp.log(0.5), maxval=jnp.log(2.0)))
    ramp_scale = 0.6 + 1.2 * jnp.arange(D, dtype=jnp.float32)[None, :] / D
    return jnp.clip(base_draw * noise_magnitude * ramp_scale, -8.0, 8.0).astype(jnp.bfloat16)


def block_scale(key, dims, pieces, least, high):
    level, own = 1.0, jax.random.fold_in(key, 6)
    for dim, shards_of in pieces:
        steps = jnp.exp(jax.random.uniform(jax.random.fold_in(own, dim), (shards_of,), jnp.float32, least / len(pieces), high / len(pieces)))
        level = level * jnp.repeat(steps, dims[dim] // shards_of).reshape([-1 if axis == dim else 1 for axis in range(len(dims))])
    return level


def routed_block(key, own, number, rows, count, top, limit, lean):
    ranking = jax.random.permutation(key, count)
    packed, common = portions_of(count, rows * top, limit, lean, True), portions_of(count, rows * top, limit, lean, False)
    places = jnp.arange(count)

    def named(sizes, rotation):
        used = int((sizes > 0).sum())
        fixed = max(1, used // 4)
        shifted = fixed + (places - fixed + rotation * (used - fixed)) % max(1, count - fixed)
        return jnp.zeros((count,), jnp.int32).at[ranking[jnp.where(places < fixed, places, shifted)]].set(jnp.asarray(sizes, jnp.int32))

    sizes = jnp.where(number % 4 == 0, named(packed, number // 4), named(common, number - number // 4 - 1))
    mixed = jax.random.permutation(jax.random.fold_in(own, 3), count)
    source_of, sink = mixed[0:count // 2 * 2:2], mixed[1:count // 2 * 2:2]
    slack = jnp.minimum(sizes[source_of] - 1, limit - sizes[sink]) // 2
    slack = jnp.where((source_of == ranking[0]) | (sink == ranking[0]) | (sizes[sink] == 0), 0, jnp.maximum(slack, 0))
    shifted = jax.random.randint(jax.random.fold_in(own, 4), (count // 2,), 0, 1 << 20) % (slack + 1)
    sizes = sizes.at[source_of].add(-shifted).at[sink].add(shifted)
    labels = jnp.searchsorted(jnp.cumsum(sizes), jnp.arange(rows * top), side="right").astype(jnp.int32)
    grid = labels.reshape(top, rows).T
    grid = grid[jax.random.permutation(jax.random.fold_in(own, 1), rows)]
    rotation = jax.random.randint(jax.random.fold_in(own, 2), (rows, 1), 0, top)
    return jnp.take_along_axis(grid, (jnp.arange(top)[None, :] + rotation) % top, axis=1)


def portions_of(number_of, total, bound, lean, full):
    portions = [(1 << 20) // math.isqrt(standing ** lean) + 1 for standing in range(1, number_of + 1)]
    largest = bound if full else min(bound, max(-(-total // number_of), total * portions[0] // sum(portions)))
    least = 1 if total - largest >= number_of - 1 else 0
    counts, surplus = [largest] + [least] * (number_of - 1), total - largest - least * (number_of - 1)
    while surplus > 0:
        movable = [i for i in range(1, number_of) if counts[i] < largest] or [i for i in range(1, number_of) if counts[i] < bound]
        whole, left = sum([portions[i] for i in movable]), surplus
        for i in movable:
            more = min(bound - counts[i], max(1, left * portions[i] // whole), surplus)
            counts[i] = counts[i] + more
            surplus = surplus - more
    return np.array(counts)


def gaussian(stream_key, shape, width, most, shards=(), held_as=jnp.bfloat16):
    array = width * jax.random.normal(stream_key, shape, jnp.float32)
    if shards:
        array = array * block_scale(stream_key, shape, shards, -0.22, 0.18)
    return jnp.clip(array, -most, most).astype(held_as)


def setup_inputs(seed: int = 0) -> dict:
    key_of = jax.random.split(jax.random.key(seed), 15)
    queries = gaussian(key_of[0], (SEQUENCE_SLOTS, HEADS * HD), 1.0, 6.0, ((0, 8), (1, 4)))
    key_vectors = gaussian(key_of[1], (SEQUENCE_SLOTS, HEADS * HD), 1.0, 6.0, ((0, 8), (1, 4)))
    value_vectors = gaussian(key_of[2], (SEQUENCE_SLOTS, HEADS * HD), 1.0, 6.0, ((0, 8), (1, 4)))
    log_decay = draw_log_decay(jax.random.fold_in(key_of[14], 71), 0)
    doc_ids = draw_doc_ids(jax.random.fold_in(key_of[14], 71), 0)
    head_gain = jnp.clip(1.0 + 0.12 * jax.random.normal(key_of[5], (HEADS * HD,), jnp.float32), 0.4, 1.6)
    output_weight = gaussian(key_of[6], (HEADS * HD, D), (HEADS * HD) ** -0.5, 0.0625, ((0, 4), (1, 8)))
    residual = draw_residual(jax.random.fold_in(key_of[14], 71), 0)
    norm_gain = jnp.clip(1.0 + 0.12 * jax.random.normal(key_of[8], (D,), jnp.float32), 0.4, 1.6)
    routing_keys = jax.random.split(jax.random.fold_in(key_of[9], 1), SEQUENCE_SLOTS // TOK_DEV)
    routing_turns = jax.random.permutation(jax.random.fold_in(key_of[9], 3), SEQUENCE_SLOTS // TOK_DEV)
    routing = jax.vmap(lambda own, number: routed_block(jax.random.fold_in(key_of[9], 2), own, number, TOK_DEV, EXPERTS, 2, CAP, 2))(routing_keys, routing_turns).reshape((SEQUENCE_SLOTS, 2))
    route_weights = jnp.clip(0.1 + 0.9 * jax.random.uniform(key_of[10], (SEQUENCE_SLOTS, 2), jnp.float32) ** block_scale(key_of[10], (SEQUENCE_SLOTS, 2), ((0, 8),), -0.2, 0.2), 0.1, 1.0)
    gate_weight = gaussian(key_of[11], (EXPERTS, D, FFW), D ** -0.5, 0.109375, ((0, 8), (2, 4)))
    up_weight = gaussian(key_of[12], (EXPERTS, D, FFW), D ** -0.5, 0.109375, ((0, 8), (2, 4)))
    down_weight = gaussian(key_of[13], (EXPERTS, FFW, D), FFW ** -0.5, 0.09375, ((0, 8), (1, 4)))
    return {"queries": queries, "key_vectors": key_vectors, "value_vectors": value_vectors, "log_decay": log_decay, "doc_ids": doc_ids, "head_gain": head_gain, "output_weight": output_weight, "residual": residual, "norm_gain": norm_gain, "routing": routing, "route_weights": route_weights, "gate_weight": gate_weight, "up_weight": up_weight, "down_weight": down_weight}


EPSILON = 1e-06
FULL_PRECISION = lax.Precision.HIGHEST

def reference(queries, key_vectors, value_vectors, log_decay, doc_ids, head_gain, output_weight, residual, norm_gain, routing, route_weights, gate_weight, up_weight, down_weight):
    blocks = SEQUENCE_SLOTS // TOK_DEV
    query_blocks = queries.reshape(blocks, TOK_DEV, HEADS, HD)
    key_blocks = key_vectors.reshape(blocks, TOK_DEV, HEADS, HD)
    value_blocks = value_vectors.reshape(blocks, TOK_DEV, HEADS, HD)
    decay_blocks = log_decay.reshape(blocks, TOK_DEV, HEADS)
    doc_blocks = doc_ids.reshape(blocks, TOK_DEV)

    def advance(carry_pair, block_data):
        carried, last_doc = carry_pair
        query_heads, key_heads, value_heads, decay_log, doc_block = block_data
        decay_sum = jnp.cumsum(decay_log, axis=0)
        decay_rows = decay_sum.T
        gap_matrix = decay_rows[:, :, None] - decay_rows[:, None, :]
        row_index = lax.broadcasted_iota(jnp.int32, (TOK_DEV, TOK_DEV), 0)
        col_index = lax.broadcasted_iota(jnp.int32, (TOK_DEV, TOK_DEV), 1)
        kept_mask = (col_index <= row_index) & (doc_block[:, None] == doc_block[None, :])
        decay_matrix = jnp.where(kept_mask[None], jnp.exp(jnp.minimum(gap_matrix, 0.0)), 0.0)
        scores = jnp.einsum('thd,shd->hts', query_heads.astype(jnp.float32), key_heads.astype(jnp.float32), precision=FULL_PRECISION)
        weighted = (scores * decay_matrix).astype(jnp.bfloat16)
        inside = jnp.einsum('hts,shd->thd', weighted.astype(jnp.float32), value_heads.astype(jnp.float32), precision=FULL_PRECISION)
        doc_float = doc_block.astype(jnp.float32)
        reach_gain = jnp.exp(decay_sum) * (doc_float == last_doc).astype(jnp.float32)[:, None]
        outside = jnp.einsum('thd,hde->the', query_heads.astype(jnp.float32), carried, precision=FULL_PRECISION) * reach_gain[:, :, None]
        tail_gain = jnp.exp(decay_sum[-1][None, :] - decay_sum) * (doc_block == doc_block[-1]).astype(jnp.float32)[:, None]
        own_state = jnp.einsum('thd,the->hde', key_heads.astype(jnp.float32) * tail_gain[:, :, None], value_heads.astype(jnp.float32), precision=FULL_PRECISION)
        through = jnp.exp(decay_sum[-1]) * ((doc_block[0] == doc_block[-1]) & (doc_float[0] == last_doc)).astype(jnp.float32)
        new_state = through[:, None, None] * carried + own_state
        return ((new_state, doc_float[-1]), inside + outside)
    start_pair = (jnp.zeros((HEADS, HD, HD), jnp.float32), jnp.asarray(-1.0, dtype=jnp.float32))
    _, heads_raw = lax.scan(advance, start_pair, (query_blocks, key_blocks, value_blocks, decay_blocks, doc_blocks))
    heads_raw = heads_raw.reshape(SEQUENCE_SLOTS, HEADS, HD)
    inv_norm = lax.rsqrt(lax.optimization_barrier(jnp.mean(heads_raw * heads_raw, axis=2, keepdims=True)) + EPSILON)
    attended = ((heads_raw * inv_norm).reshape(SEQUENCE_SLOTS, HEADS * HD) * head_gain).astype(jnp.bfloat16)
    projected = jnp.dot(attended, output_weight, preferred_element_type=jnp.float32)
    middle = lax.optimization_barrier((residual.astype(jnp.float32) + projected).astype(jnp.bfloat16))
    middle_float = middle.astype(jnp.float32)
    row_norm = lax.rsqrt(lax.optimization_barrier(jnp.mean(middle_float * middle_float, axis=1, keepdims=True)) + EPSILON)
    normed = (middle_float * row_norm * norm_gain).astype(jnp.bfloat16)
    capacity = N_SEQ * CAP
    flat_ids = routing.reshape(-1)
    hit_table = (flat_ids[:, None] == jnp.arange(EXPERTS, dtype=jnp.int32)[None, :]).astype(jnp.int32)
    slot_rank = lax.optimization_barrier(jnp.sum((jnp.cumsum(hit_table, axis=0) - 1) * hit_table, axis=1)).astype(jnp.int32)
    slot_place = (flat_ids * capacity + slot_rank).astype(jnp.int32)
    owner_row = (jnp.arange(2 * SEQUENCE_SLOTS, dtype=jnp.int32) // 2).astype(jnp.int32)
    slot_table = jnp.full((EXPERTS * capacity,), SEQUENCE_SLOTS, jnp.int32).at[slot_place].set(owner_row)
    padded = jnp.concatenate([normed, jnp.zeros((1, D), jnp.bfloat16)], axis=0)
    group_size = FFW // N_HEAD

    def serve(inputs):
        slot_rows, gate_matrix, up_matrix, down_matrix = inputs
        row_block = padded[slot_rows]
        accumulated = jnp.zeros((slot_rows.shape[0], D), jnp.float32)
        for part_index in range(N_HEAD):
            group_start = part_index * group_size
            gate_proj = jnp.dot(row_block, gate_matrix[:, group_start:group_start + group_size], preferred_element_type=jnp.float32)
            up_proj = jnp.dot(row_block, up_matrix[:, group_start:group_start + group_size], preferred_element_type=jnp.float32)
            hidden = (jax.nn.silu(gate_proj) * up_proj).astype(jnp.bfloat16)
            piece_out = jnp.dot(hidden, down_matrix[group_start:group_start + group_size], preferred_element_type=jnp.float32)
            accumulated = accumulated + piece_out.astype(jnp.bfloat16).astype(jnp.float32)
        return accumulated
    served = lax.map(serve, (slot_table.reshape(EXPERTS, capacity), gate_weight, up_weight, down_weight))
    picked = served.reshape(EXPERTS * capacity, D)[slot_place]
    expert_sum = lax.optimization_barrier(jnp.sum(picked.reshape(SEQUENCE_SLOTS, 2, D) * route_weights[:, :, None], axis=1))
    return (middle_float + expert_sum).astype(jnp.bfloat16)
```

```python
import jax
import jax.numpy as jnp
from jax import lax
from jax.sharding import PartitionSpec as P

EPSILON = 1e-06
CORES = 2
F32 = jnp.float32
BF16 = jnp.bfloat16


def permute_seq(value, move):
    count = lax.axis_size("seq")
    return lax.ppermute(value, "seq", [(source, move(source)) for source in range(count)])


def permute_head(value, move):
    count = lax.axis_size("head")
    return lax.ppermute(value, "head", [(source, move(source)) for source in range(count)])


def pick(stack, index, axis=0):
    return lax.dynamic_index_in_dim(stack, index, axis, keepdims=False)


def shards(
    queries,
    key_vectors,
    value_vectors,
    log_decay,
    doc_ids,
    head_gain,
    output_weight,
    residual,
    norm_gain,
    routing,
    route_weights,
    gate_weight,
    up_weight,
    down_weight,
):
    tokens, heads = log_decay.shape
    hw = queries.shape[1] // heads
    n_seq, n_head = lax.axis_size("seq"), lax.axis_size("head")
    ny, nz, nx = n_seq // n_head, n_head, n_head // CORES
    s, h = lax.axis_index("seq"), lax.axis_index("head")
    z, y = s // ny, s % ny
    x, c = h // CORES, h % CORES
    part = residual.shape[1]
    model_width = part * n_head

    cols = output_weight.shape[1]
    w_z = jnp.zeros((output_weight.shape[0], ny * cols), BF16)
    w_z = lax.dynamic_update_slice(w_z, output_weight, (0, y * cols))
    for k in range(1, ny):
        got = permute_seq(output_weight, lambda q, k=k: q // ny * ny + (q % ny - k) % ny)
        w_z = lax.dynamic_update_slice(w_z, got, (0, (y + k) % ny * cols))

    qh = queries.reshape(tokens, heads, hw)
    kh = key_vectors.reshape(tokens, heads, hw)
    vh = value_vectors.reshape(tokens, heads, hw)
    row = lax.broadcasted_iota(jnp.int32, (tokens, tokens), 0)
    col = lax.broadcasted_iota(jnp.int32, (tokens, tokens), 1)
    decay_sum = jnp.dot(
        (col <= row).astype(F32), log_decay, precision=lax.Precision.HIGHEST
    )
    tail = jnp.exp(decay_sum[-1][None, :] - decay_sum) * (
        doc_ids == doc_ids[-1]
    ).astype(F32)[:, None]
    own_state = jnp.einsum(
        "thd,the->hde",
        (kh.astype(F32) * tail[:, :, None]).astype(BF16),
        vh,
        preferred_element_type=F32,
    )
    own_gain = jnp.exp(decay_sum[-1]) * (doc_ids[0] == doc_ids[-1]).astype(F32)

    rows = heads * hw // n_seq
    hc = max(1, rows // hw)
    extra = -(-(2 * hc + 2) // 16) * 16
    chunk_gain = jnp.repeat(own_gain, hw).reshape(n_seq, hc, rows // hc)[:, :, 0]
    gain_hi = chunk_gain.astype(BF16)
    gain_lo = (chunk_gain - gain_hi.astype(F32)).astype(BF16)
    first = jnp.full((n_seq, 1), doc_ids[0].astype(BF16))
    last = jnp.full((n_seq, 1), doc_ids[-1].astype(BF16))
    notes = jnp.concatenate([gain_hi, gain_lo, first, last], axis=1)
    notes = jnp.pad(notes, ((0, 0), (0, extra - notes.shape[1])))
    notes = jnp.broadcast_to(notes[:, :, None], (n_seq, extra, hw))
    payload = jnp.concatenate(
        [own_state.astype(BF16).reshape(n_seq, rows, hw), notes], axis=1
    )
    blocks = lax.all_to_all(payload, "seq", split_axis=0, concat_axis=0, tiled=True)
    states = blocks[:, :rows].astype(F32).reshape(n_seq, hc, rows // hc, hw)
    info = blocks[:, rows:, 0].astype(F32)
    gains = info[:, :hc] + info[:, hc : 2 * hc]
    firsts, lasts = info[:, 2 * hc], info[:, 2 * hc + 1]
    entered = [jnp.zeros_like(states[0])]
    for b in range(1, n_seq):
        before = states[b - 1] + gains[b - 1][:, None, None] * entered[-1]
        entered.append(before * (firsts[b] == lasts[b - 1]).astype(F32))
    back = jnp.stack(entered).astype(BF16).reshape(n_seq, rows, hw)
    carried = lax.all_to_all(back, "seq", split_axis=0, concat_axis=0, tiled=True)
    carried = carried.reshape(heads, hw, hw)

    decay_rows = decay_sum.T
    gap = decay_rows[:, :, None] - decay_rows[:, None, :]
    kept = (col <= row) & (doc_ids[:, None] == doc_ids[None, :])
    decay_matrix = jnp.where(kept[None], jnp.exp(jnp.minimum(gap, 0.0)), 0.0)
    scores = jnp.einsum("thd,shd->hts", qh, kh, preferred_element_type=F32)
    weighted = (scores * decay_matrix).astype(BF16)
    inside = jnp.einsum("hts,shd->thd", weighted, vh, preferred_element_type=F32)
    reach = jnp.exp(decay_sum) * (doc_ids == doc_ids[0]).astype(F32)[:, None]
    outside = jnp.einsum("thd,hde->the", qh, carried, preferred_element_type=F32)
    heads_raw = inside + outside * reach[:, :, None]
    inv_norm = lax.rsqrt(jnp.mean(heads_raw * heads_raw, axis=2, keepdims=True) + EPSILON)
    attended = ((heads_raw * inv_norm).reshape(tokens, heads * hw) * head_gain).astype(BF16)

    products = []
    for k in range(nz):
        rows_k = attended
        if k:
            rows_k = permute_seq(
                attended, lambda q, k=k: (q // ny - k) % nz * ny + q % ny
            )
        products.append(jnp.dot(rows_k, w_z, preferred_element_type=F32).astype(BF16))
    products = jnp.stack(products)
    total = pick(products, (h - z) % nz).astype(F32)
    for m in range(1, n_head):
        sent = pick(products, (h + m - z) % nz)
        total = total + permute_head(sent, lambda q, m=m: (q + m) % n_head).astype(F32)
    spots = [
        ((zz * ny + yy) * n_head + hh, (hh * ny + yy) * n_head + zz)
        for zz in range(nz)
        for yy in range(ny)
        for hh in range(n_head)
    ]
    summed = lax.ppermute(total.astype(BF16), ("seq", "head"), spots).astype(F32)
    middle = lax.optimization_barrier((summed + residual.astype(F32)).astype(BF16))

    experts = n_seq
    capacity = 4 * tokens // experts
    flat_ids = routing.reshape(-1)
    hits = (flat_ids[:, None] == jnp.arange(experts, dtype=jnp.int32)[None, :]).astype(F32)
    pair_row = lax.broadcasted_iota(jnp.int32, (2 * tokens, 2 * tokens), 0)
    pair_col = lax.broadcasted_iota(jnp.int32, (2 * tokens, 2 * tokens), 1)
    earlier = jnp.dot((pair_col < pair_row).astype(F32), hits)
    rank = jnp.sum(earlier * hits, axis=1).astype(jnp.int32)
    place = (flat_ids * capacity + rank).reshape(tokens, 2)
    slots = jnp.arange(experts * capacity, dtype=jnp.int32)
    here = place[:, :, None] == slots[None, None, :]
    take = jnp.any(here, axis=1).astype(BF16)
    mix = jnp.sum(jnp.where(here, route_weights[:, :, None], 0.0), axis=1)

    outgoing = lax.dot_general(
        take, middle, (((0,), (0,)), ((), ())), preferred_element_type=F32
    ).astype(BF16)
    got = lax.all_to_all(
        outgoing.reshape(experts, capacity, part), "seq", split_axis=0, concat_axis=0, tiled=True
    ).reshape(experts * capacity, part)
    x_all = jnp.zeros((experts * capacity, model_width), BF16)
    pieces = [(h, got)]
    for m in range(1, nx):
        far = permute_head(got, lambda q, m=m: (q - m * CORES) % n_head)
        pieces.append(((h + m * CORES) % n_head, far))
    for owner, piece in list(pieces):
        for m in range(1, CORES):
            near = permute_head(piece, lambda q, m=m: q // CORES * CORES + (q % CORES - m) % CORES)
            pieces.append((owner // CORES * CORES + (owner % CORES + m) % CORES, near))
    for owner, piece in pieces:
        x_all = lax.dynamic_update_slice(x_all, piece, (0, owner * part))
    x_float = x_all.astype(F32)
    row_norm = lax.rsqrt(jnp.mean(x_float * x_float, axis=1, keepdims=True) + EPSILON)
    normed = (x_float * row_norm * norm_gain).astype(BF16)
    gate_proj = jnp.dot(normed, gate_weight[0], preferred_element_type=F32)
    up_proj = jnp.dot(normed, up_weight[0], preferred_element_type=F32)
    hidden = (jax.nn.silu(gate_proj) * up_proj).astype(BF16)
    result = jnp.dot(hidden, down_weight[0], preferred_element_type=F32).astype(BF16)

    result = result.reshape(experts * capacity, nx, CORES, part)
    near_sum = pick(result, c, 2).astype(F32)
    for m in range(1, CORES):
        sent = pick(result, (c + m) % CORES, 2)
        near_sum = near_sum + permute_head(
            sent, lambda q, m=m: q // CORES * CORES + (q % CORES + m) % CORES
        ).astype(F32)
    near_half = near_sum.astype(BF16)
    far_sum = pick(near_sum, x, 1)
    for m in range(1, nx):
        sent = pick(near_half, (x + m) % nx, 1)
        far_sum = far_sum + permute_head(sent, lambda q, m=m: (q + m * CORES) % n_head).astype(F32)
    returned = lax.all_to_all(
        far_sum.astype(BF16).reshape(experts, capacity, part),
        "seq",
        split_axis=0,
        concat_axis=0,
        tiled=True,
    ).reshape(experts * capacity, part)
    expert_sum = jnp.dot(
        mix, returned.astype(F32), precision=lax.Precision.HIGHEST, preferred_element_type=F32
    )
    return (middle.astype(F32) + expert_sum).astype(BF16)


def solution(mesh):
    placed = (
        P("seq", "head"),
        P("seq", "head"),
        P("seq", "head"),
        P("seq", "head"),
        P("seq"),
        P("head"),
        P("head", "seq"),
        P("seq", "head"),
        P(),
        P("seq", None),
        P("seq", None),
        P("seq", None, "head"),
        P("seq", None, "head"),
        P("seq", "head", None),
    )
    return jax.shard_map(
        shards, mesh=mesh, in_specs=placed, out_specs=P("seq", "head"), check_vma=False
    )
```

```python
import functools
import math

import jax
import jax.numpy as jnp
from jax import lax
from jax.experimental import pallas as pl
from jax.experimental.pallas import tpu as pltpu
from jax.sharding import PartitionSpec as P

EPSILON = 1e-06
CORES = 2
HALVES = 2
F32 = jnp.float32
BF16 = jnp.bfloat16
HIGHEST = lax.Precision.HIGHEST
VMEM_BYTES = 48 * 1024 * 1024


def permute_seq(value, move):
    count = lax.axis_size("seq")
    return lax.ppermute(value, "seq", [(source, move(source)) for source in range(count)])


def permute_head(value, move):
    count = lax.axis_size("head")
    return lax.ppermute(value, "head", [(source, move(source)) for source in range(count)])


def pick(stack, index, axis=0):
    return lax.dynamic_index_in_dim(stack, index, axis, keepdims=False)


def doc_column(doc):
    count = doc.shape[1]
    return jnp.broadcast_to(doc, (count, count)).T


def chunk_plan(heads, hw, n_seq):
    rows = heads * hw // n_seq
    held = max(1, rows // hw)
    extra = -(-(2 * held + 2) // 16) * 16
    return rows, held, extra


def state_kernel(doc_ref, decay_ref, k_ref, v_ref, out_ref, sum_ref):
    tokens, heads = decay_ref.shape
    n_seq, _, hw = out_ref.shape
    rows, held, extra = chunk_plan(heads, hw, n_seq)
    doc = doc_ref[...].astype(F32)
    row = lax.broadcasted_iota(jnp.int32, (tokens, tokens), 0)
    col = lax.broadcasted_iota(jnp.int32, (tokens, tokens), 1)
    sums = jnp.dot(
        (col <= row).astype(F32), decay_ref[...], precision=HIGHEST, preferred_element_type=F32
    )
    sum_ref[...] = sums
    final = sums[tokens - 1 :, :]
    last = doc[:, tokens - 1 :]
    tail = jnp.exp(final - sums) * (doc_column(doc)[:, :1] == last).astype(F32)
    gain = jnp.exp(final) * (doc[:, :1] == last).astype(F32)
    for i in range(heads):
        lanes = slice(i * hw, (i + 1) * hw)
        faded = (k_ref[:, lanes].astype(F32) * tail[:, i : i + 1]).astype(BF16)
        state = lax.dot_general(
            faded, v_ref[:, lanes], (((0,), (0,)), ((), ())), preferred_element_type=F32
        ).astype(BF16)
        if rows >= hw:
            out_ref[i // held, i % held * hw : (i % held + 1) * hw, :] = state
        else:
            for j in range(hw // rows):
                out_ref[i * (hw // rows) + j, :rows, :] = state[j * rows : (j + 1) * rows]
    line = lax.broadcasted_iota(jnp.int32, (extra, hw), 0)
    for q in range(n_seq):
        note = jnp.where(line == 2 * held, doc[:, :1], 0.0)
        note = jnp.where(line == 2 * held + 1, last, note)
        for j in range(held):
            i = q * rows // hw + j
            whole = gain[:, i : i + 1]
            high = whole.astype(BF16).astype(F32)
            note = jnp.where(line == j, high, note)
            note = jnp.where(line == held + j, whole - high, note)
        out_ref[q, rows:, :] = note.astype(BF16)


def scan_kernel(blocks_ref, out_ref):
    n_seq, rows, hw = out_ref.shape
    held = max(1, rows // hw)
    part = rows // held
    for j in range(held):
        running = jnp.zeros((part, hw), F32)
        out_ref[0, j * part : (j + 1) * part, :] = running.astype(BF16)
        for b in range(1, n_seq):
            notes = blocks_ref[b - 1, rows:, :].astype(F32)
            gain = notes[j : j + 1] + notes[held + j : held + j + 1]
            first = blocks_ref[b, rows:, :].astype(F32)[2 * held : 2 * held + 1]
            joined = (first == notes[2 * held + 1 : 2 * held + 2]).astype(F32)
            state = blocks_ref[b - 1, j * part : (j + 1) * part, :].astype(F32)
            running = (state + gain * running) * joined
            out_ref[b, j * part : (j + 1) * part, :] = running.astype(BF16)


def inside_kernel(doc_ref, sum_ref, sum_rows_ref, q_ref, k_ref, v_ref, out_ref):
    tokens, heads = sum_ref.shape
    hw = q_ref.shape[1] // heads
    doc = doc_ref[...].astype(F32)
    row = lax.broadcasted_iota(jnp.int32, (tokens, tokens), 0)
    col = lax.broadcasted_iota(jnp.int32, (tokens, tokens), 1)
    kept = (col <= row) & (doc_column(doc) == doc)
    for i in range(heads):
        lanes = slice(i * hw, (i + 1) * hw)
        gap = sum_ref[:, i : i + 1] - sum_rows_ref[i : i + 1, :]
        fade = jnp.where(kept, jnp.exp(jnp.minimum(gap, 0.0)), 0.0)
        scores = lax.dot_general(
            q_ref[:, lanes], k_ref[:, lanes], (((1,), (1,)), ((), ())), preferred_element_type=F32
        )
        out_ref[:, lanes] = jnp.dot(
            (scores * fade).astype(BF16), v_ref[:, lanes], preferred_element_type=F32
        )


def outside_kernel(doc_ref, sum_ref, q_ref, carried_ref, inside_ref, gain_ref, out_ref):
    tokens, heads = sum_ref.shape
    hw = q_ref.shape[1] // heads
    doc = doc_ref[...].astype(F32)
    reach = jnp.exp(sum_ref[...]) * (doc_column(doc)[:, :1] == doc[:, :1]).astype(F32)
    for i in range(heads):
        lanes = slice(i * hw, (i + 1) * hw)
        outside = jnp.dot(q_ref[:, lanes], carried_ref[i], preferred_element_type=F32)
        raw = inside_ref[:, lanes] + outside * reach[:, i : i + 1]
        scale = lax.rsqrt(jnp.mean(raw * raw, axis=1, keepdims=True) + EPSILON)
        out_ref[:, lanes] = (raw * scale * gain_ref[:, lanes]).astype(BF16)


def expert_kernel(n_head, steps, owner_ref, *refs):
    pieces = refs[:n_head]
    gain_ref, gate_ref, up_ref, down_ref, sent_ref, kept_ref, rows_ref, hidden_ref = refs[n_head:]
    part = pieces[0].shape[1]
    width = gate_ref.shape[2]
    step = pl.program_id(0)

    @pl.when(step == 0)
    def _():
        squares = 0.0
        for piece in pieces:
            value = piece[...].astype(F32)
            squares = squares + jnp.sum(value * value, axis=1, keepdims=True)
        scale = lax.rsqrt(squares / (part * n_head) + EPSILON)
        for i, piece in enumerate(pieces):
            lanes = pl.ds(pl.multiple_of(owner_ref[i] * part, 128), part)
            value = piece[...].astype(F32) * scale * gain_ref[:, lanes]
            rows_ref[:, lanes] = value.astype(BF16)

    @pl.when(step < steps)
    def _():
        gate = jnp.dot(rows_ref[...], gate_ref[0], preferred_element_type=F32)
        up = jnp.dot(rows_ref[...], up_ref[0], preferred_element_type=F32)
        hidden = (gate / (1.0 + jnp.exp(-gate)) * up).astype(BF16)
        if steps == 1:
            hidden_ref[...] = hidden
        else:
            hidden_ref[:, pl.ds(pl.multiple_of(step * width, 128), width)] = hidden

    @pl.when((step >= steps) & (step < steps + n_head // CORES))
    def _():
        sent_ref[0] = jnp.dot(
            hidden_ref[...], down_ref[0], preferred_element_type=F32
        ).astype(BF16)

    @pl.when(step >= steps + n_head // CORES)
    def _():
        kept_ref[0] = jnp.dot(
            hidden_ref[...], down_ref[0], preferred_element_type=F32
        ).astype(BF16)


def expert_call(owners, pieces, norm_gain, gate_weight, up_weight, down_weight):
    n_head = len(pieces)
    count, part = pieces[0].shape
    _, depth, units = gate_weight.shape
    width = units
    for tried in (384, 256, 128):
        if units % tried == 0:
            width = tried
            break
    steps, nx = units // width, n_head // CORES
    whole = lambda shape: pl.BlockSpec(shape, lambda i, o: (0,) * len(shape))
    grid_spec = pltpu.PrefetchScalarGridSpec(
        num_scalar_prefetch=1,
        grid=(steps + n_head,),
        in_specs=[whole((count, part))] * n_head
        + [
            whole((1, depth)),
            pl.BlockSpec((1, depth, width), lambda i, o: (0, 0, jnp.minimum(i, steps - 1))),
            pl.BlockSpec((1, depth, width), lambda i, o: (0, 0, jnp.minimum(i, steps - 1))),
            pl.BlockSpec(
                (1, units, part), lambda i, o: (0, 0, o[n_head + jnp.maximum(i - steps, 0)])
            ),
        ],
        out_specs=[
            pl.BlockSpec((1, count, part), lambda i, o: (jnp.clip(i - steps, 0, nx - 1), 0, 0)),
            pl.BlockSpec(
                (1, count, part), lambda i, o: (jnp.clip(i - steps - nx, 0, n_head - nx - 1), 0, 0)
            ),
        ],
        scratch_shapes=[pltpu.VMEM((count, depth), BF16), pltpu.VMEM((count, units), BF16)],
    )
    return pl.pallas_call(
        functools.partial(expert_kernel, n_head, steps),
        grid_spec=grid_spec,
        out_shape=[
            jax.ShapeDtypeStruct((nx, count, part), BF16),
            jax.ShapeDtypeStruct((n_head - nx, count, part), BF16),
        ],
        compiler_params=pltpu.CompilerParams(vmem_limit_bytes=VMEM_BYTES),
        cost_estimate=pl.CostEstimate(
            flops=6 * count * depth * units,
            bytes_accessed=6 * depth * units + 4 * count * depth,
            transcendentals=count * units,
        ),
        name="expert",
    )(owners, *pieces, norm_gain.reshape(1, depth), gate_weight, up_weight, down_weight)


def local_call(kernel, name, out_shape, flops, *operands):
    many = isinstance(out_shape, list)
    shapes = out_shape if many else [out_shape]
    sizes = [a.size * a.dtype.itemsize for a in operands]
    sizes += [math.prod(o.shape) * o.dtype.itemsize for o in shapes]
    return pl.pallas_call(
        kernel,
        out_shape=out_shape,
        compiler_params=pltpu.CompilerParams(vmem_limit_bytes=VMEM_BYTES),
        cost_estimate=pl.CostEstimate(flops=flops, bytes_accessed=sum(sizes), transcendentals=0),
        name=name,
    )(*operands)


def shards(
    queries,
    key_vectors,
    value_vectors,
    log_decay,
    doc_ids,
    head_gain,
    output_weight,
    residual,
    norm_gain,
    routing,
    route_weights,
    gate_weight,
    up_weight,
    down_weight,
):
    tokens, heads = log_decay.shape
    hw = queries.shape[1] // heads
    n_seq, n_head = lax.axis_size("seq"), lax.axis_size("head")
    ny, nz, nx = n_seq // n_head, n_head, n_head // CORES
    s, h = lax.axis_index("seq"), lax.axis_index("head")
    z, y = s // ny, s % ny
    x, c = h // CORES, h % CORES
    part = residual.shape[1]
    model_width = part * n_head

    cols = output_weight.shape[1]
    w_z = jnp.zeros((output_weight.shape[0], ny * cols), BF16)
    w_z = lax.dynamic_update_slice(w_z, output_weight, (0, y * cols))
    for k in range(1, ny):
        got = permute_seq(output_weight, lambda q, k=k: q // ny * ny + (q % ny - k) % ny)
        w_z = lax.dynamic_update_slice(w_z, got, (0, (y + k) % ny * cols))

    struct = jax.ShapeDtypeStruct
    doc_row = doc_ids.reshape(1, tokens)
    rows, held, extra = chunk_plan(heads, hw, n_seq)
    work = 2 * tokens * hw * hw * heads
    payload, decay_sum = local_call(
        state_kernel,
        "block_state",
        [struct((n_seq, rows + extra, hw), BF16), struct((tokens, heads), F32)],
        work,
        doc_row,
        log_decay,
        key_vectors,
        value_vectors,
    )
    blocks = lax.all_to_all(payload, "seq", split_axis=0, concat_axis=0, tiled=True)
    back = local_call(scan_kernel, "carry", struct((n_seq, rows, hw), BF16), work, blocks)
    back, w_z = lax.optimization_barrier((back, w_z))
    carried = lax.all_to_all(back, "seq", split_axis=0, concat_axis=0, tiled=True)
    carried = carried.reshape(heads, hw, hw)
    inside = local_call(
        inside_kernel,
        "inside",
        struct((tokens, heads * hw), F32),
        2 * work,
        doc_row,
        decay_sum,
        decay_sum.T,
        queries,
        key_vectors,
        value_vectors,
    )
    attended = local_call(
        outside_kernel,
        "outside",
        struct((tokens, heads * hw), BF16),
        work,
        doc_row,
        decay_sum,
        queries,
        carried,
        inside,
        head_gain.reshape(1, heads * hw),
    )

    products = []
    for k in range(nz):
        rows_k = attended
        if k:
            rows_k = permute_seq(
                attended, lambda q, k=k: (q // ny - k) % nz * ny + q % ny
            )
        products.append(jnp.dot(rows_k, w_z, preferred_element_type=F32).astype(BF16))
    products = jnp.stack(products)
    total = pick(products, (h - z) % nz).astype(F32)
    for m in range(1, n_head):
        sent = pick(products, (h + m - z) % nz)
        total = total + permute_head(sent, lambda q, m=m: (q + m) % n_head).astype(F32)
    spots = [
        ((zz * ny + yy) * n_head + hh, (hh * ny + yy) * n_head + zz)
        for zz in range(nz)
        for yy in range(ny)
        for hh in range(n_head)
    ]
    summed = lax.ppermute(total.astype(BF16), ("seq", "head"), spots).astype(F32)
    middle = lax.optimization_barrier((summed + residual.astype(F32)).astype(BF16))

    experts = n_seq
    capacity = 4 * tokens // experts
    flat_ids = routing.reshape(-1)
    hits = (flat_ids[:, None] == jnp.arange(experts, dtype=jnp.int32)[None, :]).astype(F32)
    pair_row = lax.broadcasted_iota(jnp.int32, (2 * tokens, 2 * tokens), 0)
    pair_col = lax.broadcasted_iota(jnp.int32, (2 * tokens, 2 * tokens), 1)
    earlier = jnp.dot((pair_col < pair_row).astype(F32), hits)
    rank = jnp.sum(earlier * hits, axis=1).astype(jnp.int32)
    place = (flat_ids * capacity + rank).reshape(tokens, 2)
    half = capacity // HALVES
    slot = jnp.arange(experts * half, dtype=jnp.int32)
    slot = slot // half * capacity + slot % half
    in_owner = [h] + [(h + m * CORES) % n_head for m in range(1, nx)]
    in_owner += [
        o // CORES * CORES + (o % CORES + m) % CORES for o in in_owner for m in range(1, CORES)
    ]
    out_owner = [
        (x + m) % nx * CORES + (c + k) % CORES for k in [*range(1, CORES), 0] for m in range(nx)
    ]
    owners = jnp.stack(in_owner + out_owner).astype(jnp.int32)

    mixed = middle.astype(F32)
    for q in range(HALVES):
        here = place[:, :, None] == (slot + q * half)[None, None, :]
        take = jnp.any(here, axis=1).astype(BF16)
        mix = jnp.sum(jnp.where(here, route_weights[:, :, None], 0.0), axis=1)

        outgoing = lax.dot_general(
            take, middle, (((0,), (0,)), ((), ())), preferred_element_type=F32
        ).astype(BF16)
        got = lax.all_to_all(
            outgoing.reshape(experts, half, part), "seq", split_axis=0, concat_axis=0, tiled=True
        ).reshape(experts * half, part)
        pieces = [got]
        for m in range(1, nx):
            pieces.append(permute_head(got, lambda q, m=m: (q - m * CORES) % n_head))
        for piece in list(pieces):
            for m in range(1, CORES):
                pieces.append(
                    permute_head(
                        piece, lambda q, m=m: q // CORES * CORES + (q % CORES - m) % CORES
                    )
                )
        sent, kept = expert_call(owners, pieces, norm_gain, gate_weight, up_weight, down_weight)

        near = permute_head(sent, lambda q: q // CORES * CORES + (q % CORES + 1) % CORES)
        near_sum = kept.astype(F32) + near.astype(F32)
        total = near_sum[0]
        for m in range(1, nx):
            total = total + permute_head(
                near_sum[m].astype(BF16), lambda q, m=m: (q + m * CORES) % n_head
            ).astype(F32)
        returned = lax.all_to_all(
            total.astype(BF16).reshape(experts, half, part),
            "seq",
            split_axis=0,
            concat_axis=0,
            tiled=True,
        ).reshape(experts * half, part)
        mixed = mixed + jnp.dot(
            mix, returned.astype(F32), precision=HIGHEST, preferred_element_type=F32
        )
    return mixed.astype(BF16)


def solution(mesh):
    placed = (
        P("seq", "head"),
        P("seq", "head"),
        P("seq", "head"),
        P("seq", "head"),
        P("seq"),
        P("head"),
        P("head", "seq"),
        P("seq", "head"),
        P(),
        P("seq", None),
        P("seq", None),
        P("seq", None, "head"),
        P("seq", None, "head"),
        P("seq", "head", None),
    )
    return jax.shard_map(
        shards, mesh=mesh, in_specs=placed, out_specs=P("seq", "head"), check_vma=False
    )
```

```python
import functools
import math

import jax
import jax.numpy as jnp
from jax import lax
from jax.experimental import pallas as pl
from jax.experimental.pallas import tpu as pltpu
from jax.sharding import PartitionSpec as P

EPSILON = 1e-06
CORES = 2
F32 = jnp.float32
BF16 = jnp.bfloat16
HIGHEST = lax.Precision.HIGHEST
SMALL_VMEM = 12 * 1024 * 1024
EXPERT_VMEM = 40 * 1024 * 1024


def permute_seq(value, move):
    count = lax.axis_size("seq")
    return lax.ppermute(value, "seq", [(source, move(source)) for source in range(count)])


def permute_head(value, move):
    count = lax.axis_size("head")
    return lax.ppermute(value, "head", [(source, move(source)) for source in range(count)])


def swap_seq(blocks):
    swapped = [blocks[0]]
    for d in range(1, len(blocks)):
        swapped.append(permute_seq(blocks[d], lambda q, d=d: q ^ d))
    return swapped


def pick(stack, index, axis=0):
    return lax.dynamic_index_in_dim(stack, index, axis, keepdims=False)


def doc_column(doc):
    count = doc.shape[1]
    return jnp.broadcast_to(doc, (count, count)).T


def chunk_plan(heads, hw, n_seq):
    rows = heads * hw // n_seq
    held = max(1, rows // hw)
    extra = -(-(2 * held + 2) // 16) * 16
    return rows, held, extra


def state_kernel(me_ref, doc_ref, decay_ref, k_ref, v_ref, *refs):
    outs, sum_ref, state_ref = refs[:-2], refs[-2], refs[-1]
    tokens, heads = decay_ref.shape
    n_seq, hw = len(outs), outs[0].shape[1]
    rows, held, extra = chunk_plan(heads, hw, n_seq)
    doc = doc_ref[...].astype(F32)
    row = lax.broadcasted_iota(jnp.int32, (tokens, tokens), 0)
    col = lax.broadcasted_iota(jnp.int32, (tokens, tokens), 1)
    sums = jnp.dot(
        (col <= row).astype(F32), decay_ref[...], precision=HIGHEST, preferred_element_type=F32
    )
    sum_ref[...] = sums
    final = sums[tokens - 1 :, :]
    last = doc[:, tokens - 1 :]
    tail = jnp.exp(final - sums) * (doc_column(doc)[:, :1] == last).astype(F32)
    gain = jnp.exp(final) * (doc[:, :1] == last).astype(F32)
    lane = lax.broadcasted_iota(jnp.int32, (1, heads), 1)
    line = lax.broadcasted_iota(jnp.int32, (extra, hw), 0)
    for d in reversed(range(n_seq)):
        chunk = me_ref[0] ^ d
        note = jnp.where(line == 2 * held, doc[:, :1], 0.0)
        note = jnp.where(line == 2 * held + 1, last, note)
        for j in range(held):
            i = chunk * rows // hw + j
            mine = (lane == i).astype(F32)
            lanes = pl.ds(pl.multiple_of(i * hw, 128), hw)
            fade = jnp.sum(tail * mine, axis=1, keepdims=True)
            faded = (k_ref[:, lanes].astype(F32) * fade).astype(BF16)
            state = lax.dot_general(
                faded, v_ref[:, lanes], (((0,), (0,)), ((), ())), preferred_element_type=F32
            )
            if rows >= hw:
                outs[d][j * hw : (j + 1) * hw, :] = state.astype(BF16)
            else:
                state_ref[...] = state
                start = pl.multiple_of(chunk % (hw // rows) * rows, rows)
                outs[d][:rows, :] = state_ref[pl.ds(start, rows), :].astype(BF16)
            whole = jnp.sum(gain * mine, axis=1, keepdims=True)
            high = whole.astype(BF16).astype(F32)
            note = jnp.where(line == j, high, note)
            note = jnp.where(line == held + j, whole - high, note)
        outs[d][rows:, :] = note.astype(BF16)


def scan_kernel(me_ref, *refs):
    n_seq = (len(refs) - 2) // 2
    ins, outs, blocks_ref, entered_ref = refs[:n_seq], refs[n_seq:-2], refs[-2], refs[-1]
    _, rows, hw = entered_ref.shape
    held = max(1, rows // hw)
    part = rows // held
    for d in range(n_seq):
        blocks_ref[me_ref[0] ^ d] = ins[d][...]
    for j in range(held):
        running = jnp.zeros((part, hw), F32)
        entered_ref[0, j * part : (j + 1) * part, :] = running.astype(BF16)
        for b in range(1, n_seq):
            notes = blocks_ref[b - 1, rows:, :].astype(F32)
            gain = notes[j : j + 1] + notes[held + j : held + j + 1]
            first = blocks_ref[b, rows:, :].astype(F32)[2 * held : 2 * held + 1]
            joined = (first == notes[2 * held + 1 : 2 * held + 2]).astype(F32)
            state = blocks_ref[b - 1, j * part : (j + 1) * part, :].astype(F32)
            running = (state + gain * running) * joined
            entered_ref[b, j * part : (j + 1) * part, :] = running.astype(BF16)
    for d in range(n_seq):
        outs[d][...] = entered_ref[me_ref[0] ^ d]


def inside_kernel(doc_ref, sum_ref, sum_rows_ref, q_ref, k_ref, v_ref, out_ref):
    tokens, heads = sum_ref.shape
    hw = q_ref.shape[1] // heads
    doc = doc_ref[...].astype(F32)
    row = lax.broadcasted_iota(jnp.int32, (tokens, tokens), 0)
    col = lax.broadcasted_iota(jnp.int32, (tokens, tokens), 1)
    kept = (col <= row) & (doc_column(doc) == doc)
    for i in range(heads):
        lanes = slice(i * hw, (i + 1) * hw)
        gap = sum_ref[:, i : i + 1] - sum_rows_ref[i : i + 1, :]
        fade = jnp.where(kept, jnp.exp(jnp.minimum(gap, 0.0)), 0.0)
        scores = lax.dot_general(
            q_ref[:, lanes], k_ref[:, lanes], (((1,), (1,)), ((), ())), preferred_element_type=F32
        )
        out_ref[:, lanes] = jnp.dot(
            (scores * fade).astype(BF16), v_ref[:, lanes], preferred_element_type=F32
        )


def outside_kernel(me_ref, doc_ref, sum_ref, q_ref, inside_ref, gain_ref, *refs):
    ins, out_ref, carried_ref = refs[:-2], refs[-2], refs[-1]
    tokens, heads = sum_ref.shape
    hw = q_ref.shape[1] // heads
    rows = ins[0].shape[0]
    for d in range(len(ins)):
        start = pl.multiple_of((me_ref[0] ^ d) * rows, rows)
        carried_ref[pl.ds(start, rows), :] = ins[d][...]
    doc = doc_ref[...].astype(F32)
    reach = jnp.exp(sum_ref[...]) * (doc_column(doc)[:, :1] == doc[:, :1]).astype(F32)
    for i in range(heads):
        lanes = slice(i * hw, (i + 1) * hw)
        outside = jnp.dot(q_ref[:, lanes], carried_ref[lanes, :], preferred_element_type=F32)
        raw = inside_ref[:, lanes] + outside * reach[:, i : i + 1]
        scale = lax.rsqrt(jnp.mean(raw * raw, axis=1, keepdims=True) + EPSILON)
        out_ref[:, lanes] = (raw * scale * gain_ref[:, lanes]).astype(BF16)


def dispatch_kernel(summed_ref, residual_ref, take_ref, middle_ref, *outs):
    middle = (summed_ref[...].astype(F32) + residual_ref[...].astype(F32)).astype(BF16)
    middle_ref[...] = middle
    count = outs[0].shape[0]
    rows = jnp.dot(take_ref[...], middle, preferred_element_type=F32).astype(BF16)
    for d in range(len(outs)):
        outs[d][...] = rows[d * count : (d + 1) * count]


def mix_kernel(middle_ref, mix_ref, *refs):
    ins, out_ref, rows_ref = refs[:-2], refs[-2], refs[-1]
    count = ins[0].shape[0]
    for d in range(len(ins)):
        rows_ref[d * count : (d + 1) * count, :] = ins[d][...]
    mix = mix_ref[...]
    high = mix.astype(BF16)
    low = (mix - high.astype(F32)).astype(BF16)
    rows = rows_ref[...]
    total = jnp.dot(high, rows, preferred_element_type=F32)
    total = total + jnp.dot(low, rows, preferred_element_type=F32)
    out_ref[...] = (middle_ref[...].astype(F32) + total).astype(BF16)


def expert_kernel(n_head, owner_ref, *refs):
    pieces = refs[:n_head]
    gain_ref, gate_ref, up_ref, down_ref, sent_ref, kept_ref, rows_ref, hidden_ref = refs[n_head:]
    part = pieces[0].shape[1]
    units, nx = hidden_ref.shape[1], sent_ref.shape[0]
    squares = 0.0
    for piece in pieces:
        value = piece[...].astype(F32)
        squares = squares + jnp.sum(value * value, axis=1, keepdims=True)
    scale = lax.rsqrt(squares / (part * n_head) + EPSILON)
    for i, piece in enumerate(pieces):
        lanes = pl.ds(pl.multiple_of(owner_ref[i] * part, 128), part)
        value = piece[...].astype(F32) * scale * gain_ref[:, lanes]
        rows_ref[:, lanes] = value.astype(BF16)

    def fill(lanes):
        gate = jnp.dot(rows_ref[...], gate_ref[0, :, lanes], preferred_element_type=F32)
        up = jnp.dot(rows_ref[...], up_ref[0, :, lanes], preferred_element_type=F32)
        hidden_ref[:, lanes] = (gate / (1.0 + jnp.exp(-gate)) * up).astype(BF16)

    width = 256
    steps = units // width

    @pl.loop(0, steps)
    def _(i):
        fill(pl.ds(pl.multiple_of(i * width, 128), width))

    if units % width:
        fill(slice(steps * width, units))

    for j, out_ref in enumerate((sent_ref, kept_ref)):

        @pl.loop(0, out_ref.shape[0])
        def _(i, j=j, out_ref=out_ref):
            start = owner_ref[n_head + j * nx + i] * part
            lanes = pl.ds(pl.multiple_of(start, 128), part)
            out_ref[i] = jnp.dot(
                hidden_ref[...], down_ref[0, :, lanes], preferred_element_type=F32
            ).astype(BF16)


def local_call(kernel, name, out_shape, flops, *operands, scratch=(), scalars=0, vmem=SMALL_VMEM):
    shapes = out_shape if isinstance(out_shape, list) else [out_shape]
    sizes = [math.prod(o.shape) * o.dtype.itemsize for o in [*operands, *shapes]]
    return pl.pallas_call(
        kernel,
        out_shape=out_shape,
        in_specs=[pl.BlockSpec(memory_space=pltpu.SMEM)] * scalars
        + [pl.BlockSpec(memory_space=pltpu.VMEM)] * (len(operands) - scalars),
        scratch_shapes=list(scratch),
        compiler_params=pltpu.CompilerParams(vmem_limit_bytes=vmem),
        cost_estimate=pl.CostEstimate(flops=flops, bytes_accessed=sum(sizes), transcendentals=0),
        name=name,
    )(*operands)


def shards(
    queries,
    key_vectors,
    value_vectors,
    log_decay,
    doc_ids,
    head_gain,
    output_weight,
    residual,
    norm_gain,
    routing,
    route_weights,
    gate_weight,
    up_weight,
    down_weight,
):
    tokens, heads = log_decay.shape
    hw = queries.shape[1] // heads
    n_seq, n_head = lax.axis_size("seq"), lax.axis_size("head")
    ny, nz, nx = n_seq // n_head, n_head, n_head // CORES
    s, h = lax.axis_index("seq"), lax.axis_index("head")
    z, y = s // ny, s % ny
    x, c = h // CORES, h % CORES
    part = residual.shape[1]
    model_width = part * n_head

    struct = jax.ShapeDtypeStruct
    me = s.astype(jnp.int32).reshape(1)
    doc_row = doc_ids.reshape(1, tokens)
    rows, held, extra = chunk_plan(heads, hw, n_seq)
    work = 2 * tokens * hw * hw * heads
    *payload, decay_sum = local_call(
        state_kernel,
        "block_state",
        [struct((rows + extra, hw), BF16)] * n_seq + [struct((tokens, heads), F32)],
        work,
        me,
        doc_row,
        log_decay,
        key_vectors,
        value_vectors,
        scratch=[pltpu.VMEM((hw, hw), F32)],
        scalars=1,
    )
    entered = local_call(
        scan_kernel,
        "carry",
        [struct((rows, hw), BF16)] * n_seq,
        work,
        me,
        *swap_seq(payload),
        scratch=[
            pltpu.VMEM((n_seq, rows + extra, hw), BF16),
            pltpu.VMEM((n_seq, rows, hw), BF16),
        ],
        scalars=1,
    )
    carried = swap_seq(entered)
    inside = local_call(
        inside_kernel,
        "inside",
        struct((tokens, heads * hw), F32),
        2 * work,
        doc_row,
        decay_sum,
        decay_sum.T,
        queries,
        key_vectors,
        value_vectors,
    )
    attended = local_call(
        outside_kernel,
        "outside",
        struct((tokens, heads * hw), BF16),
        work,
        me,
        doc_row,
        decay_sum,
        queries,
        inside,
        head_gain.reshape(1, heads * hw),
        *carried,
        scratch=[pltpu.VMEM((heads * hw, hw), BF16)],
        scalars=1,
    )
    attended, output_weight = lax.optimization_barrier((attended, output_weight))

    cols = output_weight.shape[1]
    w_z = jnp.zeros((output_weight.shape[0], ny * cols), BF16)
    w_z = lax.dynamic_update_slice(w_z, output_weight, (0, y * cols))
    for k in range(1, ny):
        got = permute_seq(output_weight, lambda q, k=k: q // ny * ny + (q % ny - k) % ny)
        w_z = lax.dynamic_update_slice(w_z, got, (0, (y + k) % ny * cols))

    products = []
    for k in range(nz):
        rows_k = attended
        if k:
            rows_k = permute_seq(
                attended, lambda q, k=k: (q // ny - k) % nz * ny + q % ny
            )
        products.append(jnp.dot(rows_k, w_z, preferred_element_type=F32).astype(BF16))
    products = jnp.stack(products)
    total = pick(products, (h - z) % nz).astype(F32)
    for m in range(1, n_head):
        sent = pick(products, (h + m - z) % nz)
        total = total + permute_head(sent, lambda q, m=m: (q + m) % n_head).astype(F32)
    spots = [
        ((zz * ny + yy) * n_head + hh, (hh * ny + yy) * n_head + zz)
        for zz in range(nz)
        for yy in range(ny)
        for hh in range(n_head)
    ]
    summed = lax.ppermute(total.astype(BF16), ("seq", "head"), spots)

    experts = n_seq
    capacity = 4 * tokens // experts
    flat_ids = routing.reshape(-1)
    hits = (flat_ids[:, None] == jnp.arange(experts, dtype=jnp.int32)[None, :]).astype(F32)
    pair_row = lax.broadcasted_iota(jnp.int32, (2 * tokens, 2 * tokens), 0)
    pair_col = lax.broadcasted_iota(jnp.int32, (2 * tokens, 2 * tokens), 1)
    earlier = jnp.dot((pair_col < pair_row).astype(F32), hits)
    rank = jnp.sum(earlier * hits, axis=1).astype(jnp.int32)
    place = (flat_ids * capacity + rank).reshape(tokens, 2)
    slot = jnp.arange(experts * capacity, dtype=jnp.int32)
    slot = (slot // capacity ^ s) * capacity + slot % capacity
    here = place[:, None, :] == slot[None, :, None]
    mix = jnp.sum(jnp.where(here, route_weights[:, None, :], 0.0), axis=2)
    take = jnp.any(here, axis=2).astype(BF16).T
    in_owner = [h] + [(h + m * CORES) % n_head for m in range(1, nx)]
    in_owner += [
        o // CORES * CORES + (o % CORES + m) % CORES for o in in_owner for m in range(1, CORES)
    ]
    out_owner = [
        (x + m) % nx * CORES + (c + k) % CORES for k in [*range(1, CORES), 0] for m in range(nx)
    ]
    owners = jnp.stack(in_owner + out_owner).astype(jnp.int32)

    middle, *outgoing = local_call(
        dispatch_kernel,
        "dispatch",
        [struct((tokens, part), BF16)] + [struct((capacity, part), BF16)] * experts,
        2 * tokens * tokens * 4 * part,
        summed,
        residual,
        take,
    )
    arrived = swap_seq(outgoing)
    depth, units = gate_weight.shape[1:]
    half = experts // 2
    count = half * capacity
    results = {}
    for group in (0, 1):
        got = jnp.concatenate(arrived[group * half : (group + 1) * half])
        pieces = [got]
        for m in range(1, nx):
            pieces.append(permute_head(got, lambda q, m=m: (q - m * CORES) % n_head))
        for piece in list(pieces):
            for m in range(1, CORES):
                pieces.append(
                    permute_head(
                        piece, lambda q, m=m: q // CORES * CORES + (q % CORES - m) % CORES
                    )
                )
        results[group] = local_call(
            functools.partial(expert_kernel, n_head),
            "expert",
            [struct((nx, count, part), BF16), struct((n_head - nx, count, part), BF16)],
            6 * count * depth * units,
            owners,
            *pieces,
            norm_gain.reshape(1, depth),
            gate_weight,
            up_weight,
            down_weight,
            scratch=[pltpu.VMEM((count, depth), BF16), pltpu.VMEM((count, units), BF16)],
            scalars=1,
            vmem=EXPERT_VMEM,
        )

    returning = [None] * experts
    for group in (1, 0):
        sent, kept = results[group]
        near = permute_head(sent, lambda q: q // CORES * CORES + (q % CORES + 1) % CORES)
        near_sum = kept.astype(F32) + near.astype(F32)
        total = near_sum[0]
        for m in range(1, nx):
            total = total + permute_head(
                near_sum[m].astype(BF16), lambda q, m=m: (q + m * CORES) % n_head
            ).astype(F32)
        total = total.astype(BF16)
        for k in range(half):
            returning[group * half + k] = total[k * capacity : (k + 1) * capacity]
    return local_call(
        mix_kernel,
        "mix",
        struct((tokens, part), BF16),
        4 * tokens * experts * capacity * part,
        middle,
        mix,
        *swap_seq(returning),
        scratch=[pltpu.VMEM((experts * capacity, part), BF16)],
    )


def solution(mesh):
    placed = (
        P("seq", "head"),
        P("seq", "head"),
        P("seq", "head"),
        P("seq", "head"),
        P("seq"),
        P("head"),
        P("head", "seq"),
        P("seq", "head"),
        P(),
        P("seq", None),
        P("seq", None),
        P("seq", None, "head"),
        P("seq", None, "head"),
        P("seq", "head", None),
    )
    return jax.shard_map(
        shards, mesh=mesh, in_specs=placed, out_specs=P("seq", "head"), check_vma=False
    )
```

```python
import functools
import math

import jax
import jax.numpy as jnp
from jax import lax
from jax.experimental import pallas as pl
from jax.experimental.pallas import tpu as pltpu
from jax.sharding import PartitionSpec as P

EPSILON = 1e-06
CORES = 2
F32 = jnp.float32
BF16 = jnp.bfloat16
HIGHEST = lax.Precision.HIGHEST
SMALL_VMEM = 12 * 1024 * 1024
EXPERT_VMEM = 40 * 1024 * 1024


def permute_seq(value, move):
    count = lax.axis_size("seq")
    return lax.ppermute(value, "seq", [(source, move(source)) for source in range(count)])


def permute_head(value, move):
    count = lax.axis_size("head")
    return lax.ppermute(value, "head", [(source, move(source)) for source in range(count)])


def swap_seq(blocks):
    swapped = [blocks[0]]
    for d in range(1, len(blocks)):
        swapped.append(permute_seq(blocks[d], lambda q, d=d: q ^ d))
    return swapped


def pick(stack, index, axis=0):
    return lax.dynamic_index_in_dim(stack, index, axis, keepdims=False)


def doc_column(doc):
    count = doc.shape[1]
    return jnp.broadcast_to(doc, (count, count)).T


def chunk_plan(heads, hw, n_seq):
    rows = heads * hw // n_seq
    held = max(1, rows // hw)
    extra = -(-(2 * held + 2) // 16) * 16
    return rows, held, extra


def state_kernel(me_ref, doc_ref, decay_ref, k_ref, v_ref, *refs):
    outs, sum_ref, state_ref = refs[:-2], refs[-2], refs[-1]
    tokens, heads = decay_ref.shape
    n_seq, hw = len(outs), outs[0].shape[1]
    rows, held, extra = chunk_plan(heads, hw, n_seq)
    doc = doc_ref[...].astype(F32)
    row = lax.broadcasted_iota(jnp.int32, (tokens, tokens), 0)
    col = lax.broadcasted_iota(jnp.int32, (tokens, tokens), 1)
    sums = jnp.dot(
        (col <= row).astype(F32), decay_ref[...], precision=HIGHEST, preferred_element_type=F32
    )
    sum_ref[...] = sums
    final = sums[tokens - 1 :, :]
    last = doc[:, tokens - 1 :]
    tail = jnp.exp(final - sums) * (doc_column(doc)[:, :1] == last).astype(F32)
    gain = jnp.exp(final) * (doc[:, :1] == last).astype(F32)
    lane = lax.broadcasted_iota(jnp.int32, (1, heads), 1)
    line = lax.broadcasted_iota(jnp.int32, (extra, hw), 0)
    for d in reversed(range(n_seq)):
        chunk = me_ref[0] ^ d
        note = jnp.where(line == 2 * held, doc[:, :1], 0.0)
        note = jnp.where(line == 2 * held + 1, last, note)
        for j in range(held):
            i = chunk * rows // hw + j
            mine = (lane == i).astype(F32)
            lanes = pl.ds(pl.multiple_of(i * hw, 128), hw)
            fade = jnp.sum(tail * mine, axis=1, keepdims=True)
            faded = (k_ref[:, lanes].astype(F32) * fade).astype(BF16)
            state = lax.dot_general(
                faded, v_ref[:, lanes], (((0,), (0,)), ((), ())), preferred_element_type=F32
            )
            if rows >= hw:
                outs[d][j * hw : (j + 1) * hw, :] = state.astype(BF16)
            else:
                state_ref[...] = state
                start = pl.multiple_of(chunk % (hw // rows) * rows, rows)
                outs[d][:rows, :] = state_ref[pl.ds(start, rows), :].astype(BF16)
            whole = jnp.sum(gain * mine, axis=1, keepdims=True)
            high = whole.astype(BF16).astype(F32)
            note = jnp.where(line == j, high, note)
            note = jnp.where(line == held + j, whole - high, note)
        outs[d][rows:, :] = note.astype(BF16)


def scan_kernel(me_ref, *refs):
    n_seq = (len(refs) - 2) // 2
    ins, outs, blocks_ref, entered_ref = refs[:n_seq], refs[n_seq:-2], refs[-2], refs[-1]
    _, rows, hw = entered_ref.shape
    held = max(1, rows // hw)
    part = rows // held
    for d in range(n_seq):
        blocks_ref[me_ref[0] ^ d] = ins[d][...]
    for j in range(held):
        running = jnp.zeros((part, hw), F32)
        entered_ref[0, j * part : (j + 1) * part, :] = running.astype(BF16)
        for b in range(1, n_seq):
            notes = blocks_ref[b - 1, rows:, :].astype(F32)
            gain = notes[j : j + 1] + notes[held + j : held + j + 1]
            first = blocks_ref[b, rows:, :].astype(F32)[2 * held : 2 * held + 1]
            joined = (first == notes[2 * held + 1 : 2 * held + 2]).astype(F32)
            state = blocks_ref[b - 1, j * part : (j + 1) * part, :].astype(F32)
            running = (state + gain * running) * joined
            entered_ref[b, j * part : (j + 1) * part, :] = running.astype(BF16)
    for d in range(n_seq):
        outs[d][...] = entered_ref[me_ref[0] ^ d]


def inside_kernel(doc_ref, sum_ref, sum_rows_ref, q_ref, k_ref, v_ref, out_ref):
    tokens, heads = sum_ref.shape
    hw = q_ref.shape[1] // heads
    doc = doc_ref[...].astype(F32)
    row = lax.broadcasted_iota(jnp.int32, (tokens, tokens), 0)
    col = lax.broadcasted_iota(jnp.int32, (tokens, tokens), 1)
    kept = (col <= row) & (doc_column(doc) == doc)
    for i in range(heads):
        lanes = slice(i * hw, (i + 1) * hw)
        gap = sum_ref[:, i : i + 1] - sum_rows_ref[i : i + 1, :]
        fade = jnp.where(kept, jnp.exp(jnp.minimum(gap, 0.0)), 0.0)
        scores = lax.dot_general(
            q_ref[:, lanes], k_ref[:, lanes], (((1,), (1,)), ((), ())), preferred_element_type=F32
        )
        out_ref[:, lanes] = jnp.dot(
            (scores * fade).astype(BF16), v_ref[:, lanes], preferred_element_type=F32
        )


def outside_kernel(me_ref, doc_ref, sum_ref, q_ref, inside_ref, gain_ref, *refs):
    ins, out_ref, carried_ref = refs[:-2], refs[-2], refs[-1]
    tokens, heads = sum_ref.shape
    hw = q_ref.shape[1] // heads
    rows = ins[0].shape[0]
    for d in range(len(ins)):
        start = pl.multiple_of((me_ref[0] ^ d) * rows, rows)
        carried_ref[pl.ds(start, rows), :] = ins[d][...]
    doc = doc_ref[...].astype(F32)
    reach = jnp.exp(sum_ref[...]) * (doc_column(doc)[:, :1] == doc[:, :1]).astype(F32)
    for i in range(heads):
        lanes = slice(i * hw, (i + 1) * hw)
        outside = jnp.dot(q_ref[:, lanes], carried_ref[lanes, :], preferred_element_type=F32)
        raw = inside_ref[:, lanes] + outside * reach[:, i : i + 1]
        scale = lax.rsqrt(jnp.mean(raw * raw, axis=1, keepdims=True) + EPSILON)
        out_ref[:, lanes] = (raw * scale * gain_ref[:, lanes]).astype(BF16)


def route_kernel(me_ref, *refs):
    ins, outs, stage_ref = refs[: (len(refs) - 1) // 2], refs[(len(refs) - 1) // 2 : -1], refs[-1]
    count = len(ins)
    for k in range(count):
        stage_ref[(me_ref[0] + k) % count] = ins[k][...]
    for m in range(count):
        outs[m][...] = stage_ref[(me_ref[1] + m) % count]


def dispatch_kernel(n_head, residual_ref, take_ref, *refs):
    total = residual_ref[...].astype(F32)
    sums = refs[0][...].astype(F32)
    for ref in refs[1:n_head]:
        sums = sums + ref[...].astype(F32)
    middle_ref, outs = refs[n_head], refs[n_head + 1 :]
    middle = (total + sums).astype(BF16)
    middle_ref[...] = middle
    count = outs[0].shape[0]
    rows = jnp.dot(take_ref[...], middle, preferred_element_type=F32).astype(BF16)
    for d in range(len(outs)):
        outs[d][...] = rows[d * count : (d + 1) * count]


def sum_kernel(nz, me_ref, *refs):
    ins, outs, stage_ref = refs[: len(refs) - 1 - nz], refs[len(refs) - 1 - nz : -1], refs[-1]
    total = ins[0][...].astype(F32)
    for ref in ins[1:]:
        total = total + ref[...].astype(F32)
    stage_ref[...] = total.astype(BF16)
    count = outs[0].shape[0]
    for k in range(nz):
        start = pl.multiple_of((me_ref[0] ^ k) * count, count)
        outs[k][...] = stage_ref[pl.ds(start, count), :]


def mix_kernel(middle_ref, mix_ref, *refs):
    ins, out_ref, rows_ref = refs[:-2], refs[-2], refs[-1]
    count = ins[0].shape[0]
    for d in range(len(ins)):
        rows_ref[d * count : (d + 1) * count, :] = ins[d][...]
    mix = mix_ref[...]
    high = mix.astype(BF16)
    low = (mix - high.astype(F32)).astype(BF16)
    rows = rows_ref[...]
    total = jnp.dot(high, rows, preferred_element_type=F32)
    total = total + jnp.dot(low, rows, preferred_element_type=F32)
    out_ref[...] = (middle_ref[...].astype(F32) + total).astype(BF16)


def expert_kernel(n_head, aligned, owner_ref, *refs):
    pieces = refs[:n_head]
    gain_ref, gate_ref, up_ref, down_ref, sent_ref, kept_ref = refs[n_head : n_head + 6]
    rows_ref, hidden_ref, wide_ref, low_ref, wide_sem, low_sem = refs[n_head + 6 :]
    _, depth, units = gate_ref.shape
    part = kept_ref.shape[2]
    nz, nx = depth // part, sent_ref.shape[0]
    count = pieces[0].shape[0] // nz
    steps = wide_ref.shape[0] // (1 if aligned else 2)
    width = units // steps

    def wide_copy(j, k):
        weight = (gate_ref, up_ref)[k]
        if aligned:
            source = weight.at[0, :, pl.ds(j * width, width)]
            target = wide_ref.at[j, :, pl.ds(k * width, width)]
        else:
            source, target = weight.at[0], wide_ref.at[k]
        return pltpu.make_async_copy(source, target, wide_sem.at[j, k])

    def low_copy(j):
        start = pl.multiple_of(owner_ref[n_head + j] * part, 128)
        return pltpu.make_async_copy(
            down_ref.at[0, :, pl.ds(start, part)], low_ref.at[j], low_sem.at[j]
        )

    for j in range(steps):
        for k in range(2):
            wide_copy(j, k).start()
    for j in range(n_head):
        low_copy(j).start()

    for i, piece in enumerate(pieces):
        squares = 0.0
        for k in range(nz):
            value = piece[k * count : (k + 1) * count, :].astype(F32)
            squares = squares + jnp.sum(value * value, axis=1, keepdims=True)
        scale = lax.rsqrt(squares / depth + EPSILON)
        lines = pl.ds(pl.multiple_of(owner_ref[i] * count, count), count)
        for k in range(nz):
            lanes = pl.ds(pl.multiple_of((owner_ref[2 * n_head] ^ k) * part, 128), part)
            value = piece[k * count : (k + 1) * count, :].astype(F32) * scale * gain_ref[:, lanes]
            rows_ref[lines, lanes] = value.astype(BF16)

    for j in range(steps):
        for k in range(2):
            wide_copy(j, k).wait()
        if aligned:
            both = jnp.dot(rows_ref[...], wide_ref[j], preferred_element_type=F32)
            gate, up = both[:, :width], both[:, width:]
        else:
            gate = jnp.dot(rows_ref[...], wide_ref[0], preferred_element_type=F32)
            up = jnp.dot(rows_ref[...], wide_ref[1], preferred_element_type=F32)
        hidden = (gate / (1.0 + jnp.exp(-gate)) * up).astype(BF16)
        hidden_ref[:, j * width : (j + 1) * width] = hidden

    for j in range(n_head):
        low_copy(j).wait()
        out = jnp.dot(hidden_ref[...], low_ref[j], preferred_element_type=F32).astype(BF16)
        if j < nx:
            sent_ref[j] = out
        else:
            kept_ref[j - nx] = out


def expert_call(owners, pieces, norm_gain, gate_weight, up_weight, down_weight):
    n_head = len(pieces)
    lines, part = pieces[0].shape
    _, depth, units = gate_weight.shape
    count = lines * part * n_head // depth
    width = next((w for w in (384, 256, 128) if units % w == 0), units)
    aligned = width % 128 == 0
    steps, nx = units // width, n_head // CORES
    wide = (steps, depth, 2 * width) if aligned else (2, depth, width)
    struct = jax.ShapeDtypeStruct
    return pl.pallas_call(
        functools.partial(expert_kernel, n_head, aligned),
        out_shape=[struct((nx, count, part), BF16), struct((n_head - nx, count, part), BF16)],
        in_specs=[pl.BlockSpec(memory_space=pltpu.SMEM)]
        + [pl.BlockSpec(memory_space=pltpu.VMEM)] * (n_head + 1)
        + [pl.BlockSpec(memory_space=pl.ANY)] * 3,
        scratch_shapes=[
            pltpu.VMEM((count, depth), BF16),
            pltpu.VMEM((count, units), BF16),
            pltpu.VMEM(wide, BF16),
            pltpu.VMEM((n_head, units, part), BF16),
            pltpu.SemaphoreType.DMA((steps, 2)),
            pltpu.SemaphoreType.DMA((n_head,)),
        ],
        compiler_params=pltpu.CompilerParams(vmem_limit_bytes=EXPERT_VMEM),
        cost_estimate=pl.CostEstimate(
            flops=6 * count * depth * units,
            bytes_accessed=6 * depth * units + 4 * count * depth,
            transcendentals=count * units,
        ),
        name="expert",
    )(owners, *pieces, norm_gain.reshape(1, depth), gate_weight, up_weight, down_weight)


def local_call(kernel, name, out_shape, flops, *operands, scratch=(), scalars=0, vmem=SMALL_VMEM):
    shapes = out_shape if isinstance(out_shape, list) else [out_shape]
    sizes = [math.prod(o.shape) * o.dtype.itemsize for o in [*operands, *shapes]]
    return pl.pallas_call(
        kernel,
        out_shape=out_shape,
        in_specs=[pl.BlockSpec(memory_space=pltpu.SMEM)] * scalars
        + [pl.BlockSpec(memory_space=pltpu.VMEM)] * (len(operands) - scalars),
        scratch_shapes=list(scratch),
        compiler_params=pltpu.CompilerParams(vmem_limit_bytes=vmem),
        cost_estimate=pl.CostEstimate(flops=flops, bytes_accessed=sum(sizes), transcendentals=0),
        name=name,
    )(*operands)


def slot_places(routing, experts, capacity):
    tokens = routing.shape[0]
    flat_ids = routing.reshape(-1)
    hits = (flat_ids[:, None] == jnp.arange(experts, dtype=jnp.int32)[None, :]).astype(F32)
    pair_row = lax.broadcasted_iota(jnp.int32, (2 * tokens, 2 * tokens), 0)
    pair_col = lax.broadcasted_iota(jnp.int32, (2 * tokens, 2 * tokens), 1)
    earlier = jnp.dot((pair_col < pair_row).astype(F32), hits)
    rank = jnp.sum(earlier * hits, axis=1).astype(jnp.int32)
    return (flat_ids * capacity + rank).reshape(tokens, 2)


def shards(
    queries,
    key_vectors,
    value_vectors,
    log_decay,
    doc_ids,
    head_gain,
    output_weight,
    residual,
    norm_gain,
    routing,
    route_weights,
    gate_weight,
    up_weight,
    down_weight,
):
    tokens, heads = log_decay.shape
    hw = queries.shape[1] // heads
    n_seq, n_head = lax.axis_size("seq"), lax.axis_size("head")
    ny, nz, nx = n_seq // n_head, n_head, n_head // CORES
    s, h = lax.axis_index("seq"), lax.axis_index("head")
    z, y = s // ny, s % ny
    x, c = h // CORES, h % CORES
    part = residual.shape[1]
    model_width = part * n_head

    struct = jax.ShapeDtypeStruct
    spots = [
        ((zz * ny + yy) * n_head + hh, (hh * ny + yy) * n_head + zz)
        for zz in range(nz)
        for yy in range(ny)
        for hh in range(n_head)
    ]
    crossed = lambda value: lax.ppermute(value, ("seq", "head"), spots)

    experts = n_seq
    capacity = 4 * tokens // experts
    residual_there, routing_there = crossed(residual), crossed(routing)
    slot = jnp.arange(experts * capacity, dtype=jnp.int32)
    slot = (slot // capacity ^ s) * capacity + slot % capacity
    place = slot_places(routing_there, experts, capacity)
    take = jnp.any(place[:, None, :] == slot[None, :, None], axis=2).astype(BF16).T
    place = slot_places(routing, experts, capacity)
    here = place[:, None, :] == slot[None, :, None]
    mix = jnp.sum(jnp.where(here, route_weights[:, None, :], 0.0), axis=2)

    me = s.astype(jnp.int32).reshape(1)
    doc_row = doc_ids.reshape(1, tokens)
    rows, held, extra = chunk_plan(heads, hw, n_seq)
    work = 2 * tokens * hw * hw * heads
    *payload, decay_sum = local_call(
        state_kernel,
        "block_state",
        [struct((rows + extra, hw), BF16)] * n_seq + [struct((tokens, heads), F32)],
        work,
        me,
        doc_row,
        log_decay,
        key_vectors,
        value_vectors,
        scratch=[pltpu.VMEM((hw, hw), F32)],
        scalars=1,
    )
    inside = local_call(
        inside_kernel,
        "inside",
        struct((tokens, heads * hw), F32),
        2 * work,
        doc_row,
        decay_sum,
        decay_sum.T,
        queries,
        key_vectors,
        value_vectors,
    )
    arrived, inside, residual_there, take = lax.optimization_barrier(
        (swap_seq(payload), inside, residual_there, take)
    )
    entered = local_call(
        scan_kernel,
        "carry",
        [struct((rows, hw), BF16)] * n_seq,
        work,
        me,
        *arrived,
        scratch=[
            pltpu.VMEM((n_seq, rows + extra, hw), BF16),
            pltpu.VMEM((n_seq, rows, hw), BF16),
        ],
        scalars=1,
    )
    carried = swap_seq(entered)
    attended = local_call(
        outside_kernel,
        "outside",
        struct((tokens, heads * hw), BF16),
        work,
        me,
        doc_row,
        decay_sum,
        queries,
        inside,
        head_gain.reshape(1, heads * hw),
        *carried,
        scratch=[pltpu.VMEM((heads * hw, hw), BF16)],
        scalars=1,
    )
    attended, output_weight = lax.optimization_barrier((attended, output_weight))

    cols = output_weight.shape[1]
    w_z = jnp.zeros((output_weight.shape[0], ny * cols), BF16)
    w_z = lax.dynamic_update_slice(w_z, output_weight, (0, y * cols))
    for k in range(1, ny):
        got = permute_seq(output_weight, lambda q, k=k: q // ny * ny + (q % ny - k) % ny)
        w_z = lax.dynamic_update_slice(w_z, got, (0, (y + k) % ny * cols))

    products = []
    for k in range(nz):
        rows_k = attended
        if k:
            rows_k = permute_seq(
                attended, lambda q, k=k: (q // ny - k) % nz * ny + q % ny
            )
        products.append(jnp.dot(rows_k, w_z, preferred_element_type=F32).astype(BF16))
    block = struct((tokens, part), BF16)
    place_me = jnp.stack([z, h]).astype(jnp.int32)
    own, *sent = local_call(
        route_kernel,
        "route",
        [block] * n_head,
        tokens * part,
        place_me,
        *products,
        scratch=[pltpu.VMEM((nz, tokens, part), BF16)],
        scalars=1,
    )
    sums = [own]
    for m in range(1, n_head):
        sums.append(permute_head(sent[m - 1], lambda q, m=m: (q + m) % n_head))
    middle_there, *outgoing = local_call(
        functools.partial(dispatch_kernel, n_head),
        "dispatch",
        [block] + [struct((capacity, part), BF16)] * experts,
        2 * tokens * tokens * 4 * part,
        residual_there,
        take,
        *sums,
    )

    arrived = swap_seq(outgoing)
    middle = crossed(middle_there)
    in_owner = [h] + [(h + m * CORES) % n_head for m in range(1, nx)]
    in_owner += [
        o // CORES * CORES + (o % CORES + m) % CORES for o in in_owner for m in range(1, CORES)
    ]
    out_owner = [
        (x + m) % nx * CORES + (c + k) % CORES for k in [*range(1, CORES), 0] for m in range(nx)
    ]
    owners = jnp.stack(in_owner + out_owner + [z]).astype(jnp.int32)
    count = n_head * capacity
    returning = [None] * experts
    for group in range(ny):
        got = jnp.concatenate([arrived[k * ny + group] for k in range(nz)])
        pieces = [got]
        for m in range(1, nx):
            pieces.append(permute_head(got, lambda q, m=m: (q - m * CORES) % n_head))
        for piece in list(pieces):
            for m in range(1, CORES):
                pieces.append(
                    permute_head(
                        piece, lambda q, m=m: q // CORES * CORES + (q % CORES - m) % CORES
                    )
                )
        sent, kept = expert_call(owners, pieces, norm_gain, gate_weight, up_weight, down_weight)

        near = permute_head(sent, lambda q: q // CORES * CORES + (q % CORES + 1) % CORES)
        near_sum = kept.astype(F32) + near.astype(F32)
        parts = [near_sum[0]]
        for m in range(1, nx):
            parts.append(
                permute_head(near_sum[m].astype(BF16), lambda q, m=m: (q + m * CORES) % n_head)
            )
        blocks = local_call(
            functools.partial(sum_kernel, nz),
            "total",
            [struct((capacity, part), BF16)] * nz,
            count * part * nx,
            z.astype(jnp.int32).reshape(1),
            *parts,
            scratch=[pltpu.VMEM((count, part), BF16)],
            scalars=1,
        )
        for k in range(nz):
            returning[k * ny + group] = blocks[k]
    return local_call(
        mix_kernel,
        "mix",
        block,
        4 * tokens * experts * capacity * part,
        middle,
        mix,
        *swap_seq(returning),
        scratch=[pltpu.VMEM((experts * capacity, part), BF16)],
    )


def solution(mesh):
    placed = (
        P("seq", "head"),
        P("seq", "head"),
        P("seq", "head"),
        P("seq", "head"),
        P("seq"),
        P("head"),
        P("head", "seq"),
        P("seq", "head"),
        P(),
        P("seq", None),
        P("seq", None),
        P("seq", None, "head"),
        P("seq", None, "head"),
        P("seq", "head", None),
    )
    return jax.shard_map(
        shards, mesh=mesh, in_specs=placed, out_specs=P("seq", "head"), check_vma=False
    )
```

```python
import functools
import math

import jax
import jax.numpy as jnp
from jax import lax
from jax.experimental import pallas as pl
from jax.experimental.pallas import tpu as pltpu
from jax.sharding import PartitionSpec as P

EPSILON = 1e-06
CORES = 2
F32 = jnp.float32
BF16 = jnp.bfloat16
HIGHEST = lax.Precision.HIGHEST
SMALL_VMEM = 12 * 1024 * 1024
EXPERT_VMEM = 40 * 1024 * 1024


def permute_seq(value, move):
    count = lax.axis_size("seq")
    return lax.ppermute(value, "seq", [(source, move(source)) for source in range(count)])


def permute_head(value, move):
    count = lax.axis_size("head")
    return lax.ppermute(value, "head", [(source, move(source)) for source in range(count)])


def swap_seq(blocks):
    swapped = [blocks[0]]
    for d in range(1, len(blocks)):
        swapped.append(permute_seq(blocks[d], lambda q, d=d: q ^ d))
    return swapped


def pick(stack, index, axis=0):
    return lax.dynamic_index_in_dim(stack, index, axis, keepdims=False)


def doc_column(doc):
    count = doc.shape[1]
    return jnp.broadcast_to(doc, (count, count)).T


def chunk_plan(heads, hw, n_seq):
    rows = heads * hw // n_seq
    held = max(1, rows // hw)
    extra = -(-(2 * held + 2) // 16) * 16
    return rows, held, extra


def state_kernel(me_ref, doc_ref, decay_ref, k_hbm, v_hbm, *refs):
    outs, (sum_ref, sum_rows_ref, doc_out_ref) = refs[:-7], refs[-7:-4]
    state_ref, k_ref, v_ref, sems = refs[-4:]
    fetches = [
        pltpu.make_async_copy(k_hbm, k_ref, sems.at[0]),
        pltpu.make_async_copy(v_hbm, v_ref, sems.at[1]),
    ]
    for fetch in fetches:
        fetch.start()
    heads, tokens = decay_ref.shape
    n_seq, hw = len(outs), outs[0].shape[1]
    rows, held, extra = chunk_plan(heads, hw, n_seq)
    doc = doc_ref[...].astype(F32)
    row = lax.broadcasted_iota(jnp.int32, (tokens, tokens), 0)
    col = lax.broadcasted_iota(jnp.int32, (tokens, tokens), 1)
    doc_out_ref[...] = doc
    sums = lax.dot_general(
        (col <= row).astype(F32),
        decay_ref[...],
        (((1,), (1,)), ((), ())),
        precision=HIGHEST,
        preferred_element_type=F32,
    )
    sum_ref[...] = sums
    sum_rows_ref[...] = jnp.dot(
        decay_ref[...], (row <= col).astype(F32), precision=HIGHEST, preferred_element_type=F32
    )
    final = sums[tokens - 1 :, :]
    last = doc[:, tokens - 1 :]
    tail = jnp.exp(final - sums) * (doc_column(doc)[:, :1] == last).astype(F32)
    gain = jnp.exp(final) * (doc[:, :1] == last).astype(F32)
    lane = lax.broadcasted_iota(jnp.int32, (1, heads), 1)
    line = lax.broadcasted_iota(jnp.int32, (extra, hw), 0)
    for fetch in fetches:
        fetch.wait()
    for d in reversed(range(n_seq)):
        chunk = me_ref[0] ^ d
        note = jnp.where(line == 2 * held, doc[:, :1], 0.0)
        note = jnp.where(line == 2 * held + 1, last, note)
        for j in range(held):
            i = chunk * rows // hw + j
            mine = (lane == i).astype(F32)
            lanes = pl.ds(pl.multiple_of(i * hw, 128), hw)
            fade = jnp.sum(tail * mine, axis=1, keepdims=True)
            faded = (k_ref[:, lanes].astype(F32) * fade).astype(BF16)
            state = lax.dot_general(
                faded, v_ref[:, lanes], (((0,), (0,)), ((), ())), preferred_element_type=F32
            )
            if rows >= hw:
                outs[d][j * hw : (j + 1) * hw, :] = state.astype(BF16)
            else:
                state_ref[...] = state
                start = pl.multiple_of(chunk % (hw // rows) * rows, rows)
                outs[d][:rows, :] = state_ref[pl.ds(start, rows), :].astype(BF16)
            whole = jnp.sum(gain * mine, axis=1, keepdims=True)
            high = whole.astype(BF16).astype(F32)
            note = jnp.where(line == j, high, note)
            note = jnp.where(line == held + j, whole - high, note)
        outs[d][rows:, :] = note.astype(BF16)


def scan_kernel(me_ref, *refs):
    n_seq = (len(refs) - 2) // 2
    ins, outs, blocks_ref, entered_ref = refs[:n_seq], refs[n_seq:-2], refs[-2], refs[-1]
    _, rows, hw = entered_ref.shape
    held = max(1, rows // hw)
    part = rows // held
    for d in range(n_seq):
        blocks_ref[me_ref[0] ^ d] = ins[d][...]
    for j in range(held):
        running = jnp.zeros((part, hw), F32)
        entered_ref[0, j * part : (j + 1) * part, :] = running.astype(BF16)
        for b in range(1, n_seq):
            notes = blocks_ref[b - 1, rows:, :].astype(F32)
            gain = notes[j : j + 1] + notes[held + j : held + j + 1]
            first = blocks_ref[b, rows:, :].astype(F32)[2 * held : 2 * held + 1]
            joined = (first == notes[2 * held + 1 : 2 * held + 2]).astype(F32)
            state = blocks_ref[b - 1, j * part : (j + 1) * part, :].astype(F32)
            running = (state + gain * running) * joined
            entered_ref[b, j * part : (j + 1) * part, :] = running.astype(BF16)
    for d in range(n_seq):
        outs[d][...] = entered_ref[me_ref[0] ^ d]


def inside_kernel(doc_ref, sum_ref, sum_rows_ref, q_hbm, k_hbm, v_hbm, out_ref, *scratch):
    q_ref, k_ref, v_ref, sems = scratch
    fetches = [
        pltpu.make_async_copy(source, target, sems.at[i])
        for i, (source, target) in enumerate(zip((q_hbm, k_hbm, v_hbm), scratch))
    ]
    for fetch in fetches:
        fetch.start()
    tokens, heads = sum_ref.shape
    hw = q_hbm.shape[1] // heads
    doc = doc_ref[...]
    row = lax.broadcasted_iota(jnp.int32, (tokens, tokens), 0)
    col = lax.broadcasted_iota(jnp.int32, (tokens, tokens), 1)
    kept = (col <= row) & (doc_column(doc) == doc)
    for fetch in fetches:
        fetch.wait()
    for i in range(heads):
        lanes = slice(i * hw, (i + 1) * hw)
        gap = sum_ref[:, i : i + 1] - sum_rows_ref[i : i + 1, :]
        fade = jnp.where(kept, jnp.exp(jnp.minimum(gap, 0.0)), 0.0)
        scores = lax.dot_general(
            q_ref[:, lanes], k_ref[:, lanes], (((1,), (1,)), ((), ())), preferred_element_type=F32
        )
        out_ref[:, lanes] = jnp.dot(
            (scores * fade).astype(BF16), v_ref[:, lanes], preferred_element_type=F32
        )


def outside_kernel(me_ref, doc_ref, sum_ref, q_ref, inside_ref, gain_ref, *refs):
    ins, out_ref, carried_ref = refs[:-2], refs[-2], refs[-1]
    tokens, heads = sum_ref.shape
    hw = q_ref.shape[1] // heads
    rows = ins[0].shape[0]
    for d in range(len(ins)):
        start = pl.multiple_of((me_ref[0] ^ d) * rows, rows)
        carried_ref[pl.ds(start, rows), :] = ins[d][...]
    doc = doc_ref[...]
    reach = jnp.exp(sum_ref[...]) * (doc_column(doc)[:, :1] == doc[:, :1]).astype(F32)
    for i in range(heads):
        lanes = slice(i * hw, (i + 1) * hw)
        outside = jnp.dot(q_ref[:, lanes], carried_ref[lanes, :], preferred_element_type=F32)
        raw = inside_ref[:, lanes] + outside * reach[:, i : i + 1]
        scale = lax.rsqrt(jnp.mean(raw * raw, axis=1, keepdims=True) + EPSILON)
        out_ref[:, lanes] = (raw * scale * gain_ref[:, lanes]).astype(BF16)


def pack_kernel(*refs):
    ins, out_ref = refs[:-1], refs[-1]
    count = ins[0].shape[0]
    for k in range(len(ins)):
        out_ref[k * count : (k + 1) * count, :] = ins[k][...]


def route_kernel(me_ref, *refs):
    ins, outs, stage_ref = refs[: (len(refs) - 1) // 2], refs[(len(refs) - 1) // 2 : -1], refs[-1]
    count = len(ins)
    for k in range(count):
        stage_ref[(me_ref[0] + k) % count] = ins[k][...]
    for m in range(count):
        outs[m][...] = stage_ref[(me_ref[1] + m) % count]


def dispatch_kernel(n_head, residual_ref, take_ref, *refs):
    total = residual_ref[...].astype(F32)
    sums = refs[0][...].astype(F32)
    for ref in refs[1:n_head]:
        sums = sums + ref[...].astype(F32)
    middle_ref, outs = refs[n_head], refs[n_head + 1 :]
    middle = (total + sums).astype(BF16)
    middle_ref[...] = middle
    count = outs[0].shape[0]
    rows = jnp.dot(take_ref[...], middle, preferred_element_type=F32).astype(BF16)
    for d in range(len(outs)):
        outs[d][...] = rows[d * count : (d + 1) * count]


def sum_kernel(nz, me_ref, *refs):
    ins, outs, stage_ref = refs[: len(refs) - 1 - nz], refs[len(refs) - 1 - nz : -1], refs[-1]
    total = ins[0][...].astype(F32)
    for ref in ins[1:]:
        total = total + ref[...].astype(F32)
    stage_ref[...] = total.astype(BF16)
    count = outs[0].shape[0]
    for k in range(nz):
        start = pl.multiple_of((me_ref[0] ^ k) * count, count)
        outs[k][...] = stage_ref[pl.ds(start, count), :]


def mix_kernel(middle_ref, mix_ref, *refs):
    ins, out_ref, rows_ref = refs[:-2], refs[-2], refs[-1]
    count = ins[0].shape[0]
    for d in range(len(ins)):
        rows_ref[d * count : (d + 1) * count, :] = ins[d][...]
    mix = mix_ref[...]
    high = mix.astype(BF16)
    low = (mix - high.astype(F32)).astype(BF16)
    rows = rows_ref[...]
    total = jnp.dot(high, rows, preferred_element_type=F32)
    total = total + jnp.dot(low, rows, preferred_element_type=F32)
    out_ref[...] = (middle_ref[...].astype(F32) + total).astype(BF16)


def expert_kernel(n_head, aligned, owner_ref, *refs):
    pieces = refs[:n_head]
    gain_ref, gate_ref, up_ref, down_ref, sent_ref, kept_ref = refs[n_head : n_head + 6]
    rows_ref, hidden_ref, wide_ref, low_ref, wide_sem, low_sem = refs[n_head + 6 :]
    _, depth, units = gate_ref.shape
    part = kept_ref.shape[2]
    nz, nx = depth // part, sent_ref.shape[0]
    count = pieces[0].shape[0] // nz
    steps = wide_ref.shape[0] // (1 if aligned else 2)
    width = units // steps

    def wide_copy(j, k):
        weight = (gate_ref, up_ref)[k]
        if aligned:
            source = weight.at[0, :, pl.ds(j * width, width)]
            target = wide_ref.at[j, :, pl.ds(k * width, width)]
        else:
            source, target = weight.at[0], wide_ref.at[k]
        return pltpu.make_async_copy(source, target, wide_sem.at[j, k])

    def low_copy(j):
        start = pl.multiple_of(owner_ref[n_head + j] * part, 128)
        return pltpu.make_async_copy(
            down_ref.at[0, :, pl.ds(start, part)], low_ref.at[j], low_sem.at[j]
        )

    for j in range(steps):
        for k in range(2):
            wide_copy(j, k).start()
    for j in range(n_head):
        low_copy(j).start()

    for i, piece in enumerate(pieces):
        squares = 0.0
        for k in range(nz):
            value = piece[k * count : (k + 1) * count, :].astype(F32)
            squares = squares + jnp.sum(value * value, axis=1, keepdims=True)
        scale = lax.rsqrt(squares / depth + EPSILON)
        lines = pl.ds(pl.multiple_of(owner_ref[i] * count, count), count)
        for k in range(nz):
            lanes = pl.ds(pl.multiple_of((owner_ref[2 * n_head] ^ k) * part, 128), part)
            value = piece[k * count : (k + 1) * count, :].astype(F32) * scale * gain_ref[:, lanes]
            rows_ref[lines, lanes] = value.astype(BF16)

    for j in range(steps):
        for k in range(2):
            wide_copy(j, k).wait()
        if aligned:
            both = jnp.dot(rows_ref[...], wide_ref[j], preferred_element_type=F32)
            gate, up = both[:, :width], both[:, width:]
        else:
            gate = jnp.dot(rows_ref[...], wide_ref[0], preferred_element_type=F32)
            up = jnp.dot(rows_ref[...], wide_ref[1], preferred_element_type=F32)
        hidden = (gate / (1.0 + jnp.exp(-gate)) * up).astype(BF16)
        hidden_ref[:, j * width : (j + 1) * width] = hidden

    for j in range(n_head):
        low_copy(j).wait()
        out = jnp.dot(hidden_ref[...], low_ref[j], preferred_element_type=F32).astype(BF16)
        if j < nx:
            sent_ref[j] = out
        else:
            kept_ref[j - nx] = out


def expert_call(owners, pieces, norm_gain, gate_weight, up_weight, down_weight):
    n_head = len(pieces)
    lines, part = pieces[0].shape
    _, depth, units = gate_weight.shape
    count = lines * part * n_head // depth
    width = next((w for w in (384, 256, 128) if units % w == 0), units)
    aligned = width % 128 == 0
    steps, nx = units // width, n_head // CORES
    wide = (steps, depth, 2 * width) if aligned else (2, depth, width)
    struct = jax.ShapeDtypeStruct
    return pl.pallas_call(
        functools.partial(expert_kernel, n_head, aligned),
        out_shape=[struct((nx, count, part), BF16), struct((n_head - nx, count, part), BF16)],
        in_specs=[pl.BlockSpec(memory_space=pltpu.SMEM)]
        + [pl.BlockSpec(memory_space=pltpu.VMEM)] * (n_head + 1)
        + [pl.BlockSpec(memory_space=pltpu.HBM)] * 3,
        scratch_shapes=[
            pltpu.VMEM((count, depth), BF16),
            pltpu.VMEM((count, units), BF16),
            pltpu.VMEM(wide, BF16),
            pltpu.VMEM((n_head, units, part), BF16),
            pltpu.SemaphoreType.DMA((steps, 2)),
            pltpu.SemaphoreType.DMA((n_head,)),
        ],
        compiler_params=pltpu.CompilerParams(vmem_limit_bytes=EXPERT_VMEM),
        cost_estimate=pl.CostEstimate(
            flops=6 * count * depth * units,
            bytes_accessed=6 * depth * units + 4 * count * depth,
            transcendentals=count * units,
        ),
        name="expert",
    )(owners, *pieces, norm_gain.reshape(1, depth), gate_weight, up_weight, down_weight)


def local_call(
    kernel, name, out_shape, flops, *operands, scratch=(), scalars=0, far=0, vmem=SMALL_VMEM
):
    shapes = out_shape if isinstance(out_shape, list) else [out_shape]
    sizes = [math.prod(o.shape) * o.dtype.itemsize for o in [*operands, *shapes]]
    return pl.pallas_call(
        kernel,
        out_shape=out_shape,
        in_specs=[pl.BlockSpec(memory_space=pltpu.SMEM)] * scalars
        + [pl.BlockSpec(memory_space=pltpu.VMEM)] * (len(operands) - scalars - far)
        + [pl.BlockSpec(memory_space=pltpu.HBM)] * far,
        scratch_shapes=list(scratch),
        compiler_params=pltpu.CompilerParams(vmem_limit_bytes=vmem),
        cost_estimate=pl.CostEstimate(flops=flops, bytes_accessed=sum(sizes), transcendentals=0),
        name=name,
    )(*operands)


def slot_places(routing, experts, capacity):
    tokens = routing.shape[0]
    flat_ids = routing.reshape(-1)
    hits = (flat_ids[:, None] == jnp.arange(experts, dtype=jnp.int32)[None, :]).astype(F32)
    pair_row = lax.broadcasted_iota(jnp.int32, (2 * tokens, 2 * tokens), 0)
    pair_col = lax.broadcasted_iota(jnp.int32, (2 * tokens, 2 * tokens), 1)
    earlier = jnp.dot((pair_col < pair_row).astype(F32), hits)
    rank = jnp.sum(earlier * hits, axis=1).astype(jnp.int32)
    return (flat_ids * capacity + rank).reshape(tokens, 2)


def shards(
    queries,
    key_vectors,
    value_vectors,
    log_decay,
    doc_ids,
    head_gain,
    output_weight,
    residual,
    norm_gain,
    routing,
    route_weights,
    gate_weight,
    up_weight,
    down_weight,
):
    tokens, heads = log_decay.shape
    hw = queries.shape[1] // heads
    n_seq, n_head = lax.axis_size("seq"), lax.axis_size("head")
    ny, nz, nx = n_seq // n_head, n_head, n_head // CORES
    s, h = lax.axis_index("seq"), lax.axis_index("head")
    z, y = s // ny, s % ny
    x, c = h // CORES, h % CORES
    part = residual.shape[1]
    model_width = part * n_head

    struct = jax.ShapeDtypeStruct
    spots = [
        ((zz * ny + yy) * n_head + hh, (hh * ny + yy) * n_head + zz)
        for zz in range(nz)
        for yy in range(ny)
        for hh in range(n_head)
    ]
    crossed = lambda value: lax.ppermute(value, ("seq", "head"), spots)

    experts = n_seq
    capacity = 4 * tokens // experts
    me = s.astype(jnp.int32).reshape(1)
    doc_row = doc_ids.reshape(1, tokens)
    rows, held, extra = chunk_plan(heads, hw, n_seq)
    work = 2 * tokens * hw * hw * heads
    whole = pltpu.VMEM((tokens, heads * hw), BF16)
    *payload, decay_sum, decay_rows, doc_float = local_call(
        state_kernel,
        "block_state",
        [struct((rows + extra, hw), BF16)] * n_seq
        + [struct((tokens, heads), F32), struct((heads, tokens), F32), struct((1, tokens), F32)],
        work,
        me,
        doc_row,
        log_decay.T,
        key_vectors,
        value_vectors,
        scratch=[pltpu.VMEM((hw, hw), F32), whole, whole, pltpu.SemaphoreType.DMA((2,))],
        scalars=1,
        far=2,
    )
    entered = local_call(
        scan_kernel,
        "carry",
        [struct((rows, hw), BF16)] * n_seq,
        work,
        me,
        *swap_seq(payload),
        scratch=[
            pltpu.VMEM((n_seq, rows + extra, hw), BF16),
            pltpu.VMEM((n_seq, rows, hw), BF16),
        ],
        scalars=1,
    )
    carried = swap_seq(entered)
    inside = local_call(
        inside_kernel,
        "inside",
        struct((tokens, heads * hw), F32),
        2 * work,
        doc_float,
        decay_sum,
        decay_rows,
        queries,
        key_vectors,
        value_vectors,
        scratch=[whole, whole, whole, pltpu.SemaphoreType.DMA((3,))],
        far=3,
    )
    attended = local_call(
        outside_kernel,
        "outside",
        struct((tokens, heads * hw), BF16),
        work,
        me,
        doc_float,
        decay_sum,
        queries,
        inside,
        head_gain.reshape(1, heads * hw),
        *carried,
        scratch=[pltpu.VMEM((heads * hw, hw), BF16)],
        scalars=1,
    )

    lanes = max(128, routing.shape[1])
    ids = jnp.pad(routing.astype(BF16), ((0, 0), (0, lanes - routing.shape[1])))
    there = jnp.concatenate([residual, ids], axis=1)
    attended, output_weight, there = lax.optimization_barrier((attended, output_weight, there))
    there = crossed(there)
    residual_there = there[:, :part]
    routing_there = there[:, part : part + routing.shape[1]].astype(jnp.int32)
    slot = jnp.arange(experts * capacity, dtype=jnp.int32)
    slot = (slot // capacity ^ s) * capacity + slot % capacity
    place = slot_places(routing_there, experts, capacity)
    take = jnp.any(place[:, None, :] == slot[None, :, None], axis=2).astype(BF16).T
    place = slot_places(routing, experts, capacity)
    here = place[:, None, :] == slot[None, :, None]
    mix = jnp.sum(jnp.where(here, route_weights[:, None, :], 0.0), axis=2)

    cols = output_weight.shape[1]
    w_z = jnp.zeros((output_weight.shape[0], ny * cols), BF16)
    w_z = lax.dynamic_update_slice(w_z, output_weight, (0, y * cols))
    for k in range(1, ny):
        got = permute_seq(output_weight, lambda q, k=k: q // ny * ny + (q % ny - k) % ny)
        w_z = lax.dynamic_update_slice(w_z, got, (0, (y + k) % ny * cols))

    products = []
    for k in range(nz):
        rows_k = attended
        if k:
            rows_k = permute_seq(
                attended, lambda q, k=k: (q // ny - k) % nz * ny + q % ny
            )
        products.append(jnp.dot(rows_k, w_z, preferred_element_type=F32).astype(BF16))
    products, take, mix = lax.optimization_barrier((products, take, mix))
    block = struct((tokens, part), BF16)
    place_me = jnp.stack([z, h]).astype(jnp.int32)
    own, *sent = local_call(
        route_kernel,
        "route",
        [block] * n_head,
        tokens * part,
        place_me,
        *products,
        scratch=[pltpu.VMEM((nz, tokens, part), BF16)],
        scalars=1,
    )
    sums = [own]
    for m in range(1, n_head):
        sums.append(permute_head(sent[m - 1], lambda q, m=m: (q + m) % n_head))
    middle_there, *outgoing = local_call(
        functools.partial(dispatch_kernel, n_head),
        "dispatch",
        [block] + [struct((capacity, part), BF16)] * experts,
        2 * tokens * tokens * 4 * part,
        residual_there,
        take,
        *sums,
    )

    in_owner = [h] + [(h + m * CORES) % n_head for m in range(1, nx)]
    in_owner += [
        o // CORES * CORES + (o % CORES + m) % CORES for o in in_owner for m in range(1, CORES)
    ]
    out_owner = [
        (x + m) % nx * CORES + (c + k) % CORES for k in [*range(1, CORES), 0] for m in range(nx)
    ]
    owners = jnp.stack(in_owner + out_owner + [z]).astype(jnp.int32)
    count = n_head * capacity
    returning = [None] * experts
    arrived, sent, crossing = None, None, None
    for group in range(ny):
        sends = [outgoing[k * ny + group] for k in range(nz)]
        if group:
            sends = lax.optimization_barrier((sends, arrived))[0]
        arrived = [
            permute_seq(sends[k], lambda q, d=k * ny + group: q ^ d) if k + group else sends[k]
            for k in range(nz)
        ]
        got = local_call(
            pack_kernel, "pack", struct((nz * capacity, part), BF16), count * part, *arrived
        )
        far = [permute_head(got, lambda q, m=m: (q - m * CORES) % n_head) for m in range(1, nx)]
        if group:
            far = lax.optimization_barrier((far, sent))[0]
        pieces = [got, *far]
        for piece in [got, *far]:
            for m in range(1, CORES):
                pieces.append(
                    permute_head(
                        piece, lambda q, m=m: q // CORES * CORES + (q % CORES - m) % CORES
                    )
                )
        if group:
            pieces = lax.optimization_barrier((pieces, crossing))[0]
        sent, kept = expert_call(owners, pieces, norm_gain, gate_weight, up_weight, down_weight)
        if group == 0:
            middle = crossed(lax.optimization_barrier((middle_there, sent))[0])

        near = permute_head(sent, lambda q: q // CORES * CORES + (q % CORES + 1) % CORES)
        near_sum = kept.astype(F32) + near.astype(F32)
        crossing = [near_sum[m].astype(BF16) for m in range(1, nx)]
        parts = [near_sum[0]]
        for m in range(1, nx):
            parts.append(permute_head(crossing[m - 1], lambda q, m=m: (q + m * CORES) % n_head))
        blocks = local_call(
            functools.partial(sum_kernel, nz),
            "total",
            [struct((capacity, part), BF16)] * nz,
            count * part * nx,
            z.astype(jnp.int32).reshape(1),
            *parts,
            scratch=[pltpu.VMEM((count, part), BF16)],
            scalars=1,
        )
        if group == ny - 1:
            blocks, middle = lax.optimization_barrier((blocks, middle))
        for k in range(nz):
            returning[k * ny + group] = blocks[k]
    return local_call(
        mix_kernel,
        "mix",
        block,
        4 * tokens * experts * capacity * part,
        middle,
        mix,
        *swap_seq(returning),
        scratch=[pltpu.VMEM((experts * capacity, part), BF16)],
    )


def solution(mesh):
    placed = (
        P("seq", "head"),
        P("seq", "head"),
        P("seq", "head"),
        P("seq", "head"),
        P("seq"),
        P("head"),
        P("head", "seq"),
        P("seq", "head"),
        P(),
        P("seq", None),
        P("seq", None),
        P("seq", None, "head"),
        P("seq", None, "head"),
        P("seq", "head", None),
    )
    return jax.shard_map(
        shards, mesh=mesh, in_specs=placed, out_specs=P("seq", "head"), check_vma=False
    )
```

```python
import functools
import math

import jax
import jax.numpy as jnp
from jax import lax
from jax.experimental import pallas as pl
from jax.experimental.pallas import tpu as pltpu
from jax.sharding import PartitionSpec as P

EPSILON = 1e-06
CORES = 2
F32 = jnp.float32
BF16 = jnp.bfloat16
HIGHEST = lax.Precision.HIGHEST
SMALL_VMEM = 12 * 1024 * 1024
EXPERT_VMEM = 40 * 1024 * 1024


def permute_seq(value, move):
    count = lax.axis_size("seq")
    return lax.ppermute(value, "seq", [(source, move(source)) for source in range(count)])


def permute_head(value, move):
    count = lax.axis_size("head")
    return lax.ppermute(value, "head", [(source, move(source)) for source in range(count)])


def swap_seq(blocks):
    swapped = [blocks[0]]
    for d in range(1, len(blocks)):
        swapped.append(permute_seq(blocks[d], lambda q, d=d: q ^ d))
    return swapped


def pick(stack, index, axis=0):
    return lax.dynamic_index_in_dim(stack, index, axis, keepdims=False)


def doc_column(doc):
    count = doc.shape[1]
    return jnp.broadcast_to(doc, (count, count)).T


def chunk_plan(heads, hw, n_seq):
    rows = heads * hw // n_seq
    held = max(1, rows // hw)
    extra = -(-(2 * held + 2) // 16) * 16
    return rows, held, extra


def state_kernel(me_ref, doc_ref, decay_ref, k_hbm, v_hbm, *refs):
    outs, (sum_ref, sum_rows_ref, doc_out_ref) = refs[:-7], refs[-7:-4]
    state_ref, k_ref, v_ref, sems = refs[-4:]
    fetches = [
        pltpu.make_async_copy(k_hbm, k_ref, sems.at[0]),
        pltpu.make_async_copy(v_hbm, v_ref, sems.at[1]),
    ]
    for fetch in fetches:
        fetch.start()
    heads, tokens = decay_ref.shape
    n_seq, hw = len(outs), outs[0].shape[1]
    rows, held, extra = chunk_plan(heads, hw, n_seq)
    doc = doc_ref[...].astype(F32)
    row = lax.broadcasted_iota(jnp.int32, (tokens, tokens), 0)
    col = lax.broadcasted_iota(jnp.int32, (tokens, tokens), 1)
    doc_out_ref[...] = doc
    sums = lax.dot_general(
        (col <= row).astype(F32),
        decay_ref[...],
        (((1,), (1,)), ((), ())),
        precision=HIGHEST,
        preferred_element_type=F32,
    )
    sum_ref[...] = sums
    sum_rows_ref[...] = jnp.dot(
        decay_ref[...], (row <= col).astype(F32), precision=HIGHEST, preferred_element_type=F32
    )
    final = sums[tokens - 1 :, :]
    last = doc[:, tokens - 1 :]
    tail = jnp.exp(final - sums) * (doc_column(doc)[:, :1] == last).astype(F32)
    gain = jnp.exp(final) * (doc[:, :1] == last).astype(F32)
    lane = lax.broadcasted_iota(jnp.int32, (1, heads), 1)
    line = lax.broadcasted_iota(jnp.int32, (extra, hw), 0)
    for fetch in fetches:
        fetch.wait()
    for d in reversed(range(n_seq)):
        chunk = me_ref[0] ^ d
        note = jnp.where(line == 2 * held, doc[:, :1], 0.0)
        note = jnp.where(line == 2 * held + 1, last, note)
        for j in range(held):
            i = chunk * rows // hw + j
            mine = (lane == i).astype(F32)
            lanes = pl.ds(pl.multiple_of(i * hw, 128), hw)
            fade = jnp.sum(tail * mine, axis=1, keepdims=True)
            faded = (k_ref[:, lanes].astype(F32) * fade).astype(BF16)
            state = lax.dot_general(
                faded, v_ref[:, lanes], (((0,), (0,)), ((), ())), preferred_element_type=F32
            )
            if rows >= hw:
                outs[d][j * hw : (j + 1) * hw, :] = state.astype(BF16)
            else:
                state_ref[...] = state
                start = pl.multiple_of(chunk % (hw // rows) * rows, rows)
                outs[d][:rows, :] = state_ref[pl.ds(start, rows), :].astype(BF16)
            whole = jnp.sum(gain * mine, axis=1, keepdims=True)
            high = whole.astype(BF16).astype(F32)
            note = jnp.where(line == j, high, note)
            note = jnp.where(line == held + j, whole - high, note)
        outs[d][rows:, :] = note.astype(BF16)


def scan_kernel(me_ref, *refs):
    n_seq = (len(refs) - 2) // 2
    ins, outs, blocks_ref, entered_ref = refs[:n_seq], refs[n_seq:-2], refs[-2], refs[-1]
    _, rows, hw = entered_ref.shape
    held = max(1, rows // hw)
    part = rows // held
    for d in range(n_seq):
        blocks_ref[me_ref[0] ^ d] = ins[d][...]
    for j in range(held):
        running = jnp.zeros((part, hw), F32)
        entered_ref[0, j * part : (j + 1) * part, :] = running.astype(BF16)
        for b in range(1, n_seq):
            notes = blocks_ref[b - 1, rows:, :].astype(F32)
            gain = notes[j : j + 1] + notes[held + j : held + j + 1]
            first = blocks_ref[b, rows:, :].astype(F32)[2 * held : 2 * held + 1]
            joined = (first == notes[2 * held + 1 : 2 * held + 2]).astype(F32)
            state = blocks_ref[b - 1, j * part : (j + 1) * part, :].astype(F32)
            running = (state + gain * running) * joined
            entered_ref[b, j * part : (j + 1) * part, :] = running.astype(BF16)
    for d in range(n_seq):
        outs[d][...] = entered_ref[me_ref[0] ^ d]


def inside_kernel(doc_ref, sum_ref, sum_rows_ref, q_hbm, k_hbm, v_hbm, out_ref, *scratch):
    q_ref, k_ref, v_ref, sems = scratch
    fetches = [
        pltpu.make_async_copy(source, target, sems.at[i])
        for i, (source, target) in enumerate(zip((q_hbm, k_hbm, v_hbm), scratch))
    ]
    for fetch in fetches:
        fetch.start()
    tokens, heads = sum_ref.shape
    hw = q_hbm.shape[1] // heads
    doc = doc_ref[...]
    row = lax.broadcasted_iota(jnp.int32, (tokens, tokens), 0)
    col = lax.broadcasted_iota(jnp.int32, (tokens, tokens), 1)
    kept = (col <= row) & (doc_column(doc) == doc)
    for fetch in fetches:
        fetch.wait()
    for i in range(heads):
        lanes = slice(i * hw, (i + 1) * hw)
        gap = sum_ref[:, i : i + 1] - sum_rows_ref[i : i + 1, :]
        fade = jnp.where(kept, jnp.exp(jnp.minimum(gap, 0.0)), 0.0)
        scores = lax.dot_general(
            q_ref[:, lanes], k_ref[:, lanes], (((1,), (1,)), ((), ())), preferred_element_type=F32
        )
        out_ref[:, lanes] = jnp.dot(
            (scores * fade).astype(BF16), v_ref[:, lanes], preferred_element_type=F32
        )


def outside_kernel(me_ref, doc_ref, sum_ref, q_ref, inside_ref, gain_ref, *refs):
    ins, out_ref, carried_ref = refs[:-2], refs[-2], refs[-1]
    tokens, heads = sum_ref.shape
    hw = q_ref.shape[1] // heads
    rows = ins[0].shape[0]
    for d in range(len(ins)):
        start = pl.multiple_of((me_ref[0] ^ d) * rows, rows)
        carried_ref[pl.ds(start, rows), :] = ins[d][...]
    doc = doc_ref[...]
    reach = jnp.exp(sum_ref[...]) * (doc_column(doc)[:, :1] == doc[:, :1]).astype(F32)
    for i in range(heads):
        lanes = slice(i * hw, (i + 1) * hw)
        outside = jnp.dot(q_ref[:, lanes], carried_ref[lanes, :], preferred_element_type=F32)
        raw = inside_ref[:, lanes] + outside * reach[:, i : i + 1]
        scale = lax.rsqrt(jnp.mean(raw * raw, axis=1, keepdims=True) + EPSILON)
        out_ref[:, lanes] = (raw * scale * gain_ref[:, lanes]).astype(BF16)


def pack_kernel(*refs):
    ins, out_ref = refs[:-1], refs[-1]
    count = ins[0].shape[0]
    for k in range(len(ins)):
        out_ref[k * count : (k + 1) * count, :] = ins[k][...]


def route_kernel(shifts, me_ref, *refs):
    ins, outs, stage_ref = refs[: len(shifts)], refs[len(shifts) : -1], refs[-1]
    count, me = len(outs), me_ref[0]
    for (up, down), ref in zip(shifts, ins):
        if not up and not down:
            stage_ref[me] = ref[...]
        if up:

            @pl.when(me >= up)
            def _(up=up, ref=ref):
                stage_ref[me - up] = ref[...]

        if down:

            @pl.when(me < count - down)
            def _(down=down, ref=ref):
                stage_ref[me + down] = ref[...]

    for m in range(count):
        outs[m][...] = stage_ref[(me_ref[1] + m) % count]


def dispatch_kernel(n_head, residual_ref, take_ref, *refs):
    total = residual_ref[...].astype(F32)
    sums = refs[0][...].astype(F32)
    for ref in refs[1:n_head]:
        sums = sums + ref[...].astype(F32)
    middle_ref, outs = refs[n_head], refs[n_head + 1 :]
    middle = (total + sums).astype(BF16)
    middle_ref[...] = middle
    count = outs[0].shape[0]
    rows = jnp.dot(take_ref[...], middle, preferred_element_type=F32).astype(BF16)
    for d in range(len(outs)):
        outs[d][...] = rows[d * count : (d + 1) * count]


def sum_kernel(nz, me_ref, *refs):
    ins, outs, stage_ref = refs[: len(refs) - 1 - nz], refs[len(refs) - 1 - nz : -1], refs[-1]
    total = ins[0][...].astype(F32)
    for ref in ins[1:]:
        total = total + ref[...].astype(F32)
    stage_ref[...] = total.astype(BF16)
    count = outs[0].shape[0]
    for k in range(nz):
        start = pl.multiple_of((me_ref[0] ^ k) * count, count)
        outs[k][...] = stage_ref[pl.ds(start, count), :]


def mix_kernel(middle_ref, mix_ref, *refs):
    ins, out_ref, rows_ref = refs[:-2], refs[-2], refs[-1]
    count = ins[0].shape[0]
    for d in range(len(ins)):
        rows_ref[d * count : (d + 1) * count, :] = ins[d][...]
    mix = mix_ref[...]
    high = mix.astype(BF16)
    low = (mix - high.astype(F32)).astype(BF16)
    rows = rows_ref[...]
    total = jnp.dot(high, rows, preferred_element_type=F32)
    total = total + jnp.dot(low, rows, preferred_element_type=F32)
    out_ref[...] = (middle_ref[...].astype(F32) + total).astype(BF16)


def wide_copies(gate_ref, up_ref, wide_ref, sems, steps, aligned):
    width = gate_ref.shape[2] // steps
    copies = []
    for j in range(steps):
        for k, weight in enumerate((gate_ref, up_ref)):
            source, target = weight.at[0], wide_ref.at[k]
            if aligned:
                source = weight.at[0, :, pl.ds(j * width, width)]
                target = wide_ref.at[j, :, pl.ds(k * width, width)]
            copies.append(pltpu.make_async_copy(source, target, sems.at[j, k]))
    return copies


def low_copies(n_head, owner_ref, down_ref, low_ref, sems):
    part = low_ref.shape[2]
    copies = []
    for j in range(n_head):
        start = pl.multiple_of(owner_ref[n_head + j] * part, 128)
        source = down_ref.at[0, :, pl.ds(start, part)]
        copies.append(pltpu.make_async_copy(source, low_ref.at[j], sems.at[j]))
    return copies


def fill_hidden(n_head, aligned, owner_ref, pieces, gain_ref, rows_ref, wide_ref, hidden_ref, copies):
    depth, units = gain_ref.shape[1], hidden_ref.shape[1]
    part = pieces[0].shape[1]
    nz = depth // part
    count = pieces[0].shape[0] // nz
    steps = len(copies) // 2
    width = units // steps
    for i, piece in enumerate(pieces):
        squares = 0.0
        for k in range(nz):
            value = piece[k * count : (k + 1) * count, :].astype(F32)
            squares = squares + jnp.sum(value * value, axis=1, keepdims=True)
        scale = lax.rsqrt(squares / depth + EPSILON)
        lines = pl.ds(pl.multiple_of(owner_ref[i] * count, count), count)
        for k in range(nz):
            lanes = pl.ds(pl.multiple_of((owner_ref[2 * n_head] ^ k) * part, 128), part)
            value = piece[k * count : (k + 1) * count, :].astype(F32) * scale * gain_ref[:, lanes]
            rows_ref[lines, lanes] = value.astype(BF16)
    for j in range(steps):
        copies[2 * j].wait()
        copies[2 * j + 1].wait()
        if aligned:
            both = jnp.dot(rows_ref[...], wide_ref[j], preferred_element_type=F32)
            gate, up = both[:, :width], both[:, width:]
        else:
            gate = jnp.dot(rows_ref[...], wide_ref[0], preferred_element_type=F32)
            up = jnp.dot(rows_ref[...], wide_ref[1], preferred_element_type=F32)
        hidden = (gate / (1.0 + jnp.exp(-gate)) * up).astype(BF16)
        hidden_ref[:, j * width : (j + 1) * width] = hidden


def write_out(hidden_ref, low_ref, sent_ref, kept_ref, copies):
    nx = sent_ref.shape[0]
    for j, copy in enumerate(copies):
        copy.wait()
        out = jnp.dot(hidden_ref[...], low_ref[j], preferred_element_type=F32).astype(BF16)
        if j < nx:
            sent_ref[j] = out
        else:
            kept_ref[j - nx] = out


def expert_kernel(n_head, steps, aligned, owner_ref, *refs):
    pieces, gain_ref = refs[:n_head], refs[n_head]
    gate_ref, up_ref, down_ref, sent_ref, kept_ref = refs[n_head + 1 : n_head + 6]
    rows_ref, hidden_ref, wide_ref, low_ref, wide_sem, low_sem = refs[n_head + 6 :]
    wide = wide_copies(gate_ref, up_ref, wide_ref, wide_sem, steps, aligned)
    low = low_copies(n_head, owner_ref, down_ref, low_ref, low_sem)
    for copy in wide + low:
        copy.start()
    fill_hidden(n_head, aligned, owner_ref, pieces, gain_ref, rows_ref, wide_ref, hidden_ref, wide)
    write_out(hidden_ref, low_ref, sent_ref, kept_ref, low)


def hidden_kernel(n_head, steps, aligned, owner_ref, *refs):
    pieces, gain_ref = refs[:n_head], refs[n_head]
    gate_ref, up_ref, hidden_ref, rows_ref, wide_ref, wide_sem = refs[n_head + 1 :]
    wide = wide_copies(gate_ref, up_ref, wide_ref, wide_sem, steps, aligned)
    for copy in wide:
        copy.start()
    fill_hidden(n_head, aligned, owner_ref, pieces, gain_ref, rows_ref, wide_ref, hidden_ref, wide)


def down_kernel(n_head, owner_ref, hidden_ref, down_ref, sent_ref, kept_ref, low_ref, low_sem):
    low = low_copies(n_head, owner_ref, down_ref, low_ref, low_sem)
    for copy in low:
        copy.start()
    write_out(hidden_ref, low_ref, sent_ref, kept_ref, low)


def expert_call(owners, pieces, norm_gain, gate_weight, up_weight, down_weight, before_down=None):
    n_head = len(pieces)
    lines, part = pieces[0].shape
    _, depth, units = gate_weight.shape
    count = lines * part * n_head // depth
    width = next((w for w in (384, 256, 128) if units % w == 0), units)
    aligned = width % 128 == 0
    steps, nx = units // width, n_head // CORES
    struct = jax.ShapeDtypeStruct
    rows = pltpu.VMEM((count, depth), BF16)
    wide = pltpu.VMEM((steps, depth, 2 * width) if aligned else (2, depth, width), BF16)
    low = pltpu.VMEM((n_head, units, part), BF16)
    wide_sem, low_sem = pltpu.SemaphoreType.DMA((steps, 2)), pltpu.SemaphoreType.DMA((n_head,))
    outs = [struct((nx, count, part), BF16), struct((n_head - nx, count, part), BF16)]
    hidden = struct((count, units), BF16)
    work = 2 * count * depth * units
    gain = norm_gain.reshape(1, depth)
    if before_down is None:
        return local_call(
            functools.partial(expert_kernel, n_head, steps, aligned),
            "expert",
            outs,
            3 * work,
            owners,
            *pieces,
            gain,
            gate_weight,
            up_weight,
            down_weight,
            scratch=[rows, pltpu.VMEM(hidden.shape, BF16), wide, low, wide_sem, low_sem],
            scalars=1,
            far=3,
            vmem=EXPERT_VMEM,
        )
    hidden = local_call(
        functools.partial(hidden_kernel, n_head, steps, aligned),
        "hidden",
        hidden,
        2 * work,
        owners,
        *pieces,
        gain,
        gate_weight,
        up_weight,
        scratch=[rows, wide, wide_sem],
        scalars=1,
        far=2,
        vmem=EXPERT_VMEM,
    )
    hidden = lax.optimization_barrier((hidden, before_down))[0]
    return local_call(
        functools.partial(down_kernel, n_head),
        "down",
        outs,
        work,
        owners,
        hidden,
        down_weight,
        scratch=[low, low_sem],
        scalars=1,
        far=1,
        vmem=EXPERT_VMEM,
    )


def local_call(
    kernel, name, out_shape, flops, *operands, scratch=(), scalars=0, far=0, vmem=SMALL_VMEM
):
    shapes = out_shape if isinstance(out_shape, list) else [out_shape]
    sizes = [math.prod(o.shape) * o.dtype.itemsize for o in [*operands, *shapes]]
    return pl.pallas_call(
        kernel,
        out_shape=out_shape,
        in_specs=[pl.BlockSpec(memory_space=pltpu.SMEM)] * scalars
        + [pl.BlockSpec(memory_space=pltpu.VMEM)] * (len(operands) - scalars - far)
        + [pl.BlockSpec(memory_space=pltpu.HBM)] * far,
        scratch_shapes=list(scratch),
        compiler_params=pltpu.CompilerParams(vmem_limit_bytes=vmem),
        cost_estimate=pl.CostEstimate(flops=flops, bytes_accessed=sum(sizes), transcendentals=0),
        name=name,
    )(*operands)


def slot_places(routing, experts, capacity):
    tokens = routing.shape[0]
    flat_ids = routing.reshape(-1)
    hits = (flat_ids[:, None] == jnp.arange(experts, dtype=jnp.int32)[None, :]).astype(F32)
    pair_row = lax.broadcasted_iota(jnp.int32, (2 * tokens, 2 * tokens), 0)
    pair_col = lax.broadcasted_iota(jnp.int32, (2 * tokens, 2 * tokens), 1)
    earlier = jnp.dot((pair_col < pair_row).astype(F32), hits)
    rank = jnp.sum(earlier * hits, axis=1).astype(jnp.int32)
    return (flat_ids * capacity + rank).reshape(tokens, 2)


def shards(
    queries,
    key_vectors,
    value_vectors,
    log_decay,
    doc_ids,
    head_gain,
    output_weight,
    residual,
    norm_gain,
    routing,
    route_weights,
    gate_weight,
    up_weight,
    down_weight,
):
    tokens, heads = log_decay.shape
    hw = queries.shape[1] // heads
    n_seq, n_head = lax.axis_size("seq"), lax.axis_size("head")
    ny, nz, nx = n_seq // n_head, n_head, n_head // CORES
    s, h = lax.axis_index("seq"), lax.axis_index("head")
    z, y = s // ny, s % ny
    x, c = h // CORES, h % CORES
    part = residual.shape[1]
    model_width = part * n_head

    struct = jax.ShapeDtypeStruct
    spots = [
        ((zz * ny + yy) * n_head + hh, (hh * ny + yy) * n_head + zz)
        for zz in range(nz)
        for yy in range(ny)
        for hh in range(n_head)
    ]
    crossed = lambda value: lax.ppermute(value, ("seq", "head"), spots)

    experts = n_seq
    capacity = 4 * tokens // experts
    me = s.astype(jnp.int32).reshape(1)
    doc_row = doc_ids.reshape(1, tokens)
    rows, held, extra = chunk_plan(heads, hw, n_seq)
    work = 2 * tokens * hw * hw * heads
    whole = pltpu.VMEM((tokens, heads * hw), BF16)
    *payload, decay_sum, decay_rows, doc_float = local_call(
        state_kernel,
        "block_state",
        [struct((rows + extra, hw), BF16)] * n_seq
        + [struct((tokens, heads), F32), struct((heads, tokens), F32), struct((1, tokens), F32)],
        work,
        me,
        doc_row,
        log_decay.T,
        key_vectors,
        value_vectors,
        scratch=[pltpu.VMEM((hw, hw), F32), whole, whole, pltpu.SemaphoreType.DMA((2,))],
        scalars=1,
        far=2,
    )
    lanes = max(128, routing.shape[1])
    ids = jnp.pad(routing.astype(BF16), ((0, 0), (0, lanes - routing.shape[1])))
    there = crossed(jnp.concatenate([residual, ids], axis=1))
    arrived, there = lax.optimization_barrier((swap_seq(payload), there))
    entered = local_call(
        scan_kernel,
        "carry",
        [struct((rows, hw), BF16)] * n_seq,
        work,
        me,
        *arrived,
        scratch=[
            pltpu.VMEM((n_seq, rows + extra, hw), BF16),
            pltpu.VMEM((n_seq, rows, hw), BF16),
        ],
        scalars=1,
    )
    carried = swap_seq(entered)
    inside = local_call(
        inside_kernel,
        "inside",
        struct((tokens, heads * hw), F32),
        2 * work,
        doc_float,
        decay_sum,
        decay_rows,
        queries,
        key_vectors,
        value_vectors,
        scratch=[whole, whole, whole, pltpu.SemaphoreType.DMA((3,))],
        far=3,
    )
    attended = local_call(
        outside_kernel,
        "outside",
        struct((tokens, heads * hw), BF16),
        work,
        me,
        doc_float,
        decay_sum,
        queries,
        inside,
        head_gain.reshape(1, heads * hw),
        *carried,
        scratch=[pltpu.VMEM((heads * hw, hw), BF16)],
        scalars=1,
    )

    attended, output_weight = lax.optimization_barrier((attended, output_weight))
    residual_there = there[:, :part]
    routing_there = there[:, part : part + routing.shape[1]].astype(jnp.int32)
    slot = jnp.arange(experts * capacity, dtype=jnp.int32)
    slot = (slot // capacity ^ s) * capacity + slot % capacity
    place = slot_places(routing_there, experts, capacity)
    take = jnp.any(place[:, None, :] == slot[None, :, None], axis=2).astype(BF16).T
    place = slot_places(routing, experts, capacity)
    here = place[:, None, :] == slot[None, :, None]
    mix = jnp.sum(jnp.where(here, route_weights[:, None, :], 0.0), axis=2)

    cols = output_weight.shape[1]
    w_z = jnp.zeros((output_weight.shape[0], ny * cols), BF16)
    w_z = lax.dynamic_update_slice(w_z, output_weight, (0, y * cols))
    for k in range(1, ny):
        got = permute_seq(output_weight, lambda q, k=k: q // ny * ny + (q % ny - k) % ny)
        w_z = lax.dynamic_update_slice(w_z, got, (0, (y + k) % ny * cols))

    def along(value, pairs):
        perm = [(a * ny + yy, b * ny + yy) for a, b in pairs for yy in range(ny)]
        return lax.ppermute(value, "seq", perm)

    ups = lambda j: [(q, q + j) for q in range(nz - j)]
    downs = lambda j: [(q + j, q) for q in range(nz - j)]
    below, above = along(attended, ups(1)), along(attended, downs(1))
    direct = lax.optimization_barrier((attended, below, above))[0]
    shifts, rows_of = [(0, 0), (1, 0), (0, 1)], [attended, below, above]
    if nz > 2:
        shifts += [(2, 0), (0, 2)]
        rows_of += [along(below, ups(1)), along(above, downs(1))]
    for j in range(3, nz):
        if 2 * j >= nz:
            shifts.append((j, j))
            rows_of.append(along(direct, ups(j) + downs(j)))
        else:
            shifts += [(j, 0), (0, j)]
            rows_of += [along(direct, ups(j)), along(direct, downs(j))]
    products = [jnp.dot(r, w_z, preferred_element_type=F32).astype(BF16) for r in rows_of]
    products, take, mix = lax.optimization_barrier((products, take, mix))
    block = struct((tokens, part), BF16)
    place_me = jnp.stack([z, h]).astype(jnp.int32)
    own, *sent = local_call(
        functools.partial(route_kernel, shifts),
        "route",
        [block] * n_head,
        tokens * part,
        place_me,
        *products,
        scratch=[pltpu.VMEM((nz, tokens, part), BF16)],
        scalars=1,
    )
    sums = [own]
    for m in range(1, n_head):
        sums.append(permute_head(sent[m - 1], lambda q, m=m: (q + m) % n_head))
    middle_there, *outgoing = local_call(
        functools.partial(dispatch_kernel, n_head),
        "dispatch",
        [block] + [struct((capacity, part), BF16)] * experts,
        2 * tokens * tokens * 4 * part,
        residual_there,
        take,
        *sums,
    )

    in_owner = [h] + [(h + m * CORES) % n_head for m in range(1, nx)]
    in_owner += [
        o // CORES * CORES + (o % CORES + m) % CORES for o in in_owner for m in range(1, CORES)
    ]
    out_owner = [
        (x + m) % nx * CORES + (c + k) % CORES for k in [*range(1, CORES), 0] for m in range(nx)
    ]
    owners = jnp.stack(in_owner + out_owner + [z]).astype(jnp.int32)
    count = n_head * capacity
    returning = [None] * experts
    arrived = None
    gots, fars = [], []
    for group in range(ny):
        sends = [outgoing[k * ny + group] for k in range(nz)]
        if group:
            sends = lax.optimization_barrier((sends, arrived))[0]
        arrived = [
            permute_seq(sends[k], lambda q, d=k * ny + group: q ^ d) if k + group else sends[k]
            for k in range(nz)
        ]
        got = local_call(
            pack_kernel, "pack", struct((nz * capacity, part), BF16), count * part, *arrived
        )
        gots.append(got)
        fars.append(
            [permute_head(got, lambda q, m=m: (q - m * CORES) % n_head) for m in range(1, nx)]
        )
    for group in range(ny):
        got, far = gots[group], fars[group]
        if group:
            far = lax.optimization_barrier((far, sent))[0]
        if group + 1 < ny:
            far = lax.optimization_barrier((far, gots[group + 1]))[0]
        pieces = [got, *far]
        for piece in [got, *far]:
            for m in range(1, CORES):
                pieces.append(
                    permute_head(
                        piece, lambda q, m=m: q // CORES * CORES + (q % CORES - m) % CORES
                    )
                )
        if group:
            pieces = lax.optimization_barrier((pieces, crossing))[0]
        first = [blocks, middle] if group else None
        if group + 1 < ny:
            first = (first, fars[group + 1])
        sent, kept = expert_call(
            owners, pieces, norm_gain, gate_weight, up_weight, down_weight, first
        )
        if group == 0:
            middle = crossed(lax.optimization_barrier((middle_there, sent))[0])

        near = permute_head(sent, lambda q: q // CORES * CORES + (q % CORES + 1) % CORES)
        near_sum = kept.astype(F32) + near.astype(F32)
        crossing = [near_sum[m].astype(BF16) for m in range(1, nx)]
        parts = [near_sum[0]]
        for m in range(1, nx):
            parts.append(permute_head(crossing[m - 1], lambda q, m=m: (q + m * CORES) % n_head))
        blocks = local_call(
            functools.partial(sum_kernel, nz),
            "total",
            [struct((capacity, part), BF16)] * nz,
            count * part * nx,
            z.astype(jnp.int32).reshape(1),
            *parts,
            scratch=[pltpu.VMEM((count, part), BF16)],
            scalars=1,
        )
        for k in range(nz):
            returning[k * ny + group] = blocks[k]
    return local_call(
        mix_kernel,
        "mix",
        block,
        4 * tokens * experts * capacity * part,
        middle,
        mix,
        *swap_seq(returning),
        scratch=[pltpu.VMEM((experts * capacity, part), BF16)],
    )


def solution(mesh):
    placed = (
        P("seq", "head"),
        P("seq", "head"),
        P("seq", "head"),
        P("seq", "head"),
        P("seq"),
        P("head"),
        P("head", "seq"),
        P("seq", "head"),
        P(),
        P("seq", None),
        P("seq", None),
        P("seq", None, "head"),
        P("seq", None, "head"),
        P("seq", "head", None),
    )
    return jax.shard_map(
        shards, mesh=mesh, in_specs=placed, out_specs=P("seq", "head"), check_vma=False
    )
```

```python
import functools
import math

import jax
import jax.numpy as jnp
from jax import lax
from jax.experimental import pallas as pl
from jax.experimental.pallas import tpu as pltpu
from jax.sharding import PartitionSpec as P

EPSILON = 1e-06
CORES = 2
F32 = jnp.float32
BF16 = jnp.bfloat16
HIGHEST = lax.Precision.HIGHEST
SMALL_VMEM = 12 * 1024 * 1024
EXPERT_VMEM = 48 * 1024 * 1024


def permute_seq(value, move):
    count = lax.axis_size("seq")
    return lax.ppermute(value, "seq", [(source, move(source)) for source in range(count)])


def permute_head(value, move):
    count = lax.axis_size("head")
    return lax.ppermute(value, "head", [(source, move(source)) for source in range(count)])


def swap_seq(blocks):
    swapped = [blocks[0]]
    for d in range(1, len(blocks)):
        swapped.append(permute_seq(blocks[d], lambda q, d=d: q ^ d))
    return swapped


def pick(stack, index, axis=0):
    return lax.dynamic_index_in_dim(stack, index, axis, keepdims=False)


def doc_column(doc):
    count = doc.shape[1]
    return jnp.broadcast_to(doc, (count, count)).T


def chunk_plan(heads, hw, n_seq):
    rows = heads * hw // n_seq
    held = max(1, rows // hw)
    extra = -(-(2 * held + 2) // 16) * 16
    return rows, held, extra


def state_kernel(me_ref, doc_ref, decay_ref, k_ref, v_ref, *refs):
    outs, (sum_ref, sum_rows_ref, doc_out_ref, state_ref) = refs[:-4], refs[-4:]
    heads, tokens = decay_ref.shape
    n_seq, hw = len(outs), outs[0].shape[1]
    rows, held, extra = chunk_plan(heads, hw, n_seq)
    doc = doc_ref[...].astype(F32)
    row = lax.broadcasted_iota(jnp.int32, (tokens, tokens), 0)
    col = lax.broadcasted_iota(jnp.int32, (tokens, tokens), 1)
    doc_out_ref[...] = doc
    sums = lax.dot_general(
        (col <= row).astype(F32),
        decay_ref[...],
        (((1,), (1,)), ((), ())),
        precision=HIGHEST,
        preferred_element_type=F32,
    )
    sum_ref[...] = sums
    sum_rows_ref[...] = jnp.dot(
        decay_ref[...], (row <= col).astype(F32), precision=HIGHEST, preferred_element_type=F32
    )
    final = sums[tokens - 1 :, :]
    last = doc[:, tokens - 1 :]
    tail = jnp.exp(final - sums) * (doc_column(doc)[:, :1] == last).astype(F32)
    gain = jnp.exp(final) * (doc[:, :1] == last).astype(F32)
    lane = lax.broadcasted_iota(jnp.int32, (1, heads), 1)
    line = lax.broadcasted_iota(jnp.int32, (extra, hw), 0)
    for d in reversed(range(n_seq)):
        chunk = me_ref[0] ^ d
        note = jnp.where(line == 2 * held, doc[:, :1], 0.0)
        note = jnp.where(line == 2 * held + 1, last, note)
        for j in range(held):
            i = chunk * rows // hw + j
            mine = (lane == i).astype(F32)
            lanes = pl.ds(pl.multiple_of(i * hw, 128), hw)
            fade = jnp.sum(tail * mine, axis=1, keepdims=True)
            faded = (k_ref[:, lanes].astype(F32) * fade).astype(BF16)
            state = lax.dot_general(
                faded, v_ref[:, lanes], (((0,), (0,)), ((), ())), preferred_element_type=F32
            )
            if rows >= hw:
                outs[d][j * hw : (j + 1) * hw, :] = state.astype(BF16)
            else:
                state_ref[...] = state
                start = pl.multiple_of(chunk % (hw // rows) * rows, rows)
                outs[d][:rows, :] = state_ref[pl.ds(start, rows), :].astype(BF16)
            whole = jnp.sum(gain * mine, axis=1, keepdims=True)
            high = whole.astype(BF16).astype(F32)
            note = jnp.where(line == j, high, note)
            note = jnp.where(line == held + j, whole - high, note)
        outs[d][rows:, :] = note.astype(BF16)


def scan_kernel(me_ref, *refs):
    n_seq = (len(refs) - 2) // 2
    ins, outs, blocks_ref, entered_ref = refs[:n_seq], refs[n_seq:-2], refs[-2], refs[-1]
    _, rows, hw = entered_ref.shape
    held = max(1, rows // hw)
    part = rows // held
    for d in range(n_seq):
        blocks_ref[me_ref[0] ^ d] = ins[d][...]
    for j in range(held):
        running = jnp.zeros((part, hw), F32)
        entered_ref[0, j * part : (j + 1) * part, :] = running.astype(BF16)
        for b in range(1, n_seq):
            notes = blocks_ref[b - 1, rows:, :].astype(F32)
            gain = notes[j : j + 1] + notes[held + j : held + j + 1]
            first = blocks_ref[b, rows:, :].astype(F32)[2 * held : 2 * held + 1]
            joined = (first == notes[2 * held + 1 : 2 * held + 2]).astype(F32)
            state = blocks_ref[b - 1, j * part : (j + 1) * part, :].astype(F32)
            running = (state + gain * running) * joined
            entered_ref[b, j * part : (j + 1) * part, :] = running.astype(BF16)
    for d in range(n_seq):
        outs[d][...] = entered_ref[me_ref[0] ^ d]


def attend_kernel(
    me_ref, doc_ref, sum_ref, sum_rows_ref, q_ref, k_ref, v_ref, gain_ref, *refs
):
    ins, out_ref, carried_ref = refs[:-2], refs[-2], refs[-1]
    tokens, heads = sum_ref.shape
    hw = q_ref.shape[1] // heads
    rows = ins[0].shape[0]
    for d in range(len(ins)):
        start = pl.multiple_of((me_ref[0] ^ d) * rows, rows)
        carried_ref[pl.ds(start, rows), :] = ins[d][...]
    doc = doc_ref[...]
    column = doc_column(doc)
    row = lax.broadcasted_iota(jnp.int32, (tokens, tokens), 0)
    col = lax.broadcasted_iota(jnp.int32, (tokens, tokens), 1)
    kept = (col <= row) & (column == doc)
    reach = jnp.exp(sum_ref[...]) * (column[:, :1] == doc[:, :1]).astype(F32)
    for i in range(heads):
        lanes = slice(i * hw, (i + 1) * hw)
        gap = sum_ref[:, i : i + 1] - sum_rows_ref[i : i + 1, :]
        fade = jnp.where(kept, jnp.exp(jnp.minimum(gap, 0.0)), 0.0)
        scores = lax.dot_general(
            q_ref[:, lanes], k_ref[:, lanes], (((1,), (1,)), ((), ())), preferred_element_type=F32
        )
        raw = jnp.dot((scores * fade).astype(BF16), v_ref[:, lanes], preferred_element_type=F32)
        outside = jnp.dot(q_ref[:, lanes], carried_ref[lanes, :], preferred_element_type=F32)
        raw = raw + outside * reach[:, i : i + 1]
        scale = lax.rsqrt(jnp.mean(raw * raw, axis=1, keepdims=True) + EPSILON)
        out_ref[:, lanes] = (raw * scale * gain_ref[:, lanes]).astype(BF16)


def pack_kernel(me_ref, gain_ref, *refs):
    ins, out_ref = refs[:-1], refs[-1]
    part, depth = ins[0].shape[1], out_ref.shape[1]
    squares = 0.0
    for ref in ins:
        value = ref[...].astype(F32)
        squares = squares + jnp.sum(value * value, axis=1, keepdims=True)
    scale = lax.rsqrt(squares / depth + EPSILON)
    for k, ref in enumerate(ins):
        lanes = pl.ds(pl.multiple_of((me_ref[0] ^ k) * part, 128), part)
        out_ref[:, lanes] = (ref[...].astype(F32) * scale * gain_ref[:, lanes]).astype(BF16)


def route_kernel(shifts, me_ref, *refs):
    ins, outs, stage_ref = refs[: len(shifts)], refs[len(shifts) : -1], refs[-1]
    count, me = len(outs), me_ref[0]
    for (up, down), ref in zip(shifts, ins):
        if not up and not down:
            stage_ref[me] = ref[...]
        if up:

            @pl.when(me >= up)
            def _(up=up, ref=ref):
                stage_ref[me - up] = ref[...]

        if down:

            @pl.when(me < count - down)
            def _(down=down, ref=ref):
                stage_ref[me + down] = ref[...]

    for m in range(count):
        outs[m][...] = stage_ref[(me_ref[1] + m) % count]


def dispatch_kernel(n_head, residual_ref, take_ref, *refs):
    total = residual_ref[...].astype(F32)
    sums = refs[0][...].astype(F32)
    for ref in refs[1:n_head]:
        sums = sums + ref[...].astype(F32)
    middle_ref, outs = refs[n_head], refs[n_head + 1 :]
    middle = (total + sums).astype(BF16)
    middle_ref[...] = middle
    count = outs[0].shape[0]
    rows = jnp.dot(take_ref[...], middle, preferred_element_type=F32).astype(BF16)
    for d in range(len(outs)):
        outs[d][...] = rows[d * count : (d + 1) * count]


def sum_kernel(nz, me_ref, *refs):
    ins, outs, stage_ref = refs[: len(refs) - 1 - nz], refs[len(refs) - 1 - nz : -1], refs[-1]
    total = ins[0][...].astype(F32)
    for ref in ins[1:]:
        total = total + ref[...].astype(F32)
    stage_ref[...] = total.astype(BF16)
    count = outs[0].shape[0]
    for k in range(nz):
        start = pl.multiple_of((me_ref[0] ^ k) * count, count)
        outs[k][...] = stage_ref[pl.ds(start, count), :]


def mix_kernel(middle_ref, mix_ref, *refs):
    ins, out_ref, rows_ref = refs[:-2], refs[-2], refs[-1]
    count = ins[0].shape[0]
    for d in range(len(ins)):
        rows_ref[d * count : (d + 1) * count, :] = ins[d][...]
    mix = mix_ref[...]
    high = mix.astype(BF16)
    low = (mix - high.astype(F32)).astype(BF16)
    rows = rows_ref[...]
    total = jnp.dot(high, rows, preferred_element_type=F32)
    total = total + jnp.dot(low, rows, preferred_element_type=F32)
    out_ref[...] = (middle_ref[...].astype(F32) + total).astype(BF16)


def wide_copies(gate_ref, up_ref, wide_ref, sems, steps, aligned):
    width = gate_ref.shape[2] // steps
    copies = []
    for j in range(steps):
        for k, weight in enumerate((gate_ref, up_ref)):
            source, target = weight.at[0], wide_ref.at[k]
            if aligned:
                source = weight.at[0, :, pl.ds(j * width, width)]
                target = wide_ref.at[j, :, pl.ds(k * width, width)]
            copies.append(pltpu.make_async_copy(source, target, sems.at[j, k]))
    return copies


def low_copies(n_head, owner_ref, down_ref, low_ref, sems):
    part = low_ref.shape[2]
    copies = []
    for j in range(n_head):
        start = pl.multiple_of(owner_ref[n_head + j] * part, 128)
        source = down_ref.at[0, :, pl.ds(start, part)]
        copies.append(pltpu.make_async_copy(source, low_ref.at[j], sems.at[j]))
    return copies


def fill_hidden(aligned, owner_ref, pieces, rows_ref, wide_ref, hidden_ref, copies):
    steps = len(copies) // 2
    width = hidden_ref.shape[1] // steps
    count = pieces[0].shape[0]
    for i, piece in enumerate(pieces):
        lines = pl.ds(pl.multiple_of(owner_ref[i] * count, count), count)
        rows_ref[lines, :] = piece[...]
    for j in range(steps):
        copies[2 * j].wait()
        copies[2 * j + 1].wait()
        if aligned:
            both = jnp.dot(rows_ref[...], wide_ref[j], preferred_element_type=F32)
            gate, up = both[:, :width], both[:, width:]
        else:
            gate = jnp.dot(rows_ref[...], wide_ref[0], preferred_element_type=F32)
            up = jnp.dot(rows_ref[...], wide_ref[1], preferred_element_type=F32)
        hidden = (gate / (1.0 + jnp.exp(-gate)) * up).astype(BF16)
        hidden_ref[:, j * width : (j + 1) * width] = hidden


def write_out(hidden_ref, low_ref, sent_ref, kept_ref, copies):
    nx = sent_ref.shape[0]
    for j, copy in enumerate(copies):
        copy.wait()
        out = jnp.dot(hidden_ref[...], low_ref[j], preferred_element_type=F32).astype(BF16)
        if j < nx:
            sent_ref[j] = out
        else:
            kept_ref[j - nx] = out


def hidden_kernel(n_head, steps, aligned, owner_ref, *refs):
    pieces = refs[:n_head]
    gate_ref, up_ref, hidden_ref, rows_ref, wide_ref, wide_sem = refs[n_head:]
    wide = wide_copies(gate_ref, up_ref, wide_ref, wide_sem, steps, aligned)
    for copy in wide:
        copy.start()
    fill_hidden(aligned, owner_ref, pieces, rows_ref, wide_ref, hidden_ref, wide)


def down_kernel(n_head, owner_ref, hidden_ref, down_ref, sent_ref, kept_ref, low_ref, low_sem):
    low = low_copies(n_head, owner_ref, down_ref, low_ref, low_sem)
    for copy in low:
        copy.start()
    write_out(hidden_ref, low_ref, sent_ref, kept_ref, low)


def expert_call(owners, pieces, gate_weight, up_weight, down_weight, before_down):
    n_head = len(pieces)
    _, depth, units = gate_weight.shape
    count, part = pieces[0].shape[0] * n_head, depth // n_head
    width = next((w for w in (384, 256, 128) if units % w == 0), units)
    aligned = width % 128 == 0
    steps, nx = units // width, n_head // CORES
    struct = jax.ShapeDtypeStruct
    rows = pltpu.VMEM((count, depth), BF16)
    wide = pltpu.VMEM((steps, depth, 2 * width) if aligned else (2, depth, width), BF16)
    low = pltpu.VMEM((n_head, units, part), BF16)
    wide_sem, low_sem = pltpu.SemaphoreType.DMA((steps, 2)), pltpu.SemaphoreType.DMA((n_head,))
    outs = [struct((nx, count, part), BF16), struct((n_head - nx, count, part), BF16)]
    hidden = struct((count, units), BF16)
    work = 2 * count * depth * units
    hidden = local_call(
        functools.partial(hidden_kernel, n_head, steps, aligned),
        "hidden",
        hidden,
        2 * work,
        owners,
        *pieces,
        gate_weight,
        up_weight,
        scratch=[rows, wide, wide_sem],
        scalars=1,
        far=2,
        vmem=EXPERT_VMEM,
    )
    hidden = lax.optimization_barrier((hidden, before_down))[0]
    return local_call(
        functools.partial(down_kernel, n_head),
        "down",
        outs,
        work,
        owners,
        hidden,
        down_weight,
        scratch=[low, low_sem],
        scalars=1,
        far=1,
        vmem=EXPERT_VMEM,
    )


def local_call(
    kernel, name, out_shape, flops, *operands, scratch=(), scalars=0, far=0, vmem=SMALL_VMEM
):
    shapes = out_shape if isinstance(out_shape, list) else [out_shape]
    sizes = [math.prod(o.shape) * o.dtype.itemsize for o in [*operands, *shapes]]
    return pl.pallas_call(
        kernel,
        out_shape=out_shape,
        in_specs=[pl.BlockSpec(memory_space=pltpu.SMEM)] * scalars
        + [pl.BlockSpec(memory_space=pltpu.VMEM)] * (len(operands) - scalars - far)
        + [pl.BlockSpec(memory_space=pltpu.HBM)] * far,
        scratch_shapes=list(scratch),
        compiler_params=pltpu.CompilerParams(vmem_limit_bytes=vmem),
        cost_estimate=pl.CostEstimate(flops=flops, bytes_accessed=sum(sizes), transcendentals=0),
        name=name,
    )(*operands)


def slot_places(routing, experts, capacity):
    tokens = routing.shape[0]
    flat_ids = routing.reshape(-1)
    hits = (flat_ids[:, None] == jnp.arange(experts, dtype=jnp.int32)[None, :]).astype(F32)
    pair_row = lax.broadcasted_iota(jnp.int32, (2 * tokens, 2 * tokens), 0)
    pair_col = lax.broadcasted_iota(jnp.int32, (2 * tokens, 2 * tokens), 1)
    earlier = jnp.dot((pair_col < pair_row).astype(F32), hits)
    rank = jnp.sum(earlier * hits, axis=1).astype(jnp.int32)
    return (flat_ids * capacity + rank).reshape(tokens, 2)


def shards(
    queries,
    key_vectors,
    value_vectors,
    log_decay,
    doc_ids,
    head_gain,
    output_weight,
    residual,
    norm_gain,
    routing,
    route_weights,
    gate_weight,
    up_weight,
    down_weight,
):
    tokens, heads = log_decay.shape
    hw = queries.shape[1] // heads
    n_seq, n_head = lax.axis_size("seq"), lax.axis_size("head")
    ny, nz, nx = n_seq // n_head, n_head, n_head // CORES
    s, h = lax.axis_index("seq"), lax.axis_index("head")
    z, y = s // ny, s % ny
    x, c = h // CORES, h % CORES
    part = residual.shape[1]
    model_width = part * n_head

    struct = jax.ShapeDtypeStruct
    spots = [
        ((zz * ny + yy) * n_head + hh, (hh * ny + yy) * n_head + zz)
        for zz in range(nz)
        for yy in range(ny)
        for hh in range(n_head)
    ]
    crossed = lambda value: lax.ppermute(value, ("seq", "head"), spots)

    experts = n_seq
    capacity = 4 * tokens // experts
    me = s.astype(jnp.int32).reshape(1)
    doc_row = doc_ids.reshape(1, tokens)
    rows, held, extra = chunk_plan(heads, hw, n_seq)
    work = 2 * tokens * hw * hw * heads
    *payload, decay_sum, decay_rows, doc_float = local_call(
        state_kernel,
        "block_state",
        [struct((rows + extra, hw), BF16)] * n_seq
        + [struct((tokens, heads), F32), struct((heads, tokens), F32), struct((1, tokens), F32)],
        work,
        me,
        doc_row,
        log_decay.T,
        key_vectors,
        value_vectors,
        scratch=[pltpu.VMEM((hw, hw), F32)],
        scalars=1,
    )
    lanes = max(128, routing.shape[1])
    ids = jnp.pad(routing.astype(BF16), ((0, 0), (0, lanes - routing.shape[1])))
    there = jnp.concatenate([residual, ids], axis=1)
    payload, there = lax.optimization_barrier((payload, there))
    there = crossed(there)
    arrived, there = lax.optimization_barrier((swap_seq(payload), there))
    entered = local_call(
        scan_kernel,
        "carry",
        [struct((rows, hw), BF16)] * n_seq,
        work,
        me,
        *arrived,
        scratch=[
            pltpu.VMEM((n_seq, rows + extra, hw), BF16),
            pltpu.VMEM((n_seq, rows, hw), BF16),
        ],
        scalars=1,
    )
    carried = swap_seq(entered)
    attended = local_call(
        attend_kernel,
        "attend",
        struct((tokens, heads * hw), BF16),
        3 * work,
        me,
        doc_float,
        decay_sum,
        decay_rows,
        queries,
        key_vectors,
        value_vectors,
        head_gain.reshape(1, heads * hw),
        *carried,
        scratch=[pltpu.VMEM((heads * hw, hw), BF16)],
        scalars=1,
    )

    attended, output_weight = lax.optimization_barrier((attended, output_weight))
    cols = output_weight.shape[1]
    w_z = jnp.zeros((output_weight.shape[0], ny * cols), BF16)
    w_z = lax.dynamic_update_slice(w_z, output_weight, (0, y * cols))
    for k in range(1, ny):
        got = permute_seq(output_weight, lambda q, k=k: q // ny * ny + (q % ny - k) % ny)
        w_z = lax.dynamic_update_slice(w_z, got, (0, (y + k) % ny * cols))

    def along(value, pairs):
        perm = [(a * ny + yy, b * ny + yy) for a, b in pairs for yy in range(ny)]
        return lax.ppermute(value, "seq", perm)

    ups = lambda j: [(q, q + j) for q in range(nz - j)]
    downs = lambda j: [(q + j, q) for q in range(nz - j)]
    below, above = along(attended, ups(1)), along(attended, downs(1))
    direct, there, own_routing = lax.optimization_barrier(
        (attended, there, routing, below, above)
    )[:3]
    residual_there = there[:, :part]
    routing_there = there[:, part : part + routing.shape[1]].astype(jnp.int32)
    slot = jnp.arange(experts * capacity, dtype=jnp.int32)
    slot = (slot // capacity ^ s) * capacity + slot % capacity
    place = slot_places(routing_there, experts, capacity)
    take = jnp.any(place[:, None, :] == slot[None, :, None], axis=2).astype(BF16).T
    place = slot_places(own_routing, experts, capacity)
    here = place[:, None, :] == slot[None, :, None]
    mix = jnp.sum(jnp.where(here, route_weights[:, None, :], 0.0), axis=2)
    shifts, rows_of = [(0, 0), (1, 0), (0, 1)], [attended, below, above]
    if nz > 2:
        shifts += [(2, 0), (0, 2)]
        rows_of += [along(below, ups(1)), along(above, downs(1))]
    for j in range(3, nz):
        if 2 * j >= nz:
            shifts.append((j, j))
            rows_of.append(along(direct, ups(j) + downs(j)))
        else:
            shifts += [(j, 0), (0, j)]
            rows_of += [along(direct, ups(j)), along(direct, downs(j))]
    products = [jnp.dot(r, w_z, preferred_element_type=F32).astype(BF16) for r in rows_of]
    products, take, mix = lax.optimization_barrier((products, take, mix))
    block = struct((tokens, part), BF16)
    place_me = jnp.stack([z, h]).astype(jnp.int32)
    own, *sent = local_call(
        functools.partial(route_kernel, shifts),
        "route",
        [block] * n_head,
        tokens * part,
        place_me,
        *products,
        scratch=[pltpu.VMEM((nz, tokens, part), BF16)],
        scalars=1,
    )
    sums = [own]
    for m in range(1, n_head):
        sums.append(permute_head(sent[m - 1], lambda q, m=m: (q + m) % n_head))
    middle_there, *outgoing = local_call(
        functools.partial(dispatch_kernel, n_head),
        "dispatch",
        [block] + [struct((capacity, part), BF16)] * experts,
        2 * tokens * tokens * 4 * part,
        residual_there,
        take,
        *sums,
    )

    in_owner = [h] + [(h + m * CORES) % n_head for m in range(1, nx)]
    in_owner += [
        o // CORES * CORES + (o % CORES + m) % CORES for o in in_owner for m in range(1, CORES)
    ]
    out_owner = [
        (x + m) % nx * CORES + (c + k) % CORES for k in [*range(1, CORES), 0] for m in range(nx)
    ]
    owners = jnp.stack(in_owner + out_owner + [z]).astype(jnp.int32)
    count = n_head * capacity
    returning = [None] * experts
    arrived = None
    gots, fars = [], []
    for group in range(ny):
        sends = [outgoing[k * ny + group] for k in range(nz)]
        if group:
            sends = lax.optimization_barrier((sends, arrived))[0]
        arrived = [
            permute_seq(sends[k], lambda q, d=k * ny + group: q ^ d) if k + group else sends[k]
            for k in range(nz)
        ]
        got = local_call(
            pack_kernel,
            "pack",
            struct((capacity, model_width), BF16),
            count * part,
            z.astype(jnp.int32).reshape(1),
            norm_gain.reshape(1, model_width),
            *arrived,
            scalars=1,
        )
        gots.append(got)
        fars.append(
            [permute_head(got, lambda q, m=m: (q - m * CORES) % n_head) for m in range(1, nx)]
        )
    for group in range(ny):
        got, far = gots[group], fars[group]
        if group + 1 < ny:
            far = lax.optimization_barrier((far, gots[group + 1]))[0]
        pieces = [got, *far]
        for piece in [got, *far]:
            for m in range(1, CORES):
                pieces.append(
                    permute_head(
                        piece, lambda q, m=m: q // CORES * CORES + (q % CORES - m) % CORES
                    )
                )
        first = [crossing, middle] if group else None
        if group + 1 < ny:
            first = (first, fars[group + 1])
        sent, kept = expert_call(owners, pieces, gate_weight, up_weight, down_weight, first)
        if group == 0:
            middle = crossed(lax.optimization_barrier((middle_there, sent))[0])

        near = permute_head(sent, lambda q: q // CORES * CORES + (q % CORES + 1) % CORES)
        near_sum = kept.astype(F32) + near.astype(F32)
        crossing = [near_sum[m].astype(BF16) for m in range(1, nx)]
        parts = [near_sum[0]]
        for m in range(1, nx):
            parts.append(permute_head(crossing[m - 1], lambda q, m=m: (q + m * CORES) % n_head))
        blocks = local_call(
            functools.partial(sum_kernel, nz),
            "total",
            [struct((capacity, part), BF16)] * nz,
            count * part * nx,
            z.astype(jnp.int32).reshape(1),
            *parts,
            scratch=[pltpu.VMEM((count, part), BF16)],
            scalars=1,
        )
        for k in range(nz):
            returning[k * ny + group] = blocks[k]
    return local_call(
        mix_kernel,
        "mix",
        block,
        4 * tokens * experts * capacity * part,
        middle,
        mix,
        *swap_seq(returning),
        scratch=[pltpu.VMEM((experts * capacity, part), BF16)],
    )


def solution(mesh):
    placed = (
        P("seq", "head"),
        P("seq", "head"),
        P("seq", "head"),
        P("seq", "head"),
        P("seq"),
        P("head"),
        P("head", "seq"),
        P("seq", "head"),
        P(),
        P("seq", None),
        P("seq", None),
        P("seq", None, "head"),
        P("seq", None, "head"),
        P("seq", "head", None),
    )
    return jax.shard_map(
        shards, mesh=mesh, in_specs=placed, out_specs=P("seq", "head"), check_vma=False
    )
```

```python
import functools
import math

import jax
import jax.numpy as jnp
from jax import lax
from jax.experimental import pallas as pl
from jax.experimental.pallas import tpu as pltpu
from jax.sharding import PartitionSpec as P

EPSILON = 1e-06
CORES = 2
F32 = jnp.float32
BF16 = jnp.bfloat16
HIGHEST = lax.Precision.HIGHEST
SMALL_VMEM = 12 * 1024 * 1024
EXPERT_VMEM = 48 * 1024 * 1024


def permute_seq(value, move):
    count = lax.axis_size("seq")
    return lax.ppermute(value, "seq", [(source, move(source)) for source in range(count)])


def permute_head(value, move):
    count = lax.axis_size("head")
    return lax.ppermute(value, "head", [(source, move(source)) for source in range(count)])


def swap_seq(blocks):
    swapped = [blocks[0]]
    for d in range(1, len(blocks)):
        swapped.append(permute_seq(blocks[d], lambda q, d=d: q ^ d))
    return swapped


def pick(stack, index, axis=0):
    return lax.dynamic_index_in_dim(stack, index, axis, keepdims=False)


def doc_column(doc):
    count = doc.shape[1]
    return jnp.broadcast_to(doc, (count, count)).T


def chunk_plan(heads, hw, n_seq):
    rows = heads * hw // n_seq
    held = max(1, rows // hw)
    extra = -(-(2 * held + 2) // 16) * 16
    return rows, held, extra


def state_kernel(me_ref, doc_ref, decay_ref, k_ref, v_ref, *refs):
    outs, refs = refs[:-6], refs[-6:]
    sum_ref, sum_rows_ref, doc_out_ref, k_out_ref, v_out_ref, state_ref = refs
    k_out_ref[...] = k_ref[...]
    v_out_ref[...] = v_ref[...]
    heads, tokens = decay_ref.shape
    n_seq, hw = len(outs), outs[0].shape[1]
    rows, held, extra = chunk_plan(heads, hw, n_seq)
    doc = doc_ref[...].astype(F32)
    row = lax.broadcasted_iota(jnp.int32, (tokens, tokens), 0)
    col = lax.broadcasted_iota(jnp.int32, (tokens, tokens), 1)
    doc_out_ref[...] = doc
    sums = lax.dot_general(
        (col <= row).astype(F32),
        decay_ref[...],
        (((1,), (1,)), ((), ())),
        precision=HIGHEST,
        preferred_element_type=F32,
    )
    sum_ref[...] = sums
    sum_rows_ref[...] = jnp.dot(
        decay_ref[...], (row <= col).astype(F32), precision=HIGHEST, preferred_element_type=F32
    )
    final = sums[tokens - 1 :, :]
    last = doc[:, tokens - 1 :]
    tail = jnp.exp(final - sums) * (doc_column(doc)[:, :1] == last).astype(F32)
    gain = jnp.exp(final) * (doc[:, :1] == last).astype(F32)
    lane = lax.broadcasted_iota(jnp.int32, (1, heads), 1)
    line = lax.broadcasted_iota(jnp.int32, (extra, hw), 0)
    for d in reversed(range(n_seq)):
        chunk = me_ref[0] ^ d
        note = jnp.where(line == 2 * held, doc[:, :1], 0.0)
        note = jnp.where(line == 2 * held + 1, last, note)
        for j in range(held):
            i = chunk * rows // hw + j
            mine = (lane == i).astype(F32)
            lanes = pl.ds(pl.multiple_of(i * hw, 128), hw)
            fade = jnp.sum(tail * mine, axis=1, keepdims=True)
            faded = (k_ref[:, lanes].astype(F32) * fade).astype(BF16)
            state = lax.dot_general(
                faded, v_ref[:, lanes], (((0,), (0,)), ((), ())), preferred_element_type=F32
            )
            if rows >= hw:
                outs[d][j * hw : (j + 1) * hw, :] = state.astype(BF16)
            else:
                state_ref[...] = state
                start = pl.multiple_of(chunk % (hw // rows) * rows, rows)
                outs[d][:rows, :] = state_ref[pl.ds(start, rows), :].astype(BF16)
            whole = jnp.sum(gain * mine, axis=1, keepdims=True)
            high = whole.astype(BF16).astype(F32)
            note = jnp.where(line == j, high, note)
            note = jnp.where(line == held + j, whole - high, note)
        outs[d][rows:, :] = note.astype(BF16)


def scan_kernel(me_ref, *refs):
    n_seq = (len(refs) - 2) // 2
    ins, outs, blocks_ref, entered_ref = refs[:n_seq], refs[n_seq:-2], refs[-2], refs[-1]
    _, rows, hw = entered_ref.shape
    held = max(1, rows // hw)
    part = rows // held
    for d in range(n_seq):
        blocks_ref[me_ref[0] ^ d] = ins[d][...]
    for j in range(held):
        running = jnp.zeros((part, hw), F32)
        entered_ref[0, j * part : (j + 1) * part, :] = running.astype(BF16)
        for b in range(1, n_seq):
            notes = blocks_ref[b - 1, rows:, :].astype(F32)
            gain = notes[j : j + 1] + notes[held + j : held + j + 1]
            first = blocks_ref[b, rows:, :].astype(F32)[2 * held : 2 * held + 1]
            joined = (first == notes[2 * held + 1 : 2 * held + 2]).astype(F32)
            state = blocks_ref[b - 1, j * part : (j + 1) * part, :].astype(F32)
            running = (state + gain * running) * joined
            entered_ref[b, j * part : (j + 1) * part, :] = running.astype(BF16)
    for d in range(n_seq):
        outs[d][...] = entered_ref[me_ref[0] ^ d]


def attend_kernel(
    me_ref, doc_ref, sum_ref, sum_rows_ref, q_ref, k_ref, v_ref, gain_ref, *refs
):
    ins, out_ref, carried_ref = refs[:-2], refs[-2], refs[-1]
    tokens, heads = sum_ref.shape
    hw = q_ref.shape[1] // heads
    rows = ins[0].shape[0]
    for d in range(len(ins)):
        start = pl.multiple_of((me_ref[0] ^ d) * rows, rows)
        carried_ref[pl.ds(start, rows), :] = ins[d][...]
    doc = doc_ref[...]
    column = doc_column(doc)
    row = lax.broadcasted_iota(jnp.int32, (tokens, tokens), 0)
    col = lax.broadcasted_iota(jnp.int32, (tokens, tokens), 1)
    kept = (col <= row) & (column == doc)
    reach = jnp.exp(sum_ref[...]) * (column[:, :1] == doc[:, :1]).astype(F32)
    for i in range(heads):
        lanes = slice(i * hw, (i + 1) * hw)
        gap = sum_ref[:, i : i + 1] - sum_rows_ref[i : i + 1, :]
        fade = jnp.where(kept, jnp.exp(jnp.minimum(gap, 0.0)), 0.0)
        scores = lax.dot_general(
            q_ref[:, lanes], k_ref[:, lanes], (((1,), (1,)), ((), ())), preferred_element_type=F32
        )
        raw = jnp.dot((scores * fade).astype(BF16), v_ref[:, lanes], preferred_element_type=F32)
        outside = jnp.dot(q_ref[:, lanes], carried_ref[lanes, :], preferred_element_type=F32)
        raw = raw + outside * reach[:, i : i + 1]
        scale = lax.rsqrt(jnp.mean(raw * raw, axis=1, keepdims=True) + EPSILON)
        out_ref[:, lanes] = (raw * scale * gain_ref[:, lanes]).astype(BF16)


def pack_kernel(me_ref, gain_ref, *refs):
    ins, out_ref = refs[:-1], refs[-1]
    part, depth = ins[0].shape[1], out_ref.shape[1]
    squares = 0.0
    for ref in ins:
        value = ref[...].astype(F32)
        squares = squares + jnp.sum(value * value, axis=1, keepdims=True)
    scale = lax.rsqrt(squares / depth + EPSILON)
    for k, ref in enumerate(ins):
        lanes = pl.ds(pl.multiple_of((me_ref[0] ^ k) * part, 128), part)
        out_ref[:, lanes] = (ref[...].astype(F32) * scale * gain_ref[:, lanes]).astype(BF16)


def route_kernel(shifts, me_ref, *refs):
    ins, outs, stage_ref = refs[: len(shifts)], refs[len(shifts) : -1], refs[-1]
    count, me = len(outs), me_ref[0]
    for (up, down), ref in zip(shifts, ins):
        if not up and not down:
            stage_ref[me] = ref[...]
        if up:

            @pl.when(me >= up)
            def _(up=up, ref=ref):
                stage_ref[me - up] = ref[...]

        if down:

            @pl.when(me < count - down)
            def _(down=down, ref=ref):
                stage_ref[me + down] = ref[...]

    for m in range(count):
        outs[m][...] = stage_ref[(me_ref[1] + m) % count]


def dispatch_kernel(n_head, residual_ref, take_ref, *refs):
    total = residual_ref[...].astype(F32)
    sums = refs[0][...].astype(F32)
    for ref in refs[1:n_head]:
        sums = sums + ref[...].astype(F32)
    middle_ref, outs = refs[n_head], refs[n_head + 1 :]
    middle = (total + sums).astype(BF16)
    middle_ref[...] = middle
    count = outs[0].shape[0]
    rows = lax.dot_general(
        take_ref[...], middle, (((0,), (0,)), ((), ())), preferred_element_type=F32
    ).astype(BF16)
    for d in range(len(outs)):
        outs[d][...] = rows[d * count : (d + 1) * count]


def sum_kernel(nz, me_ref, *refs):
    ins, outs, stage_ref = refs[: len(refs) - 1 - nz], refs[len(refs) - 1 - nz : -1], refs[-1]
    total = ins[0][...].astype(F32)
    for ref in ins[1:]:
        total = total + ref[...].astype(F32)
    stage_ref[...] = total.astype(BF16)
    count = outs[0].shape[0]
    for k in range(nz):
        start = pl.multiple_of((me_ref[0] ^ k) * count, count)
        outs[k][...] = stage_ref[pl.ds(start, count), :]


def mix_kernel(middle_ref, mix_ref, *refs):
    ins, out_ref, rows_ref = refs[:-2], refs[-2], refs[-1]
    count = ins[0].shape[0]
    for d in range(len(ins)):
        rows_ref[d * count : (d + 1) * count, :] = ins[d][...]
    mix = mix_ref[...]
    high = mix.astype(BF16)
    low = (mix - high.astype(F32)).astype(BF16)
    rows = rows_ref[...]
    total = jnp.dot(high, rows, preferred_element_type=F32)
    total = total + jnp.dot(low, rows, preferred_element_type=F32)
    out_ref[...] = (middle_ref[...].astype(F32) + total).astype(BF16)


def wide_copies(gate_ref, up_ref, wide_ref, sems, steps, aligned):
    width = gate_ref.shape[2] // steps
    copies = []
    for j in range(steps):
        for k, weight in enumerate((gate_ref, up_ref)):
            source, target = weight.at[0], wide_ref.at[k]
            if aligned:
                source = weight.at[0, :, pl.ds(j * width, width)]
                target = wide_ref.at[j, :, pl.ds(k * width, width)]
            copies.append(pltpu.make_async_copy(source, target, sems.at[j, k]))
    return copies


def low_copies(n_head, owner_ref, down_ref, low_ref, sems):
    part = low_ref.shape[2]
    copies = []
    for j in range(n_head):
        start = pl.multiple_of(owner_ref[n_head + j] * part, 128)
        source = down_ref.at[0, :, pl.ds(start, part)]
        copies.append(pltpu.make_async_copy(source, low_ref.at[j], sems.at[j]))
    return copies


def fill_hidden(aligned, owner_ref, pieces, rows_ref, wide_ref, hidden_ref, copies):
    steps = len(copies) // 2
    width = hidden_ref.shape[1] // steps
    count = pieces[0].shape[0]
    for i, piece in enumerate(pieces):
        lines = pl.ds(pl.multiple_of(owner_ref[i] * count, count), count)
        rows_ref[lines, :] = piece[...]
    for j in range(steps):
        copies[2 * j].wait()
        copies[2 * j + 1].wait()
        if aligned:
            both = jnp.dot(rows_ref[...], wide_ref[j], preferred_element_type=F32)
            gate, up = both[:, :width], both[:, width:]
        else:
            gate = jnp.dot(rows_ref[...], wide_ref[0], preferred_element_type=F32)
            up = jnp.dot(rows_ref[...], wide_ref[1], preferred_element_type=F32)
        hidden = (gate / (1.0 + jnp.exp(-gate)) * up).astype(BF16)
        hidden_ref[:, j * width : (j + 1) * width] = hidden


def write_out(hidden_ref, low_ref, sent_ref, kept_ref, copies):
    nx = sent_ref.shape[0]
    for j, copy in enumerate(copies):
        copy.wait()
        out = jnp.dot(hidden_ref[...], low_ref[j], preferred_element_type=F32).astype(BF16)
        if j < nx:
            sent_ref[j] = out
        else:
            kept_ref[j - nx] = out


def hidden_kernel(n_head, steps, aligned, owner_ref, *refs):
    pieces = refs[:n_head]
    gate_ref, up_ref, hidden_ref, rows_ref, wide_ref, wide_sem = refs[n_head:]
    wide = wide_copies(gate_ref, up_ref, wide_ref, wide_sem, steps, aligned)
    for copy in wide:
        copy.start()
    fill_hidden(aligned, owner_ref, pieces, rows_ref, wide_ref, hidden_ref, wide)


def down_kernel(n_head, owner_ref, hidden_ref, down_ref, sent_ref, kept_ref, low_ref, low_sem):
    low = low_copies(n_head, owner_ref, down_ref, low_ref, low_sem)
    for copy in low:
        copy.start()
    write_out(hidden_ref, low_ref, sent_ref, kept_ref, low)


def expert_call(owners, pieces, gate_weight, up_weight, down_weight, before_down):
    n_head = len(pieces)
    _, depth, units = gate_weight.shape
    count, part = pieces[0].shape[0] * n_head, depth // n_head
    width = next((w for w in (384, 256, 128) if units % w == 0), units)
    aligned = width % 128 == 0
    steps, nx = units // width, n_head // CORES
    struct = jax.ShapeDtypeStruct
    rows = pltpu.VMEM((count, depth), BF16)
    wide = pltpu.VMEM((steps, depth, 2 * width) if aligned else (2, depth, width), BF16)
    low = pltpu.VMEM((n_head, units, part), BF16)
    wide_sem, low_sem = pltpu.SemaphoreType.DMA((steps, 2)), pltpu.SemaphoreType.DMA((n_head,))
    outs = [struct((nx, count, part), BF16), struct((n_head - nx, count, part), BF16)]
    hidden = struct((count, units), BF16)
    work = 2 * count * depth * units
    hidden = local_call(
        functools.partial(hidden_kernel, n_head, steps, aligned),
        "hidden",
        hidden,
        2 * work,
        owners,
        *pieces,
        gate_weight,
        up_weight,
        scratch=[rows, wide, wide_sem],
        scalars=1,
        far=2,
        vmem=EXPERT_VMEM,
    )
    hidden = lax.optimization_barrier((hidden, before_down))[0]
    return local_call(
        functools.partial(down_kernel, n_head),
        "down",
        outs,
        work,
        owners,
        hidden,
        down_weight,
        scratch=[low, low_sem],
        scalars=1,
        far=1,
        vmem=EXPERT_VMEM,
    )


def local_call(
    kernel, name, out_shape, flops, *operands, scratch=(), scalars=0, far=0, vmem=SMALL_VMEM
):
    shapes = out_shape if isinstance(out_shape, list) else [out_shape]
    sizes = [math.prod(o.shape) * o.dtype.itemsize for o in [*operands, *shapes]]
    return pl.pallas_call(
        kernel,
        out_shape=out_shape,
        in_specs=[pl.BlockSpec(memory_space=pltpu.SMEM)] * scalars
        + [pl.BlockSpec(memory_space=pltpu.VMEM)] * (len(operands) - scalars - far)
        + [pl.BlockSpec(memory_space=pltpu.HBM)] * far,
        scratch_shapes=list(scratch),
        compiler_params=pltpu.CompilerParams(vmem_limit_bytes=vmem),
        cost_estimate=pl.CostEstimate(flops=flops, bytes_accessed=sum(sizes), transcendentals=0),
        name=name,
    )(*operands)


def plan_kernel(capacity, me_ref, ids_ref, routing_ref, weights_ref, take_ref, mix_ref):
    tokens, slots = take_ref.shape
    experts = slots // capacity
    row = lax.broadcasted_iota(jnp.int32, (tokens, tokens), 0)
    col = lax.broadcasted_iota(jnp.int32, (tokens, tokens), 1)
    before = (col < row).astype(BF16)
    expert = lax.broadcasted_iota(jnp.int32, (tokens, experts), 1)
    slot = lax.broadcasted_iota(jnp.int32, (tokens, slots), 1)

    def found(ids):
        hits = [(expert == one).astype(F32) for one in ids]
        earlier = jnp.dot(before, (hits[0] + hits[1]).astype(BF16), preferred_element_type=F32)
        ranks = [jnp.sum(earlier * hit, axis=1, keepdims=True).astype(jnp.int32) for hit in hits]
        return [slot == (one ^ me_ref[0]) * capacity + rank for one, rank in zip(ids, ranks)]

    there = ids_ref[...].astype(F32).astype(jnp.int32)
    first, second = found([there[:, :1], there[:, 1:2]])
    take_ref[...] = (first | second).astype(F32).astype(BF16)
    first, second = found([routing_ref[:, :1], routing_ref[:, 1:2]])
    weights = weights_ref[...]
    mix_ref[...] = jnp.where(first, weights[:, :1], 0.0) + jnp.where(second, weights[:, 1:2], 0.0)


def shards(
    queries,
    key_vectors,
    value_vectors,
    log_decay,
    doc_ids,
    head_gain,
    output_weight,
    residual,
    norm_gain,
    routing,
    route_weights,
    gate_weight,
    up_weight,
    down_weight,
):
    tokens, heads = log_decay.shape
    hw = queries.shape[1] // heads
    n_seq, n_head = lax.axis_size("seq"), lax.axis_size("head")
    ny, nz, nx = n_seq // n_head, n_head, n_head // CORES
    s, h = lax.axis_index("seq"), lax.axis_index("head")
    z, y = s // ny, s % ny
    x, c = h // CORES, h % CORES
    part = residual.shape[1]
    model_width = part * n_head

    struct = jax.ShapeDtypeStruct
    spots = [
        ((zz * ny + yy) * n_head + hh, (hh * ny + yy) * n_head + zz)
        for zz in range(nz)
        for yy in range(ny)
        for hh in range(n_head)
    ]
    crossed = lambda value: lax.ppermute(value, ("seq", "head"), spots)

    experts = n_seq
    capacity = 4 * tokens // experts
    me = s.astype(jnp.int32).reshape(1)
    doc_row = doc_ids.reshape(1, tokens)
    rows, held, extra = chunk_plan(heads, hw, n_seq)
    work = 2 * tokens * hw * hw * heads
    *payload, decay_sum, decay_rows, doc_float, keys_near, values_near = local_call(
        state_kernel,
        "block_state",
        [struct((rows + extra, hw), BF16)] * n_seq
        + [struct((tokens, heads), F32), struct((heads, tokens), F32), struct((1, tokens), F32)]
        + [struct((tokens, heads * hw), BF16)] * 2,
        work,
        me,
        doc_row,
        log_decay.T,
        key_vectors,
        value_vectors,
        scratch=[pltpu.VMEM((hw, hw), F32)],
        scalars=1,
    )
    residual_there = crossed(residual)
    arrived, residual_there = lax.optimization_barrier((swap_seq(payload), residual_there))
    entered = local_call(
        scan_kernel,
        "carry",
        [struct((rows, hw), BF16)] * n_seq,
        work,
        me,
        *arrived,
        scratch=[
            pltpu.VMEM((n_seq, rows + extra, hw), BF16),
            pltpu.VMEM((n_seq, rows, hw), BF16),
        ],
        scalars=1,
    )
    carried, output_weight = lax.optimization_barrier((swap_seq(entered), output_weight))
    attended = local_call(
        attend_kernel,
        "attend",
        struct((tokens, heads * hw), BF16),
        3 * work,
        me,
        doc_float,
        decay_sum,
        decay_rows,
        queries,
        keys_near,
        values_near,
        head_gain.reshape(1, heads * hw),
        *carried,
        scratch=[pltpu.VMEM((heads * hw, hw), BF16)],
        scalars=1,
    )

    ids = jnp.pad(routing.astype(BF16), ((0, 0), (0, 128 - routing.shape[1])))
    ids = crossed(lax.optimization_barrier((ids, attended))[0])
    cols = output_weight.shape[1]
    w_z = jnp.zeros((output_weight.shape[0], ny * cols), BF16)
    w_z = lax.dynamic_update_slice(w_z, output_weight, (0, y * cols))
    for k in range(1, ny):
        got = permute_seq(output_weight, lambda q, k=k: q // ny * ny + (q % ny - k) % ny)
        w_z = lax.dynamic_update_slice(w_z, got, (0, (y + k) % ny * cols))

    def along(value, pairs):
        perm = [(a * ny + yy, b * ny + yy) for a, b in pairs for yy in range(ny)]
        return lax.ppermute(value, "seq", perm)

    ups = lambda j: [(q, q + j) for q in range(nz - j)]
    downs = lambda j: [(q + j, q) for q in range(nz - j)]
    below, above = along(attended, ups(1)), along(attended, downs(1))
    direct = lax.optimization_barrier((attended, below, above))[0]
    take, mix = local_call(
        functools.partial(plan_kernel, capacity),
        "plan",
        [struct((tokens, experts * capacity), BF16), struct((tokens, experts * capacity), F32)],
        4 * tokens * tokens * experts,
        me,
        ids,
        routing,
        route_weights,
        scalars=1,
    )
    shifts, rows_of = [(0, 0), (1, 0), (0, 1)], [attended, below, above]
    if nz > 2:
        shifts += [(2, 0), (0, 2)]
        rows_of += [along(below, ups(1)), along(above, downs(1))]
    for j in range(3, nz):
        if 2 * j >= nz:
            shifts.append((j, j))
            rows_of.append(along(direct, ups(j) + downs(j)))
        else:
            shifts += [(j, 0), (0, j)]
            rows_of += [along(direct, ups(j)), along(direct, downs(j))]
    products = [jnp.dot(r, w_z, preferred_element_type=F32).astype(BF16) for r in rows_of]
    products, take, mix = lax.optimization_barrier((products, take, mix))
    block = struct((tokens, part), BF16)
    place_me = jnp.stack([z, h]).astype(jnp.int32)
    own, *sent = local_call(
        functools.partial(route_kernel, shifts),
        "route",
        [block] * n_head,
        tokens * part,
        place_me,
        *products,
        scratch=[pltpu.VMEM((nz, tokens, part), BF16)],
        scalars=1,
    )
    sums = [own]
    for m in range(1, n_head):
        sums.append(permute_head(sent[m - 1], lambda q, m=m: (q + m) % n_head))
    middle_there, *outgoing = local_call(
        functools.partial(dispatch_kernel, n_head),
        "dispatch",
        [block] + [struct((capacity, part), BF16)] * experts,
        2 * tokens * tokens * 4 * part,
        residual_there,
        take,
        *sums,
    )

    in_owner = [h] + [(h + m * CORES) % n_head for m in range(1, nx)]
    in_owner += [
        o // CORES * CORES + (o % CORES + m) % CORES for o in in_owner for m in range(1, CORES)
    ]
    out_owner = [
        (x + m) % nx * CORES + (c + k) % CORES for k in [*range(1, CORES), 0] for m in range(nx)
    ]
    owners = jnp.stack(in_owner + out_owner + [z]).astype(jnp.int32)
    count = n_head * capacity
    returning = [None] * experts
    arrived = None
    gots, fars = [], []
    for group in range(ny):
        sends = [outgoing[k * ny + group] for k in range(nz)]
        if group:
            sends = lax.optimization_barrier((sends, arrived))[0]
        arrived = [
            permute_seq(sends[k], lambda q, d=k * ny + group: q ^ d) if k + group else sends[k]
            for k in range(nz)
        ]
        got = local_call(
            pack_kernel,
            "pack",
            struct((capacity, model_width), BF16),
            count * part,
            z.astype(jnp.int32).reshape(1),
            norm_gain.reshape(1, model_width),
            *arrived,
            scalars=1,
        )
        gots.append(got)
        fars.append(
            [permute_head(got, lambda q, m=m: (q - m * CORES) % n_head) for m in range(1, nx)]
        )
    for group in range(ny):
        got, far = gots[group], fars[group]
        if group + 1 < ny:
            far = lax.optimization_barrier((far, gots[group + 1]))[0]
        pieces = [got, *far]
        for piece in [got, *far]:
            for m in range(1, CORES):
                pieces.append(
                    permute_head(
                        piece, lambda q, m=m: q // CORES * CORES + (q % CORES - m) % CORES
                    )
                )
        first = [crossing, middle] if group else None
        if group + 1 < ny:
            first = (first, fars[group + 1])
        sent, kept = expert_call(owners, pieces, gate_weight, up_weight, down_weight, first)
        if group == 0:
            middle = crossed(lax.optimization_barrier((middle_there, sent))[0])

        near = permute_head(sent, lambda q: q // CORES * CORES + (q % CORES + 1) % CORES)
        near_sum = kept.astype(F32) + near.astype(F32)
        crossing = [near_sum[m].astype(BF16) for m in range(1, nx)]
        parts = [near_sum[0]]
        for m in range(1, nx):
            parts.append(permute_head(crossing[m - 1], lambda q, m=m: (q + m * CORES) % n_head))
        blocks = local_call(
            functools.partial(sum_kernel, nz),
            "total",
            [struct((capacity, part), BF16)] * nz,
            count * part * nx,
            z.astype(jnp.int32).reshape(1),
            *parts,
            scratch=[pltpu.VMEM((count, part), BF16)],
            scalars=1,
        )
        for k in range(nz):
            returning[k * ny + group] = blocks[k]
    return local_call(
        mix_kernel,
        "mix",
        block,
        4 * tokens * experts * capacity * part,
        middle,
        mix,
        *swap_seq(returning),
        scratch=[pltpu.VMEM((experts * capacity, part), BF16)],
    )


def solution(mesh):
    placed = (
        P("seq", "head"),
        P("seq", "head"),
        P("seq", "head"),
        P("seq", "head"),
        P("seq"),
        P("head"),
        P("head", "seq"),
        P("seq", "head"),
        P(),
        P("seq", None),
        P("seq", None),
        P("seq", None, "head"),
        P("seq", None, "head"),
        P("seq", "head", None),
    )
    return jax.shard_map(
        shards, mesh=mesh, in_specs=placed, out_specs=P("seq", "head"), check_vma=False
    )
```

```python
import functools
import math

import jax
import jax.numpy as jnp
from jax import lax
from jax.experimental import pallas as pl
from jax.experimental.pallas import tpu as pltpu
from jax.sharding import PartitionSpec as P

EPSILON = 1e-06
CORES = 2
F32 = jnp.float32
BF16 = jnp.bfloat16
HIGHEST = lax.Precision.HIGHEST
SMALL_VMEM = 12 * 1024 * 1024
EXPERT_VMEM = 42 * 1024 * 1024


def permute_seq(value, move):
    count = lax.axis_size("seq")
    return lax.ppermute(value, "seq", [(source, move(source)) for source in range(count)])


def permute_head(value, move):
    count = lax.axis_size("head")
    return lax.ppermute(value, "head", [(source, move(source)) for source in range(count)])


def swap_seq(blocks):
    swapped = [blocks[0]]
    for d in range(1, len(blocks)):
        swapped.append(permute_seq(blocks[d], lambda q, d=d: q ^ d))
    return swapped


def pick(stack, index, axis=0):
    return lax.dynamic_index_in_dim(stack, index, axis, keepdims=False)


def doc_column(doc):
    count = doc.shape[1]
    return jnp.broadcast_to(doc, (count, count)).T


def chunk_plan(heads, hw, n_seq):
    rows = heads * hw // n_seq
    held = max(1, rows // hw)
    extra = -(-(2 * held + 2) // 16) * 16
    return rows, held, extra


def state_kernel(me_ref, doc_ref, decay_ref, k_ref, v_ref, *refs):
    outs, refs = refs[:-6], refs[-6:]
    sum_ref, sum_rows_ref, doc_out_ref, k_out_ref, v_out_ref, state_ref = refs
    k_out_ref[...] = k_ref[...]
    v_out_ref[...] = v_ref[...]
    heads, tokens = decay_ref.shape
    n_seq, hw = len(outs), outs[0].shape[1]
    rows, held, extra = chunk_plan(heads, hw, n_seq)
    doc = doc_ref[...].astype(F32)
    row = lax.broadcasted_iota(jnp.int32, (tokens, tokens), 0)
    col = lax.broadcasted_iota(jnp.int32, (tokens, tokens), 1)
    doc_out_ref[...] = doc
    sums = lax.dot_general(
        (col <= row).astype(F32),
        decay_ref[...],
        (((1,), (1,)), ((), ())),
        precision=HIGHEST,
        preferred_element_type=F32,
    )
    sum_ref[...] = sums
    sum_rows_ref[...] = jnp.dot(
        decay_ref[...], (row <= col).astype(F32), precision=HIGHEST, preferred_element_type=F32
    )
    final = sums[tokens - 1 :, :]
    last = doc[:, tokens - 1 :]
    tail = jnp.exp(final - sums) * (doc_column(doc)[:, :1] == last).astype(F32)
    gain = jnp.exp(final) * (doc[:, :1] == last).astype(F32)
    lane = lax.broadcasted_iota(jnp.int32, (1, heads), 1)
    line = lax.broadcasted_iota(jnp.int32, (extra, hw), 0)
    for d in reversed(range(n_seq)):
        chunk = me_ref[0] ^ d
        note = jnp.where(line == 2 * held, doc[:, :1], 0.0)
        note = jnp.where(line == 2 * held + 1, last, note)
        for j in range(held):
            i = chunk * rows // hw + j
            mine = (lane == i).astype(F32)
            lanes = pl.ds(pl.multiple_of(i * hw, 128), hw)
            fade = jnp.sum(tail * mine, axis=1, keepdims=True)
            faded = (k_ref[:, lanes].astype(F32) * fade).astype(BF16)
            state = lax.dot_general(
                faded, v_ref[:, lanes], (((0,), (0,)), ((), ())), preferred_element_type=F32
            )
            if rows >= hw:
                outs[d][j * hw : (j + 1) * hw, :] = state.astype(BF16)
            else:
                state_ref[...] = state
                start = pl.multiple_of(chunk % (hw // rows) * rows, rows)
                outs[d][:rows, :] = state_ref[pl.ds(start, rows), :].astype(BF16)
            whole = jnp.sum(gain * mine, axis=1, keepdims=True)
            high = whole.astype(BF16).astype(F32)
            note = jnp.where(line == j, high, note)
            note = jnp.where(line == held + j, whole - high, note)
        outs[d][rows:, :] = note.astype(BF16)


def scan_kernel(me_ref, *refs):
    n_seq = (len(refs) - 2) // 2
    ins, outs, blocks_ref, entered_ref = refs[:n_seq], refs[n_seq:-2], refs[-2], refs[-1]
    _, rows, hw = entered_ref.shape
    held = max(1, rows // hw)
    part = rows // held
    for d in range(n_seq):
        blocks_ref[me_ref[0] ^ d] = ins[d][...]
    for j in range(held):
        running = jnp.zeros((part, hw), F32)
        entered_ref[0, j * part : (j + 1) * part, :] = running.astype(BF16)
        for b in range(1, n_seq):
            notes = blocks_ref[b - 1, rows:, :].astype(F32)
            gain = notes[j : j + 1] + notes[held + j : held + j + 1]
            first = blocks_ref[b, rows:, :].astype(F32)[2 * held : 2 * held + 1]
            joined = (first == notes[2 * held + 1 : 2 * held + 2]).astype(F32)
            state = blocks_ref[b - 1, j * part : (j + 1) * part, :].astype(F32)
            running = (state + gain * running) * joined
            entered_ref[b, j * part : (j + 1) * part, :] = running.astype(BF16)
    for d in range(n_seq):
        outs[d][...] = entered_ref[me_ref[0] ^ d]


def attend_kernel(
    me_ref, doc_ref, sum_ref, sum_rows_ref, q_ref, k_ref, v_ref, gain_ref, *refs
):
    ins, out_ref, carried_ref = refs[:-2], refs[-2], refs[-1]
    tokens, heads = sum_ref.shape
    hw = q_ref.shape[1] // heads
    rows = ins[0].shape[0]
    for d in range(len(ins)):
        start = pl.multiple_of((me_ref[0] ^ d) * rows, rows)
        carried_ref[pl.ds(start, rows), :] = ins[d][...]
    doc = doc_ref[...]
    column = doc_column(doc)
    row = lax.broadcasted_iota(jnp.int32, (tokens, tokens), 0)
    col = lax.broadcasted_iota(jnp.int32, (tokens, tokens), 1)
    kept = (col <= row) & (column == doc)
    reach = jnp.exp(sum_ref[...]) * (column[:, :1] == doc[:, :1]).astype(F32)
    for i in range(heads):
        lanes = slice(i * hw, (i + 1) * hw)
        gap = sum_ref[:, i : i + 1] - sum_rows_ref[i : i + 1, :]
        fade = jnp.where(kept, jnp.exp(jnp.minimum(gap, 0.0)), 0.0)
        scores = lax.dot_general(
            q_ref[:, lanes], k_ref[:, lanes], (((1,), (1,)), ((), ())), preferred_element_type=F32
        )
        raw = jnp.dot((scores * fade).astype(BF16), v_ref[:, lanes], preferred_element_type=F32)
        outside = jnp.dot(q_ref[:, lanes], carried_ref[lanes, :], preferred_element_type=F32)
        raw = raw + outside * reach[:, i : i + 1]
        scale = lax.rsqrt(jnp.mean(raw * raw, axis=1, keepdims=True) + EPSILON)
        out_ref[:, lanes] = (raw * scale * gain_ref[:, lanes]).astype(BF16)


def pack_kernel(me_ref, gain_ref, *refs):
    ins, out_ref = refs[:-1], refs[-1]
    part, depth = ins[0].shape[1], out_ref.shape[1]
    squares = 0.0
    for ref in ins:
        value = ref[...].astype(F32)
        squares = squares + jnp.sum(value * value, axis=1, keepdims=True)
    scale = lax.rsqrt(squares / depth + EPSILON)
    for k, ref in enumerate(ins):
        lanes = pl.ds(pl.multiple_of((me_ref[0] ^ k) * part, 128), part)
        out_ref[:, lanes] = (ref[...].astype(F32) * scale * gain_ref[:, lanes]).astype(BF16)


def route_kernel(shifts, me_ref, *refs):
    ins, outs, stage_ref = refs[: len(shifts)], refs[len(shifts) : -1], refs[-1]
    count, me = len(outs), me_ref[0]
    for (up, down), ref in zip(shifts, ins):
        if not up and not down:
            stage_ref[me] = ref[...]
        if up:

            @pl.when(me >= up)
            def _(up=up, ref=ref):
                stage_ref[me - up] = ref[...]

        if down:

            @pl.when(me < count - down)
            def _(down=down, ref=ref):
                stage_ref[me + down] = ref[...]

    for m in range(count):
        outs[m][...] = stage_ref[(me_ref[1] + m) % count]


def dispatch_kernel(n_head, residual_ref, take_ref, *refs):
    total = residual_ref[...].astype(F32)
    sums = refs[0][...].astype(F32)
    for ref in refs[1:n_head]:
        sums = sums + ref[...].astype(F32)
    middle_ref, outs = refs[n_head], refs[n_head + 1 :]
    middle = (total + sums).astype(BF16)
    middle_ref[...] = middle
    count = outs[0].shape[0]
    rows = lax.dot_general(
        take_ref[...], middle, (((0,), (0,)), ((), ())), preferred_element_type=F32
    ).astype(BF16)
    for d in range(len(outs)):
        outs[d][...] = rows[d * count : (d + 1) * count]


def sum_kernel(nz, me_ref, *refs):
    ins, outs, stage_ref = refs[: len(refs) - 1 - nz], refs[len(refs) - 1 - nz : -1], refs[-1]
    total = ins[0][...].astype(F32)
    for ref in ins[1:]:
        total = total + ref[...].astype(F32)
    stage_ref[...] = total.astype(BF16)
    count = outs[0].shape[0]
    for k in range(nz):
        start = pl.multiple_of((me_ref[0] ^ k) * count, count)
        outs[k][...] = stage_ref[pl.ds(start, count), :]


def mix_kernel(middle_ref, mix_ref, *refs):
    ins, out_ref, rows_ref = refs[:-2], refs[-2], refs[-1]
    count = ins[0].shape[0]
    for d in range(len(ins)):
        rows_ref[d * count : (d + 1) * count, :] = ins[d][...]
    mix = mix_ref[...]
    high = mix.astype(BF16)
    low = (mix - high.astype(F32)).astype(BF16)
    rows = rows_ref[...]
    total = jnp.dot(high, rows, preferred_element_type=F32)
    total = total + jnp.dot(low, rows, preferred_element_type=F32)
    out_ref[...] = (middle_ref[...].astype(F32) + total).astype(BF16)


def wide_copies(gate_ref, up_ref, wide_ref, sems, steps, aligned):
    width = gate_ref.shape[2] // steps
    copies = []
    for j in range(steps):
        for k, weight in enumerate((gate_ref, up_ref)):
            source, target = weight.at[0], wide_ref.at[k]
            if aligned:
                source = weight.at[0, :, pl.ds(j * width, width)]
                target = wide_ref.at[j, :, pl.ds(k * width, width)]
            copies.append(pltpu.make_async_copy(source, target, sems.at[j, k]))
    return copies


def low_copies(n_head, owner_ref, down_ref, low_ref, sems):
    part = low_ref.shape[2]
    copies = []
    for j in range(n_head):
        start = pl.multiple_of(owner_ref[n_head + j] * part, 128)
        source = down_ref.at[0, :, pl.ds(start, part)]
        copies.append(pltpu.make_async_copy(source, low_ref.at[j], sems.at[j]))
    return copies


def fill_hidden(aligned, owner_ref, pieces, rows_ref, wide_ref, hidden_ref, copies):
    steps = len(copies) // 2
    width = hidden_ref.shape[1] // steps
    count = pieces[0].shape[0]
    for i, piece in enumerate(pieces):
        lines = pl.ds(pl.multiple_of(owner_ref[i] * count, count), count)
        rows_ref[lines, :] = piece[...]
    for j in range(steps):
        copies[2 * j].wait()
        copies[2 * j + 1].wait()
        if aligned:
            both = jnp.dot(rows_ref[...], wide_ref[j], preferred_element_type=F32)
            gate, up = both[:, :width], both[:, width:]
        else:
            gate = jnp.dot(rows_ref[...], wide_ref[0], preferred_element_type=F32)
            up = jnp.dot(rows_ref[...], wide_ref[1], preferred_element_type=F32)
        hidden = (gate / (1.0 + jnp.exp(-gate)) * up).astype(BF16)
        hidden_ref[:, j * width : (j + 1) * width] = hidden


def hidden_kernel(n_head, steps, aligned, owner_ref, *refs):
    pieces = refs[:n_head]
    gate_ref, up_ref, down_ref, hidden_ref, low_ref = refs[n_head : n_head + 5]
    rows_ref, wide_ref, wide_sem, low_sem = refs[n_head + 5 :]
    wide = wide_copies(gate_ref, up_ref, wide_ref, wide_sem, steps, aligned)
    low = low_copies(n_head, owner_ref, down_ref, low_ref, low_sem)
    for copy in wide + low:
        copy.start()
    fill_hidden(aligned, owner_ref, pieces, rows_ref, wide_ref, hidden_ref, wide)
    for copy in low:
        copy.wait()


def down_kernel(hidden_ref, low_ref, sent_ref, kept_ref):
    nx = sent_ref.shape[0]
    for j in range(low_ref.shape[0]):
        out = jnp.dot(hidden_ref[...], low_ref[j], preferred_element_type=F32).astype(BF16)
        if j < nx:
            sent_ref[j] = out
        else:
            kept_ref[j - nx] = out


def expert_call(owners, pieces, gate_weight, up_weight, down_weight, before_down):
    n_head = len(pieces)
    _, depth, units = gate_weight.shape
    count, part = pieces[0].shape[0] * n_head, depth // n_head
    width = next((w for w in (384, 256, 128) if units % w == 0), units)
    aligned = width % 128 == 0
    steps, nx = units // width, n_head // CORES
    struct = jax.ShapeDtypeStruct
    rows = pltpu.VMEM((count, depth), BF16)
    wide = pltpu.VMEM((steps, depth, 2 * width) if aligned else (2, depth, width), BF16)
    wide_sem, low_sem = pltpu.SemaphoreType.DMA((steps, 2)), pltpu.SemaphoreType.DMA((n_head,))
    outs = [struct((nx, count, part), BF16), struct((n_head - nx, count, part), BF16)]
    hidden = struct((count, units), BF16)
    work = 2 * count * depth * units
    hidden, low = local_call(
        functools.partial(hidden_kernel, n_head, steps, aligned),
        "hidden",
        [hidden, struct((n_head, units, part), BF16)],
        2 * work,
        owners,
        *pieces,
        gate_weight,
        up_weight,
        down_weight,
        scratch=[rows, wide, wide_sem, low_sem],
        scalars=1,
        far=3,
        vmem=EXPERT_VMEM,
    )
    hidden = lax.optimization_barrier((hidden, before_down))[0]
    return local_call(
        down_kernel,
        "down",
        outs,
        work,
        hidden,
        low,
        vmem=EXPERT_VMEM,
    )


def local_call(
    kernel, name, out_shape, flops, *operands, scratch=(), scalars=0, far=0, vmem=SMALL_VMEM
):
    shapes = out_shape if isinstance(out_shape, list) else [out_shape]
    sizes = [math.prod(o.shape) * o.dtype.itemsize for o in [*operands, *shapes]]
    return pl.pallas_call(
        kernel,
        out_shape=out_shape,
        in_specs=[pl.BlockSpec(memory_space=pltpu.SMEM)] * scalars
        + [pl.BlockSpec(memory_space=pltpu.VMEM)] * (len(operands) - scalars - far)
        + [pl.BlockSpec(memory_space=pltpu.HBM)] * far,
        scratch_shapes=list(scratch),
        compiler_params=pltpu.CompilerParams(vmem_limit_bytes=vmem),
        cost_estimate=pl.CostEstimate(flops=flops, bytes_accessed=sum(sizes), transcendentals=0),
        name=name,
    )(*operands)


def plan_kernel(capacity, me_ref, ids_ref, routing_ref, weights_ref, take_ref, mix_ref):
    tokens, slots = take_ref.shape
    experts = slots // capacity
    row = lax.broadcasted_iota(jnp.int32, (tokens, tokens), 0)
    col = lax.broadcasted_iota(jnp.int32, (tokens, tokens), 1)
    before = (col < row).astype(BF16)
    expert = lax.broadcasted_iota(jnp.int32, (tokens, experts), 1)
    slot = lax.broadcasted_iota(jnp.int32, (tokens, slots), 1)

    def found(ids):
        hits = [(expert == one).astype(F32) for one in ids]
        earlier = jnp.dot(before, (hits[0] + hits[1]).astype(BF16), preferred_element_type=F32)
        ranks = [jnp.sum(earlier * hit, axis=1, keepdims=True).astype(jnp.int32) for hit in hits]
        return [slot == (one ^ me_ref[0]) * capacity + rank for one, rank in zip(ids, ranks)]

    there = ids_ref[...].astype(F32).astype(jnp.int32)
    first, second = found([there[:, :1], there[:, 1:2]])
    take_ref[...] = (first | second).astype(F32).astype(BF16)
    first, second = found([routing_ref[:, :1], routing_ref[:, 1:2]])
    weights = weights_ref[...]
    mix_ref[...] = jnp.where(first, weights[:, :1], 0.0) + jnp.where(second, weights[:, 1:2], 0.0)


def shards(
    queries,
    key_vectors,
    value_vectors,
    log_decay,
    doc_ids,
    head_gain,
    output_weight,
    residual,
    norm_gain,
    routing,
    route_weights,
    gate_weight,
    up_weight,
    down_weight,
):
    tokens, heads = log_decay.shape
    hw = queries.shape[1] // heads
    n_seq, n_head = lax.axis_size("seq"), lax.axis_size("head")
    ny, nz, nx = n_seq // n_head, n_head, n_head // CORES
    s, h = lax.axis_index("seq"), lax.axis_index("head")
    z, y = s // ny, s % ny
    x, c = h // CORES, h % CORES
    part = residual.shape[1]
    model_width = part * n_head

    struct = jax.ShapeDtypeStruct
    spots = [
        ((zz * ny + yy) * n_head + hh, (hh * ny + yy) * n_head + zz)
        for zz in range(nz)
        for yy in range(ny)
        for hh in range(n_head)
    ]
    crossed = lambda value: lax.ppermute(value, ("seq", "head"), spots)

    experts = n_seq
    capacity = 4 * tokens // experts
    me = s.astype(jnp.int32).reshape(1)
    doc_row = doc_ids.reshape(1, tokens)
    rows, held, extra = chunk_plan(heads, hw, n_seq)
    work = 2 * tokens * hw * hw * heads
    *payload, decay_sum, decay_rows, doc_float, keys_near, values_near = local_call(
        state_kernel,
        "block_state",
        [struct((rows + extra, hw), BF16)] * n_seq
        + [struct((tokens, heads), F32), struct((heads, tokens), F32), struct((1, tokens), F32)]
        + [struct((tokens, heads * hw), BF16)] * 2,
        work,
        me,
        doc_row,
        log_decay.T,
        key_vectors,
        value_vectors,
        scratch=[pltpu.VMEM((hw, hw), F32)],
        scalars=1,
    )
    residual_there = crossed(residual)
    arrived, residual_there = lax.optimization_barrier((swap_seq(payload), residual_there))
    entered = local_call(
        scan_kernel,
        "carry",
        [struct((rows, hw), BF16)] * n_seq,
        work,
        me,
        *arrived,
        scratch=[
            pltpu.VMEM((n_seq, rows + extra, hw), BF16),
            pltpu.VMEM((n_seq, rows, hw), BF16),
        ],
        scalars=1,
    )
    carried, output_weight = lax.optimization_barrier((swap_seq(entered), output_weight))
    attended = local_call(
        attend_kernel,
        "attend",
        struct((tokens, heads * hw), BF16),
        3 * work,
        me,
        doc_float,
        decay_sum,
        decay_rows,
        queries,
        keys_near,
        values_near,
        head_gain.reshape(1, heads * hw),
        *carried,
        scratch=[pltpu.VMEM((heads * hw, hw), BF16)],
        scalars=1,
    )

    ids = jnp.pad(routing.astype(BF16), ((0, 0), (0, 128 - routing.shape[1])))
    ids = crossed(lax.optimization_barrier((ids, attended))[0])
    cols = output_weight.shape[1]
    w_z = jnp.zeros((output_weight.shape[0], ny * cols), BF16)
    w_z = lax.dynamic_update_slice(w_z, output_weight, (0, y * cols))
    for k in range(1, ny):
        got = permute_seq(output_weight, lambda q, k=k: q // ny * ny + (q % ny - k) % ny)
        w_z = lax.dynamic_update_slice(w_z, got, (0, (y + k) % ny * cols))

    def along(value, pairs):
        perm = [(a * ny + yy, b * ny + yy) for a, b in pairs for yy in range(ny)]
        return lax.ppermute(value, "seq", perm)

    ups = lambda j: [(q, q + j) for q in range(nz - j)]
    downs = lambda j: [(q + j, q) for q in range(nz - j)]
    below, above = along(attended, ups(1)), along(attended, downs(1))
    take, mix = local_call(
        functools.partial(plan_kernel, capacity),
        "plan",
        [struct((tokens, experts * capacity), BF16), struct((tokens, experts * capacity), F32)],
        4 * tokens * tokens * experts,
        me,
        ids,
        routing,
        route_weights,
        scalars=1,
    )
    shifts, rows_of = [(0, 0), (1, 0), (0, 1)], [attended, below, above]
    if nz > 2:
        shifts += [(2, 0), (0, 2)]
        rows_of += [along(below, ups(1)), along(above, downs(1))]
    for j in range(3, nz):
        if 2 * j >= nz:
            shifts.append((j, j))
            rows_of.append(along(attended, ups(j) + downs(j)))
        else:
            shifts += [(j, 0), (0, j)]
            rows_of += [along(attended, ups(j)), along(attended, downs(j))]
    products = [jnp.dot(r, w_z, preferred_element_type=F32).astype(BF16) for r in rows_of]
    products, take, mix = lax.optimization_barrier((products, take, mix))
    block = struct((tokens, part), BF16)
    place_me = jnp.stack([z, h]).astype(jnp.int32)
    own, *sent = local_call(
        functools.partial(route_kernel, shifts),
        "route",
        [block] * n_head,
        tokens * part,
        place_me,
        *products,
        scratch=[pltpu.VMEM((nz, tokens, part), BF16)],
        scalars=1,
    )
    sums = [own]
    for m in range(1, n_head):
        sums.append(permute_head(sent[m - 1], lambda q, m=m: (q + m) % n_head))
    middle_there, *outgoing = local_call(
        functools.partial(dispatch_kernel, n_head),
        "dispatch",
        [block] + [struct((capacity, part), BF16)] * experts,
        2 * tokens * tokens * 4 * part,
        residual_there,
        take,
        *sums,
    )

    in_owner = [h] + [(h + m * CORES) % n_head for m in range(1, nx)]
    in_owner += [
        o // CORES * CORES + (o % CORES + m) % CORES for o in in_owner for m in range(1, CORES)
    ]
    out_owner = [
        (x + m) % nx * CORES + (c + k) % CORES for k in [*range(1, CORES), 0] for m in range(nx)
    ]
    owners = jnp.stack(in_owner + out_owner + [z]).astype(jnp.int32)
    count = n_head * capacity
    returning = [None] * experts
    arrived = None
    gots, fars = [], []
    for group in range(ny):
        sends = [outgoing[k * ny + group] for k in range(nz)]
        if group:
            sends = lax.optimization_barrier((sends, arrived))[0]
        arrived = [
            permute_seq(sends[k], lambda q, d=k * ny + group: q ^ d) if k + group else sends[k]
            for k in range(nz)
        ]
        got = local_call(
            pack_kernel,
            "pack",
            struct((capacity, model_width), BF16),
            count * part,
            z.astype(jnp.int32).reshape(1),
            norm_gain.reshape(1, model_width),
            *arrived,
            scalars=1,
        )
        gots.append(got)
        fars.append(
            [permute_head(got, lambda q, m=m: (q - m * CORES) % n_head) for m in range(1, nx)]
        )
    for group in range(ny):
        got, far = gots[group], fars[group]
        if group + 1 < ny:
            far = lax.optimization_barrier((far, gots[group + 1]))[0]
        pieces = [got, *far]
        for piece in [got, *far]:
            for m in range(1, CORES):
                pieces.append(
                    permute_head(
                        piece, lambda q, m=m: q // CORES * CORES + (q % CORES - m) % CORES
                    )
                )
        first = [blocks, middle] if group else None
        if group + 1 < ny:
            first = (first, fars[group + 1])
        if group:
            pieces = lax.optimization_barrier((pieces, crossing))[0]
        sent, kept = expert_call(owners, pieces, gate_weight, up_weight, down_weight, first)
        if group == 0:
            middle = crossed(lax.optimization_barrier((middle_there, sent))[0])

        near = permute_head(sent, lambda q: q // CORES * CORES + (q % CORES + 1) % CORES)
        near_sum = kept.astype(F32) + near.astype(F32)
        crossing = [near_sum[m].astype(BF16) for m in range(1, nx)]
        parts = [near_sum[0]]
        for m in range(1, nx):
            parts.append(permute_head(crossing[m - 1], lambda q, m=m: (q + m * CORES) % n_head))
        blocks = local_call(
            functools.partial(sum_kernel, nz),
            "total",
            [struct((capacity, part), BF16)] * nz,
            count * part * nx,
            z.astype(jnp.int32).reshape(1),
            *parts,
            scratch=[pltpu.VMEM((count, part), BF16)],
            scalars=1,
        )
        for k in range(nz):
            returning[k * ny + group] = blocks[k]
    return local_call(
        mix_kernel,
        "mix",
        block,
        4 * tokens * experts * capacity * part,
        middle,
        mix,
        *swap_seq(returning),
        scratch=[pltpu.VMEM((experts * capacity, part), BF16)],
    )


def solution(mesh):
    placed = (
        P("seq", "head"),
        P("seq", "head"),
        P("seq", "head"),
        P("seq", "head"),
        P("seq"),
        P("head"),
        P("head", "seq"),
        P("seq", "head"),
        P(),
        P("seq", None),
        P("seq", None),
        P("seq", None, "head"),
        P("seq", None, "head"),
        P("seq", "head", None),
    )
    return jax.shard_map(
        shards, mesh=mesh, in_specs=placed, out_specs=P("seq", "head"), check_vma=False
    )
```

```python
import functools
import math

import jax
import jax.numpy as jnp
from jax import lax
from jax.experimental import pallas as pl
from jax.experimental.pallas import tpu as pltpu
from jax.sharding import PartitionSpec as P

EPSILON = 1e-06
CORES = 2
F32 = jnp.float32
BF16 = jnp.bfloat16
HIGHEST = lax.Precision.HIGHEST
SMALL_VMEM = 12 * 1024 * 1024
EXPERT_VMEM = 42 * 1024 * 1024


def permute_seq(value, move):
    count = lax.axis_size("seq")
    return lax.ppermute(value, "seq", [(source, move(source)) for source in range(count)])


def permute_head(value, move):
    count = lax.axis_size("head")
    return lax.ppermute(value, "head", [(source, move(source)) for source in range(count)])


def swap_seq(blocks):
    half = len(blocks) // 2
    order = [*range(2, min(3, half)), *reversed(range(half, len(blocks))), *range(3, half)]
    order += [d for d in range(1, len(blocks)) if d not in order]
    swapped = [permute_seq(blocks[d], lambda q, d=d: q ^ d) for d in order]
    swapped = dict(zip(order, lax.optimization_barrier(swapped)))
    return [blocks[0]] + [swapped[d] for d in range(1, len(blocks))]


def pick(stack, index, axis=0):
    return lax.dynamic_index_in_dim(stack, index, axis, keepdims=False)


def doc_column(doc):
    count = doc.shape[1]
    return jnp.broadcast_to(doc, (count, count)).T


def chunk_plan(heads, hw, n_seq):
    rows = heads * hw // n_seq
    held = max(1, rows // hw)
    extra = -(-(2 * held + 2) // 16) * 16
    return rows, held, extra


def state_kernel(me_ref, doc_ref, decay_ref, k_ref, v_ref, *refs):
    outs, refs = refs[:-6], refs[-6:]
    sum_ref, sum_rows_ref, doc_out_ref, k_out_ref, v_out_ref, state_ref = refs
    k_out_ref[...] = k_ref[...]
    v_out_ref[...] = v_ref[...]
    heads, tokens = decay_ref.shape
    n_seq, hw = len(outs), outs[0].shape[1]
    rows, held, extra = chunk_plan(heads, hw, n_seq)
    doc = doc_ref[...].astype(F32)
    row = lax.broadcasted_iota(jnp.int32, (tokens, tokens), 0)
    col = lax.broadcasted_iota(jnp.int32, (tokens, tokens), 1)
    doc_out_ref[...] = doc
    sums = lax.dot_general(
        (col <= row).astype(F32),
        decay_ref[...],
        (((1,), (1,)), ((), ())),
        precision=HIGHEST,
        preferred_element_type=F32,
    )
    sum_ref[...] = sums
    sum_rows_ref[...] = jnp.dot(
        decay_ref[...], (row <= col).astype(F32), precision=HIGHEST, preferred_element_type=F32
    )
    final = sums[tokens - 1 :, :]
    last = doc[:, tokens - 1 :]
    tail = jnp.exp(final - sums) * (doc_column(doc)[:, :1] == last).astype(F32)
    gain = jnp.exp(final) * (doc[:, :1] == last).astype(F32)
    lane = lax.broadcasted_iota(jnp.int32, (1, heads), 1)
    line = lax.broadcasted_iota(jnp.int32, (extra, hw), 0)
    for d in reversed(range(n_seq)):
        chunk = me_ref[0] ^ d
        note = jnp.where(line == 2 * held, doc[:, :1], 0.0)
        note = jnp.where(line == 2 * held + 1, last, note)
        for j in range(held):
            i = chunk * rows // hw + j
            mine = (lane == i).astype(F32)
            lanes = pl.ds(pl.multiple_of(i * hw, 128), hw)
            fade = jnp.sum(tail * mine, axis=1, keepdims=True)
            faded = (k_ref[:, lanes].astype(F32) * fade).astype(BF16)
            state = lax.dot_general(
                faded, v_ref[:, lanes], (((0,), (0,)), ((), ())), preferred_element_type=F32
            )
            if rows >= hw:
                outs[d][j * hw : (j + 1) * hw, :] = state.astype(BF16)
            else:
                state_ref[...] = state
                start = pl.multiple_of(chunk % (hw // rows) * rows, rows)
                outs[d][:rows, :] = state_ref[pl.ds(start, rows), :].astype(BF16)
            whole = jnp.sum(gain * mine, axis=1, keepdims=True)
            high = whole.astype(BF16).astype(F32)
            note = jnp.where(line == j, high, note)
            note = jnp.where(line == held + j, whole - high, note)
        outs[d][rows:, :] = note.astype(BF16)


def scan_kernel(me_ref, *refs):
    n_seq = (len(refs) - 2) // 2
    ins, outs, blocks_ref, entered_ref = refs[:n_seq], refs[n_seq:-2], refs[-2], refs[-1]
    _, rows, hw = entered_ref.shape
    held = max(1, rows // hw)
    part = rows // held
    for d in range(n_seq):
        blocks_ref[me_ref[0] ^ d] = ins[d][...]
    for j in range(held):
        running = jnp.zeros((part, hw), F32)
        entered_ref[0, j * part : (j + 1) * part, :] = running.astype(BF16)
        for b in range(1, n_seq):
            notes = blocks_ref[b - 1, rows:, :].astype(F32)
            gain = notes[j : j + 1] + notes[held + j : held + j + 1]
            first = blocks_ref[b, rows:, :].astype(F32)[2 * held : 2 * held + 1]
            joined = (first == notes[2 * held + 1 : 2 * held + 2]).astype(F32)
            state = blocks_ref[b - 1, j * part : (j + 1) * part, :].astype(F32)
            running = (state + gain * running) * joined
            entered_ref[b, j * part : (j + 1) * part, :] = running.astype(BF16)
    for d in range(n_seq):
        outs[d][...] = entered_ref[me_ref[0] ^ d]


def attend_kernel(
    me_ref, doc_ref, sum_ref, sum_rows_ref, q_ref, k_ref, v_ref, gain_ref, *refs
):
    ins, out_ref, carried_ref = refs[:-2], refs[-2], refs[-1]
    tokens, heads = sum_ref.shape
    hw = q_ref.shape[1] // heads
    rows = ins[0].shape[0]
    for d in range(len(ins)):
        start = pl.multiple_of((me_ref[0] ^ d) * rows, rows)
        carried_ref[pl.ds(start, rows), :] = ins[d][...]
    doc = doc_ref[...]
    column = doc_column(doc)
    row = lax.broadcasted_iota(jnp.int32, (tokens, tokens), 0)
    col = lax.broadcasted_iota(jnp.int32, (tokens, tokens), 1)
    kept = (col <= row) & (column == doc)
    reach = jnp.exp(sum_ref[...]) * (column[:, :1] == doc[:, :1]).astype(F32)
    for i in range(heads):
        lanes = slice(i * hw, (i + 1) * hw)
        gap = sum_ref[:, i : i + 1] - sum_rows_ref[i : i + 1, :]
        fade = jnp.where(kept, jnp.exp(jnp.minimum(gap, 0.0)), 0.0)
        scores = lax.dot_general(
            q_ref[:, lanes], k_ref[:, lanes], (((1,), (1,)), ((), ())), preferred_element_type=F32
        )
        raw = jnp.dot((scores * fade).astype(BF16), v_ref[:, lanes], preferred_element_type=F32)
        outside = jnp.dot(q_ref[:, lanes], carried_ref[lanes, :], preferred_element_type=F32)
        raw = raw + outside * reach[:, i : i + 1]
        scale = lax.rsqrt(jnp.mean(raw * raw, axis=1, keepdims=True) + EPSILON)
        out_ref[:, lanes] = (raw * scale * gain_ref[:, lanes]).astype(BF16)


def pack_kernel(me_ref, gain_ref, *refs):
    ins, out_ref = refs[:-1], refs[-1]
    part, depth = ins[0].shape[1], out_ref.shape[1]
    squares = 0.0
    for ref in ins:
        value = ref[...].astype(F32)
        squares = squares + jnp.sum(value * value, axis=1, keepdims=True)
    scale = lax.rsqrt(squares / depth + EPSILON)
    for k, ref in enumerate(ins):
        lanes = pl.ds(pl.multiple_of((me_ref[0] ^ k) * part, 128), part)
        out_ref[:, lanes] = (ref[...].astype(F32) * scale * gain_ref[:, lanes]).astype(BF16)


def route_kernel(shifts, me_ref, *refs):
    ins, outs, stage_ref = refs[: len(shifts)], refs[len(shifts) : -1], refs[-1]
    count, me = len(outs), me_ref[0]
    for (up, down), ref in zip(shifts, ins):
        if not up and not down:
            stage_ref[me] = ref[...]
        if up:

            @pl.when(me >= up)
            def _(up=up, ref=ref):
                stage_ref[me - up] = ref[...]

        if down:

            @pl.when(me < count - down)
            def _(down=down, ref=ref):
                stage_ref[me + down] = ref[...]

    for m in range(count):
        outs[m][...] = stage_ref[(me_ref[1] + m) % count]


def dispatch_kernel(n_head, residual_ref, take_ref, *refs):
    total = residual_ref[...].astype(F32)
    sums = refs[0][...].astype(F32)
    for ref in refs[1:n_head]:
        sums = sums + ref[...].astype(F32)
    middle_ref, outs = refs[n_head], refs[n_head + 1 :]
    middle = (total + sums).astype(BF16)
    middle_ref[...] = middle
    count = outs[0].shape[0]
    rows = lax.dot_general(
        take_ref[...], middle, (((0,), (0,)), ((), ())), preferred_element_type=F32
    ).astype(BF16)
    for d in range(len(outs)):
        outs[d][...] = rows[d * count : (d + 1) * count]


def sum_kernel(nz, me_ref, *refs):
    ins, outs, stage_ref = refs[: len(refs) - 1 - nz], refs[len(refs) - 1 - nz : -1], refs[-1]
    total = ins[0][...].astype(F32)
    for ref in ins[1:]:
        total = total + ref[...].astype(F32)
    stage_ref[...] = total.astype(BF16)
    count = outs[0].shape[0]
    for k in range(nz):
        start = pl.multiple_of((me_ref[0] ^ k) * count, count)
        outs[k][...] = stage_ref[pl.ds(start, count), :]


def mix_kernel(middle_ref, mix_ref, *refs):
    ins, out_ref, rows_ref = refs[:-2], refs[-2], refs[-1]
    count = ins[0].shape[0]
    for d in range(len(ins)):
        rows_ref[d * count : (d + 1) * count, :] = ins[d][...]
    mix = mix_ref[...]
    high = mix.astype(BF16)
    low = (mix - high.astype(F32)).astype(BF16)
    rows = rows_ref[...]
    total = jnp.dot(high, rows, preferred_element_type=F32)
    total = total + jnp.dot(low, rows, preferred_element_type=F32)
    out_ref[...] = (middle_ref[...].astype(F32) + total).astype(BF16)


def wide_copies(gate_ref, up_ref, wide_ref, sems, steps, aligned):
    width = gate_ref.shape[2] // steps
    copies = []
    for j in range(steps):
        for k, weight in enumerate((gate_ref, up_ref)):
            source, target = weight.at[0], wide_ref.at[k]
            if aligned:
                source = weight.at[0, :, pl.ds(j * width, width)]
                target = wide_ref.at[j, :, pl.ds(k * width, width)]
            copies.append(pltpu.make_async_copy(source, target, sems.at[j, k]))
    return copies


def low_copies(n_head, owner_ref, down_ref, low_ref, sems):
    part = low_ref.shape[2]
    copies = []
    for j in range(n_head):
        start = pl.multiple_of(owner_ref[n_head + j] * part, 128)
        source = down_ref.at[0, :, pl.ds(start, part)]
        copies.append(pltpu.make_async_copy(source, low_ref.at[j], sems.at[j]))
    return copies


def fill_hidden(aligned, owner_ref, pieces, rows_ref, wide_ref, hidden_ref, copies):
    steps = len(copies) // 2
    width = hidden_ref.shape[1] // steps
    count = pieces[0].shape[0]
    for i, piece in enumerate(pieces):
        lines = pl.ds(pl.multiple_of(owner_ref[i] * count, count), count)
        rows_ref[lines, :] = piece[...]
    for j in range(steps):
        copies[2 * j].wait()
        copies[2 * j + 1].wait()
        if aligned:
            both = jnp.dot(rows_ref[...], wide_ref[j], preferred_element_type=F32)
            gate, up = both[:, :width], both[:, width:]
        else:
            gate = jnp.dot(rows_ref[...], wide_ref[0], preferred_element_type=F32)
            up = jnp.dot(rows_ref[...], wide_ref[1], preferred_element_type=F32)
        hidden = (gate / (1.0 + jnp.exp(-gate)) * up).astype(BF16)
        hidden_ref[:, j * width : (j + 1) * width] = hidden


def hidden_kernel(n_head, steps, aligned, owner_ref, *refs):
    pieces = refs[:n_head]
    gate_ref, up_ref, down_ref, hidden_ref, low_ref = refs[n_head : n_head + 5]
    rows_ref, wide_ref, wide_sem, low_sem = refs[n_head + 5 :]
    wide = wide_copies(gate_ref, up_ref, wide_ref, wide_sem, steps, aligned)
    low = low_copies(n_head, owner_ref, down_ref, low_ref, low_sem)
    for copy in wide + low:
        copy.start()
    fill_hidden(aligned, owner_ref, pieces, rows_ref, wide_ref, hidden_ref, wide)
    for copy in low:
        copy.wait()


def down_kernel(hidden_ref, low_ref, sent_ref, kept_ref):
    nx = sent_ref.shape[0]
    for j in range(low_ref.shape[0]):
        out = jnp.dot(hidden_ref[...], low_ref[j], preferred_element_type=F32).astype(BF16)
        if j < nx:
            sent_ref[j] = out
        else:
            kept_ref[j - nx] = out


def expert_call(owners, pieces, gate_weight, up_weight, down_weight, before_down):
    n_head = len(pieces)
    _, depth, units = gate_weight.shape
    count, part = pieces[0].shape[0] * n_head, depth // n_head
    width = next((w for w in (384, 256, 128) if units % w == 0), units)
    aligned = width % 128 == 0
    steps, nx = units // width, n_head // CORES
    struct = jax.ShapeDtypeStruct
    rows = pltpu.VMEM((count, depth), BF16)
    wide = pltpu.VMEM((steps, depth, 2 * width) if aligned else (2, depth, width), BF16)
    wide_sem, low_sem = pltpu.SemaphoreType.DMA((steps, 2)), pltpu.SemaphoreType.DMA((n_head,))
    outs = [struct((nx, count, part), BF16), struct((n_head - nx, count, part), BF16)]
    hidden = struct((count, units), BF16)
    work = 2 * count * depth * units
    hidden, low = local_call(
        functools.partial(hidden_kernel, n_head, steps, aligned),
        "hidden",
        [hidden, struct((n_head, units, part), BF16)],
        2 * work,
        owners,
        *pieces,
        gate_weight,
        up_weight,
        down_weight,
        scratch=[rows, wide, wide_sem, low_sem],
        scalars=1,
        far=3,
        vmem=EXPERT_VMEM,
    )
    hidden = lax.optimization_barrier((hidden, before_down))[0]
    return local_call(
        down_kernel,
        "down",
        outs,
        work,
        hidden,
        low,
        vmem=EXPERT_VMEM,
    )


def local_call(
    kernel, name, out_shape, flops, *operands, scratch=(), scalars=0, far=0, vmem=SMALL_VMEM
):
    shapes = out_shape if isinstance(out_shape, list) else [out_shape]
    sizes = [math.prod(o.shape) * o.dtype.itemsize for o in [*operands, *shapes]]
    return pl.pallas_call(
        kernel,
        out_shape=out_shape,
        in_specs=[pl.BlockSpec(memory_space=pltpu.SMEM)] * scalars
        + [pl.BlockSpec(memory_space=pltpu.VMEM)] * (len(operands) - scalars - far)
        + [pl.BlockSpec(memory_space=pltpu.HBM)] * far,
        scratch_shapes=list(scratch),
        compiler_params=pltpu.CompilerParams(vmem_limit_bytes=vmem),
        cost_estimate=pl.CostEstimate(flops=flops, bytes_accessed=sum(sizes), transcendentals=0),
        name=name,
    )(*operands)


def plan_kernel(capacity, me_ref, ids_ref, routing_ref, weights_ref, take_ref, mix_ref):
    tokens, slots = take_ref.shape
    experts = slots // capacity
    row = lax.broadcasted_iota(jnp.int32, (tokens, tokens), 0)
    col = lax.broadcasted_iota(jnp.int32, (tokens, tokens), 1)
    before = (col < row).astype(BF16)
    expert = lax.broadcasted_iota(jnp.int32, (tokens, experts), 1)
    slot = lax.broadcasted_iota(jnp.int32, (tokens, slots), 1)

    def found(ids):
        hits = [(expert == one).astype(F32) for one in ids]
        earlier = jnp.dot(before, (hits[0] + hits[1]).astype(BF16), preferred_element_type=F32)
        ranks = [jnp.sum(earlier * hit, axis=1, keepdims=True).astype(jnp.int32) for hit in hits]
        return [slot == (one ^ me_ref[0]) * capacity + rank for one, rank in zip(ids, ranks)]

    there = ids_ref[...].astype(F32).astype(jnp.int32)
    first, second = found([there[:, :1], there[:, 1:2]])
    take_ref[...] = (first | second).astype(F32).astype(BF16)
    first, second = found([routing_ref[:, :1], routing_ref[:, 1:2]])
    weights = weights_ref[...]
    mix_ref[...] = jnp.where(first, weights[:, :1], 0.0) + jnp.where(second, weights[:, 1:2], 0.0)


def shards(
    queries,
    key_vectors,
    value_vectors,
    log_decay,
    doc_ids,
    head_gain,
    output_weight,
    residual,
    norm_gain,
    routing,
    route_weights,
    gate_weight,
    up_weight,
    down_weight,
):
    tokens, heads = log_decay.shape
    hw = queries.shape[1] // heads
    n_seq, n_head = lax.axis_size("seq"), lax.axis_size("head")
    ny, nz, nx = n_seq // n_head, n_head, n_head // CORES
    s, h = lax.axis_index("seq"), lax.axis_index("head")
    z, y = s // ny, s % ny
    x, c = h // CORES, h % CORES
    part = residual.shape[1]
    model_width = part * n_head

    struct = jax.ShapeDtypeStruct
    spots = [
        ((zz * ny + yy) * n_head + hh, (hh * ny + yy) * n_head + zz)
        for zz in range(nz)
        for yy in range(ny)
        for hh in range(n_head)
    ]
    crossed = lambda value: lax.ppermute(value, ("seq", "head"), spots)

    experts = n_seq
    capacity = 4 * tokens // experts
    me = s.astype(jnp.int32).reshape(1)
    doc_row = doc_ids.reshape(1, tokens)
    rows, held, extra = chunk_plan(heads, hw, n_seq)
    work = 2 * tokens * hw * hw * heads
    *payload, decay_sum, decay_rows, doc_float, keys_near, values_near = local_call(
        state_kernel,
        "block_state",
        [struct((rows + extra, hw), BF16)] * n_seq
        + [struct((tokens, heads), F32), struct((heads, tokens), F32), struct((1, tokens), F32)]
        + [struct((tokens, heads * hw), BF16)] * 2,
        work,
        me,
        doc_row,
        log_decay.T,
        key_vectors,
        value_vectors,
        scratch=[pltpu.VMEM((hw, hw), F32)],
        scalars=1,
    )
    residual_there = crossed(residual)
    arrived, residual_there = lax.optimization_barrier((swap_seq(payload), residual_there))
    entered = local_call(
        scan_kernel,
        "carry",
        [struct((rows, hw), BF16)] * n_seq,
        work,
        me,
        *arrived,
        scratch=[
            pltpu.VMEM((n_seq, rows + extra, hw), BF16),
            pltpu.VMEM((n_seq, rows, hw), BF16),
        ],
        scalars=1,
    )
    carried, output_weight = lax.optimization_barrier((swap_seq(entered), output_weight))
    attended = local_call(
        attend_kernel,
        "attend",
        struct((tokens, heads * hw), BF16),
        3 * work,
        me,
        doc_float,
        decay_sum,
        decay_rows,
        queries,
        keys_near,
        values_near,
        head_gain.reshape(1, heads * hw),
        *carried,
        scratch=[pltpu.VMEM((heads * hw, hw), BF16)],
        scalars=1,
    )

    ids = jnp.pad(routing.astype(BF16), ((0, 0), (0, 128 - routing.shape[1])))
    ids = crossed(lax.optimization_barrier((ids, attended))[0])
    cols = output_weight.shape[1]
    w_z = jnp.zeros((output_weight.shape[0], ny * cols), BF16)
    w_z = lax.dynamic_update_slice(w_z, output_weight, (0, y * cols))
    for k in range(1, ny):
        got = permute_seq(output_weight, lambda q, k=k: q // ny * ny + (q % ny - k) % ny)
        w_z = lax.dynamic_update_slice(w_z, got, (0, (y + k) % ny * cols))

    def along(value, pairs):
        perm = [(a * ny + yy, b * ny + yy) for a, b in pairs for yy in range(ny)]
        return lax.ppermute(value, "seq", perm)

    ups = lambda j: [(q, q + j) for q in range(nz - j)]
    downs = lambda j: [(q + j, q) for q in range(nz - j)]
    below, above = along(attended, ups(1)), along(attended, downs(1))
    take, mix = local_call(
        functools.partial(plan_kernel, capacity),
        "plan",
        [struct((tokens, experts * capacity), BF16), struct((tokens, experts * capacity), F32)],
        4 * tokens * tokens * experts,
        me,
        ids,
        routing,
        route_weights,
        scalars=1,
    )
    shifts, rows_of = [(0, 0), (1, 0), (0, 1)], [attended, below, above]
    if nz > 2:
        shifts += [(2, 0), (0, 2)]
        rows_of += [along(below, ups(1)), along(above, downs(1))]
    for j in range(3, nz):
        if 2 * j >= nz:
            shifts.append((j, j))
            rows_of.append(along(attended, ups(j) + downs(j)))
        else:
            shifts += [(j, 0), (0, j)]
            rows_of += [along(attended, ups(j)), along(attended, downs(j))]
    products = [jnp.dot(r, w_z, preferred_element_type=F32).astype(BF16) for r in rows_of]
    products, take, mix = lax.optimization_barrier((products, take, mix))
    block = struct((tokens, part), BF16)
    place_me = jnp.stack([z, h]).astype(jnp.int32)
    own, *sent = local_call(
        functools.partial(route_kernel, shifts),
        "route",
        [block] * n_head,
        tokens * part,
        place_me,
        *products,
        scratch=[pltpu.VMEM((nz, tokens, part), BF16)],
        scalars=1,
    )
    sums = [own]
    for m in range(1, n_head):
        sums.append(permute_head(sent[m - 1], lambda q, m=m: (q + m) % n_head))
    middle_there, *outgoing = local_call(
        functools.partial(dispatch_kernel, n_head),
        "dispatch",
        [block] + [struct((capacity, part), BF16)] * experts,
        2 * tokens * tokens * 4 * part,
        residual_there,
        take,
        *sums,
    )

    in_owner = [h] + [(h + m * CORES) % n_head for m in range(1, nx)]
    in_owner += [
        o // CORES * CORES + (o % CORES + m) % CORES for o in in_owner for m in range(1, CORES)
    ]
    out_owner = [
        (x + m) % nx * CORES + (c + k) % CORES for k in [*range(1, CORES), 0] for m in range(nx)
    ]
    owners = jnp.stack(in_owner + out_owner + [z]).astype(jnp.int32)
    count = n_head * capacity
    returning = [None] * experts
    arrived = None
    gots, fars = [], []
    for group in range(ny):
        sends = [outgoing[k * ny + group] for k in range(nz)]
        if group:
            sends = lax.optimization_barrier((sends, arrived))[0]
        arrived = [
            permute_seq(sends[k], lambda q, d=k * ny + group: q ^ d) if k + group else sends[k]
            for k in reversed(range(nz))
        ]
        arrived = lax.optimization_barrier(arrived)[::-1]
        got = local_call(
            pack_kernel,
            "pack",
            struct((capacity, model_width), BF16),
            count * part,
            z.astype(jnp.int32).reshape(1),
            norm_gain.reshape(1, model_width),
            *arrived,
            scalars=1,
        )
        gots.append(got)
        fars.append(
            [permute_head(got, lambda q, m=m: (q - m * CORES) % n_head) for m in range(1, nx)]
        )
    for group in range(ny):
        got, far = gots[group], fars[group]
        if group + 1 < ny:
            far = lax.optimization_barrier((far, gots[group + 1]))[0]
        pieces = [got, *far]
        for piece in [got, *far]:
            for m in range(1, CORES):
                pieces.append(
                    permute_head(
                        piece, lambda q, m=m: q // CORES * CORES + (q % CORES - m) % CORES
                    )
                )
        first = [blocks, middle] if group else None
        if group + 1 < ny:
            first = (first, fars[group + 1])
        if group:
            pieces = lax.optimization_barrier((pieces, crossing))[0]
        sent, kept = expert_call(owners, pieces, gate_weight, up_weight, down_weight, first)
        if group == 0:
            middle = crossed(lax.optimization_barrier((middle_there, sent))[0])

        near = permute_head(sent, lambda q: q // CORES * CORES + (q % CORES + 1) % CORES)
        near_sum = kept.astype(F32) + near.astype(F32)
        crossing = [near_sum[m].astype(BF16) for m in range(1, nx)]
        parts = [near_sum[0]]
        for m in range(1, nx):
            parts.append(permute_head(crossing[m - 1], lambda q, m=m: (q + m * CORES) % n_head))
        blocks = local_call(
            functools.partial(sum_kernel, nz),
            "total",
            [struct((capacity, part), BF16)] * nz,
            count * part * nx,
            z.astype(jnp.int32).reshape(1),
            *parts,
            scratch=[pltpu.VMEM((count, part), BF16)],
            scalars=1,
        )
        for k in range(nz):
            returning[k * ny + group] = blocks[k]
    return local_call(
        mix_kernel,
        "mix",
        block,
        4 * tokens * experts * capacity * part,
        middle,
        mix,
        *swap_seq(returning),
        scratch=[pltpu.VMEM((experts * capacity, part), BF16)],
    )


def solution(mesh):
    placed = (
        P("seq", "head"),
        P("seq", "head"),
        P("seq", "head"),
        P("seq", "head"),
        P("seq"),
        P("head"),
        P("head", "seq"),
        P("seq", "head"),
        P(),
        P("seq", None),
        P("seq", None),
        P("seq", None, "head"),
        P("seq", None, "head"),
        P("seq", "head", None),
    )
    return jax.shard_map(
        shards, mesh=mesh, in_specs=placed, out_specs=P("seq", "head"), check_vma=False
    )
```

```python
import functools
import math

import jax
import jax.numpy as jnp
from jax import lax
from jax.experimental import pallas as pl
from jax.experimental.pallas import tpu as pltpu
from jax.sharding import PartitionSpec as P

EPSILON = 1e-06
CORES = 2
F32 = jnp.float32
BF16 = jnp.bfloat16
HIGHEST = lax.Precision.HIGHEST
SMALL_VMEM = 12 * 1024 * 1024
EXPERT_VMEM = 42 * 1024 * 1024


def permute_seq(value, move):
    count = lax.axis_size("seq")
    return lax.ppermute(value, "seq", [(source, move(source)) for source in range(count)])


def permute_head(value, move):
    count = lax.axis_size("head")
    return lax.ppermute(value, "head", [(source, move(source)) for source in range(count)])


def swap_seq(blocks, far_first=True):
    half = len(blocks) // 2
    order = [*range(2, min(3, half)), *reversed(range(half, len(blocks))), *range(3, half)]
    order += [d for d in range(1, len(blocks)) if d not in order]
    order = order if far_first else list(range(1, len(blocks)))
    swapped = [permute_seq(blocks[d], lambda q, d=d: q ^ d) for d in order]
    swapped = dict(zip(order, lax.optimization_barrier(swapped)))
    return [blocks[0]] + [swapped[d] for d in range(1, len(blocks))]


def pick(stack, index, axis=0):
    return lax.dynamic_index_in_dim(stack, index, axis, keepdims=False)


def doc_column(doc):
    count = doc.shape[1]
    return jnp.broadcast_to(doc, (count, count)).T


def chunk_plan(heads, hw, n_seq):
    rows = heads * hw // n_seq
    held = max(1, rows // hw)
    extra = -(-(2 * held + 2) // 16) * 16
    return rows, held, extra


def state_kernel(me_ref, doc_ref, decay_ref, k_ref, v_ref, *refs):
    outs, refs = refs[:-6], refs[-6:]
    sum_ref, sum_rows_ref, doc_out_ref, k_out_ref, v_out_ref, state_ref = refs
    k_out_ref[...] = k_ref[...]
    v_out_ref[...] = v_ref[...]
    heads, tokens = decay_ref.shape
    n_seq, hw = len(outs), outs[0].shape[1]
    rows, held, extra = chunk_plan(heads, hw, n_seq)
    doc = doc_ref[...].astype(F32)
    row = lax.broadcasted_iota(jnp.int32, (tokens, tokens), 0)
    col = lax.broadcasted_iota(jnp.int32, (tokens, tokens), 1)
    doc_out_ref[...] = doc
    sums = lax.dot_general(
        (col <= row).astype(F32),
        decay_ref[...],
        (((1,), (1,)), ((), ())),
        precision=HIGHEST,
        preferred_element_type=F32,
    )
    sum_ref[...] = sums
    sum_rows_ref[...] = jnp.dot(
        decay_ref[...], (row <= col).astype(F32), precision=HIGHEST, preferred_element_type=F32
    )
    final = sums[tokens - 1 :, :]
    last = doc[:, tokens - 1 :]
    tail = jnp.exp(final - sums) * (doc_column(doc)[:, :1] == last).astype(F32)
    gain = jnp.exp(final) * (doc[:, :1] == last).astype(F32)
    lane = lax.broadcasted_iota(jnp.int32, (1, heads), 1)
    line = lax.broadcasted_iota(jnp.int32, (extra, hw), 0)
    for d in reversed(range(n_seq)):
        chunk = me_ref[0] ^ d
        note = jnp.where(line == 2 * held, doc[:, :1], 0.0)
        note = jnp.where(line == 2 * held + 1, last, note)
        for j in range(held):
            i = chunk * rows // hw + j
            mine = (lane == i).astype(F32)
            lanes = pl.ds(pl.multiple_of(i * hw, 128), hw)
            fade = jnp.sum(tail * mine, axis=1, keepdims=True)
            faded = (k_ref[:, lanes].astype(F32) * fade).astype(BF16)
            state = lax.dot_general(
                faded, v_ref[:, lanes], (((0,), (0,)), ((), ())), preferred_element_type=F32
            )
            if rows >= hw:
                outs[d][j * hw : (j + 1) * hw, :] = state.astype(BF16)
            else:
                state_ref[...] = state
                start = pl.multiple_of(chunk % (hw // rows) * rows, rows)
                outs[d][:rows, :] = state_ref[pl.ds(start, rows), :].astype(BF16)
            whole = jnp.sum(gain * mine, axis=1, keepdims=True)
            high = whole.astype(BF16).astype(F32)
            note = jnp.where(line == j, high, note)
            note = jnp.where(line == held + j, whole - high, note)
        outs[d][rows:, :] = note.astype(BF16)


def scan_kernel(me_ref, *refs):
    n_seq = (len(refs) - 2) // 2
    ins, outs, blocks_ref, entered_ref = refs[:n_seq], refs[n_seq:-2], refs[-2], refs[-1]
    _, rows, hw = entered_ref.shape
    held = max(1, rows // hw)
    part = rows // held
    for d in range(n_seq):
        blocks_ref[me_ref[0] ^ d] = ins[d][...]
    for j in range(held):
        running = jnp.zeros((part, hw), F32)
        entered_ref[0, j * part : (j + 1) * part, :] = running.astype(BF16)
        for b in range(1, n_seq):
            notes = blocks_ref[b - 1, rows:, :].astype(F32)
            gain = notes[j : j + 1] + notes[held + j : held + j + 1]
            first = blocks_ref[b, rows:, :].astype(F32)[2 * held : 2 * held + 1]
            joined = (first == notes[2 * held + 1 : 2 * held + 2]).astype(F32)
            state = blocks_ref[b - 1, j * part : (j + 1) * part, :].astype(F32)
            running = (state + gain * running) * joined
            entered_ref[b, j * part : (j + 1) * part, :] = running.astype(BF16)
    for d in range(n_seq):
        outs[d][...] = entered_ref[me_ref[0] ^ d]


def attend_kernel(
    me_ref, doc_ref, sum_ref, sum_rows_ref, q_ref, k_ref, v_ref, gain_ref, *refs
):
    ins, out_ref, carried_ref = refs[:-2], refs[-2], refs[-1]
    tokens, heads = sum_ref.shape
    hw = q_ref.shape[1] // heads
    rows = ins[0].shape[0]
    for d in range(len(ins)):
        start = pl.multiple_of((me_ref[0] ^ d) * rows, rows)
        carried_ref[pl.ds(start, rows), :] = ins[d][...]
    doc = doc_ref[...]
    column = doc_column(doc)
    row = lax.broadcasted_iota(jnp.int32, (tokens, tokens), 0)
    col = lax.broadcasted_iota(jnp.int32, (tokens, tokens), 1)
    kept = (col <= row) & (column == doc)
    reach = jnp.exp(sum_ref[...]) * (column[:, :1] == doc[:, :1]).astype(F32)
    for i in range(heads):
        lanes = slice(i * hw, (i + 1) * hw)
        gap = sum_ref[:, i : i + 1] - sum_rows_ref[i : i + 1, :]
        fade = jnp.where(kept, jnp.exp(jnp.minimum(gap, 0.0)), 0.0)
        scores = lax.dot_general(
            q_ref[:, lanes], k_ref[:, lanes], (((1,), (1,)), ((), ())), preferred_element_type=F32
        )
        raw = jnp.dot((scores * fade).astype(BF16), v_ref[:, lanes], preferred_element_type=F32)
        outside = jnp.dot(q_ref[:, lanes], carried_ref[lanes, :], preferred_element_type=F32)
        raw = raw + outside * reach[:, i : i + 1]
        scale = lax.rsqrt(jnp.mean(raw * raw, axis=1, keepdims=True) + EPSILON)
        out_ref[:, lanes] = (raw * scale * gain_ref[:, lanes]).astype(BF16)


def pack_kernel(me_ref, gain_ref, *refs):
    ins, out_ref = refs[:-1], refs[-1]
    part, depth = ins[0].shape[1], out_ref.shape[1]
    squares = 0.0
    for ref in ins:
        value = ref[...].astype(F32)
        squares = squares + jnp.sum(value * value, axis=1, keepdims=True)
    scale = lax.rsqrt(squares / depth + EPSILON)
    for k, ref in enumerate(ins):
        lanes = pl.ds(pl.multiple_of((me_ref[0] ^ k) * part, 128), part)
        out_ref[:, lanes] = (ref[...].astype(F32) * scale * gain_ref[:, lanes]).astype(BF16)


def route_kernel(shifts, me_ref, *refs):
    ins, outs, stage_ref = refs[: len(shifts)], refs[len(shifts) : -1], refs[-1]
    count, me = len(outs), me_ref[0]
    for (up, down), ref in zip(shifts, ins):
        if not up and not down:
            stage_ref[me] = ref[...]
        if up:

            @pl.when(me >= up)
            def _(up=up, ref=ref):
                stage_ref[me - up] = ref[...]

        if down:

            @pl.when(me < count - down)
            def _(down=down, ref=ref):
                stage_ref[me + down] = ref[...]

    for m in range(count):
        outs[m][...] = stage_ref[(me_ref[1] + m) % count]


def dispatch_kernel(n_head, residual_ref, take_ref, *refs):
    total = residual_ref[...].astype(F32)
    sums = refs[0][...].astype(F32)
    for ref in refs[1:n_head]:
        sums = sums + ref[...].astype(F32)
    middle_ref, outs = refs[n_head], refs[n_head + 1 :]
    middle = (total + sums).astype(BF16)
    middle_ref[...] = middle
    count = outs[0].shape[0]
    rows = lax.dot_general(
        take_ref[...], middle, (((0,), (0,)), ((), ())), preferred_element_type=F32
    ).astype(BF16)
    for d in range(len(outs)):
        outs[d][...] = rows[d * count : (d + 1) * count]


def sum_kernel(nz, me_ref, *refs):
    ins, outs, stage_ref = refs[: len(refs) - 1 - nz], refs[len(refs) - 1 - nz : -1], refs[-1]
    total = ins[0][...].astype(F32)
    for ref in ins[1:]:
        total = total + ref[...].astype(F32)
    stage_ref[...] = total.astype(BF16)
    count = outs[0].shape[0]
    for k in range(nz):
        start = pl.multiple_of((me_ref[0] ^ k) * count, count)
        outs[k][...] = stage_ref[pl.ds(start, count), :]


def mix_kernel(middle_ref, mix_ref, *refs):
    ins, out_ref, rows_ref = refs[:-2], refs[-2], refs[-1]
    count = ins[0].shape[0]
    for d in range(len(ins)):
        rows_ref[d * count : (d + 1) * count, :] = ins[d][...]
    mix = mix_ref[...]
    high = mix.astype(BF16)
    low = (mix - high.astype(F32)).astype(BF16)
    rows = rows_ref[...]
    total = jnp.dot(high, rows, preferred_element_type=F32)
    total = total + jnp.dot(low, rows, preferred_element_type=F32)
    out_ref[...] = (middle_ref[...].astype(F32) + total).astype(BF16)


def wide_copies(gate_ref, up_ref, wide_ref, sems, steps, aligned):
    width = gate_ref.shape[2] // steps
    copies = []
    for j in range(steps):
        for k, weight in enumerate((gate_ref, up_ref)):
            source, target = weight.at[0], wide_ref.at[k]
            if aligned:
                source = weight.at[0, :, pl.ds(j * width, width)]
                target = wide_ref.at[j, :, pl.ds(k * width, width)]
            copies.append(pltpu.make_async_copy(source, target, sems.at[j, k]))
    return copies


def low_copies(n_head, owner_ref, down_ref, low_ref, sems):
    part = low_ref.shape[2]
    copies = []
    for j in range(n_head):
        start = pl.multiple_of(owner_ref[n_head + j] * part, 128)
        source = down_ref.at[0, :, pl.ds(start, part)]
        copies.append(pltpu.make_async_copy(source, low_ref.at[j], sems.at[j]))
    return copies


def fill_hidden(aligned, owner_ref, pieces, rows_ref, wide_ref, hidden_ref, copies):
    steps = len(copies) // 2
    width = hidden_ref.shape[1] // steps
    count = pieces[0].shape[0]
    for i, piece in enumerate(pieces):
        lines = pl.ds(pl.multiple_of(owner_ref[i] * count, count), count)
        rows_ref[lines, :] = piece[...]
    for j in range(steps):
        copies[2 * j].wait()
        copies[2 * j + 1].wait()
        if aligned:
            both = jnp.dot(rows_ref[...], wide_ref[j], preferred_element_type=F32)
            gate, up = both[:, :width], both[:, width:]
        else:
            gate = jnp.dot(rows_ref[...], wide_ref[0], preferred_element_type=F32)
            up = jnp.dot(rows_ref[...], wide_ref[1], preferred_element_type=F32)
        hidden = (gate / (1.0 + jnp.exp(-gate)) * up).astype(BF16)
        hidden_ref[:, j * width : (j + 1) * width] = hidden


def hidden_kernel(n_head, steps, aligned, owner_ref, *refs):
    pieces = refs[:n_head]
    gate_ref, up_ref, down_ref, hidden_ref, low_ref = refs[n_head : n_head + 5]
    rows_ref, wide_ref, wide_sem, low_sem = refs[n_head + 5 :]
    wide = wide_copies(gate_ref, up_ref, wide_ref, wide_sem, steps, aligned)
    low = low_copies(n_head, owner_ref, down_ref, low_ref, low_sem)
    for copy in wide + low:
        copy.start()
    fill_hidden(aligned, owner_ref, pieces, rows_ref, wide_ref, hidden_ref, wide)
    for copy in low:
        copy.wait()


def down_kernel(hidden_ref, low_ref, sent_ref, kept_ref):
    nx = sent_ref.shape[0]
    for j in range(low_ref.shape[0]):
        out = jnp.dot(hidden_ref[...], low_ref[j], preferred_element_type=F32).astype(BF16)
        if j < nx:
            sent_ref[j] = out
        else:
            kept_ref[j - nx] = out


def expert_call(owners, pieces, gate_weight, up_weight, down_weight, before_down):
    n_head = len(pieces)
    _, depth, units = gate_weight.shape
    count, part = pieces[0].shape[0] * n_head, depth // n_head
    width = next((w for w in (384, 256, 128) if units % w == 0), units)
    aligned = width % 128 == 0
    steps, nx = units // width, n_head // CORES
    struct = jax.ShapeDtypeStruct
    rows = pltpu.VMEM((count, depth), BF16)
    wide = pltpu.VMEM((steps, depth, 2 * width) if aligned else (2, depth, width), BF16)
    wide_sem, low_sem = pltpu.SemaphoreType.DMA((steps, 2)), pltpu.SemaphoreType.DMA((n_head,))
    outs = [struct((nx, count, part), BF16), struct((n_head - nx, count, part), BF16)]
    hidden = struct((count, units), BF16)
    work = 2 * count * depth * units
    hidden, low = local_call(
        functools.partial(hidden_kernel, n_head, steps, aligned),
        "hidden",
        [hidden, struct((n_head, units, part), BF16)],
        2 * work,
        owners,
        *pieces,
        gate_weight,
        up_weight,
        down_weight,
        scratch=[rows, wide, wide_sem, low_sem],
        scalars=1,
        far=3,
        vmem=EXPERT_VMEM,
    )
    hidden = lax.optimization_barrier((hidden, before_down))[0]
    return local_call(
        down_kernel,
        "down",
        outs,
        work,
        hidden,
        low,
        vmem=EXPERT_VMEM,
    )


def local_call(
    kernel, name, out_shape, flops, *operands, scratch=(), scalars=0, far=0, vmem=SMALL_VMEM
):
    shapes = out_shape if isinstance(out_shape, list) else [out_shape]
    sizes = [math.prod(o.shape) * o.dtype.itemsize for o in [*operands, *shapes]]
    return pl.pallas_call(
        kernel,
        out_shape=out_shape,
        in_specs=[pl.BlockSpec(memory_space=pltpu.SMEM)] * scalars
        + [pl.BlockSpec(memory_space=pltpu.VMEM)] * (len(operands) - scalars - far)
        + [pl.BlockSpec(memory_space=pltpu.HBM)] * far,
        scratch_shapes=list(scratch),
        compiler_params=pltpu.CompilerParams(vmem_limit_bytes=vmem),
        cost_estimate=pl.CostEstimate(flops=flops, bytes_accessed=sum(sizes), transcendentals=0),
        name=name,
    )(*operands)


def plan_kernel(capacity, me_ref, ids_ref, routing_ref, weights_ref, take_ref, mix_ref):
    tokens, slots = take_ref.shape
    experts = slots // capacity
    row = lax.broadcasted_iota(jnp.int32, (tokens, tokens), 0)
    col = lax.broadcasted_iota(jnp.int32, (tokens, tokens), 1)
    before = (col < row).astype(BF16)
    expert = lax.broadcasted_iota(jnp.int32, (tokens, experts), 1)
    slot = lax.broadcasted_iota(jnp.int32, (tokens, slots), 1)

    def found(ids):
        hits = [(expert == one).astype(F32) for one in ids]
        earlier = jnp.dot(before, (hits[0] + hits[1]).astype(BF16), preferred_element_type=F32)
        ranks = [jnp.sum(earlier * hit, axis=1, keepdims=True).astype(jnp.int32) for hit in hits]
        return [slot == (one ^ me_ref[0]) * capacity + rank for one, rank in zip(ids, ranks)]

    there = ids_ref[...].astype(F32).astype(jnp.int32)
    first, second = found([there[:, :1], there[:, 1:2]])
    take_ref[...] = (first | second).astype(F32).astype(BF16)
    first, second = found([routing_ref[:, :1], routing_ref[:, 1:2]])
    weights = weights_ref[...]
    mix_ref[...] = jnp.where(first, weights[:, :1], 0.0) + jnp.where(second, weights[:, 1:2], 0.0)


def shards(
    queries,
    key_vectors,
    value_vectors,
    log_decay,
    doc_ids,
    head_gain,
    output_weight,
    residual,
    norm_gain,
    routing,
    route_weights,
    gate_weight,
    up_weight,
    down_weight,
):
    tokens, heads = log_decay.shape
    hw = queries.shape[1] // heads
    n_seq, n_head = lax.axis_size("seq"), lax.axis_size("head")
    ny, nz, nx = n_seq // n_head, n_head, n_head // CORES
    s, h = lax.axis_index("seq"), lax.axis_index("head")
    z, y = s // ny, s % ny
    x, c = h // CORES, h % CORES
    part = residual.shape[1]
    model_width = part * n_head

    struct = jax.ShapeDtypeStruct
    spots = [
        ((zz * ny + yy) * n_head + hh, (hh * ny + yy) * n_head + zz)
        for zz in range(nz)
        for yy in range(ny)
        for hh in range(n_head)
    ]
    crossed = lambda value: lax.ppermute(value, ("seq", "head"), spots)

    experts = n_seq
    capacity = 4 * tokens // experts
    me = s.astype(jnp.int32).reshape(1)
    doc_row = doc_ids.reshape(1, tokens)
    rows, held, extra = chunk_plan(heads, hw, n_seq)
    work = 2 * tokens * hw * hw * heads
    *payload, decay_sum, decay_rows, doc_float, keys_near, values_near = local_call(
        state_kernel,
        "block_state",
        [struct((rows + extra, hw), BF16)] * n_seq
        + [struct((tokens, heads), F32), struct((heads, tokens), F32), struct((1, tokens), F32)]
        + [struct((tokens, heads * hw), BF16)] * 2,
        work,
        me,
        doc_row,
        log_decay.T,
        key_vectors,
        value_vectors,
        scratch=[pltpu.VMEM((hw, hw), F32)],
        scalars=1,
    )
    residual_there = crossed(residual)
    arrived, residual_there = lax.optimization_barrier((swap_seq(payload, far_first=False), residual_there))
    entered = local_call(
        scan_kernel,
        "carry",
        [struct((rows, hw), BF16)] * n_seq,
        work,
        me,
        *arrived,
        scratch=[
            pltpu.VMEM((n_seq, rows + extra, hw), BF16),
            pltpu.VMEM((n_seq, rows, hw), BF16),
        ],
        scalars=1,
    )
    carried, output_weight = lax.optimization_barrier((swap_seq(entered), output_weight))
    attended = local_call(
        attend_kernel,
        "attend",
        struct((tokens, heads * hw), BF16),
        3 * work,
        me,
        doc_float,
        decay_sum,
        decay_rows,
        queries,
        keys_near,
        values_near,
        head_gain.reshape(1, heads * hw),
        *carried,
        scratch=[pltpu.VMEM((heads * hw, hw), BF16)],
        scalars=1,
    )

    ids = jnp.pad(routing.astype(BF16), ((0, 0), (0, 128 - routing.shape[1])))
    ids = crossed(lax.optimization_barrier((ids, attended))[0])
    cols = output_weight.shape[1]
    w_z = jnp.zeros((output_weight.shape[0], ny * cols), BF16)
    w_z = lax.dynamic_update_slice(w_z, output_weight, (0, y * cols))
    for k in range(1, ny):
        got = permute_seq(output_weight, lambda q, k=k: q // ny * ny + (q % ny - k) % ny)
        w_z = lax.dynamic_update_slice(w_z, got, (0, (y + k) % ny * cols))

    def along(value, pairs):
        perm = [(a * ny + yy, b * ny + yy) for a, b in pairs for yy in range(ny)]
        return lax.ppermute(value, "seq", perm)

    ups = lambda j: [(q, q + j) for q in range(nz - j)]
    downs = lambda j: [(q + j, q) for q in range(nz - j)]
    below, above = along(attended, ups(1)), along(attended, downs(1))
    take, mix = local_call(
        functools.partial(plan_kernel, capacity),
        "plan",
        [struct((tokens, experts * capacity), BF16), struct((tokens, experts * capacity), F32)],
        4 * tokens * tokens * experts,
        me,
        ids,
        routing,
        route_weights,
        scalars=1,
    )
    shifts, rows_of = [(0, 0), (1, 0), (0, 1)], [attended, below, above]
    if nz > 2:
        shifts += [(2, 0), (0, 2)]
        rows_of += [along(below, ups(1)), along(above, downs(1))]
    for j in range(3, nz):
        if 2 * j >= nz:
            shifts.append((j, j))
            rows_of.append(along(attended, ups(j) + downs(j)))
        else:
            shifts += [(j, 0), (0, j)]
            rows_of += [along(attended, ups(j)), along(attended, downs(j))]
    products = [jnp.dot(r, w_z, preferred_element_type=F32).astype(BF16) for r in rows_of]
    products, take, mix = lax.optimization_barrier((products, take, mix))
    block = struct((tokens, part), BF16)
    place_me = jnp.stack([z, h]).astype(jnp.int32)
    own, *sent = local_call(
        functools.partial(route_kernel, shifts),
        "route",
        [block] * n_head,
        tokens * part,
        place_me,
        *products,
        scratch=[pltpu.VMEM((nz, tokens, part), BF16)],
        scalars=1,
    )
    sums = [own]
    for m in range(1, n_head):
        sums.append(permute_head(sent[m - 1], lambda q, m=m: (q + m) % n_head))
    middle_there, *outgoing = local_call(
        functools.partial(dispatch_kernel, n_head),
        "dispatch",
        [block] + [struct((capacity, part), BF16)] * experts,
        2 * tokens * tokens * 4 * part,
        residual_there,
        take,
        *sums,
    )

    in_owner = [h] + [(h + m * CORES) % n_head for m in range(1, nx)]
    in_owner += [
        o // CORES * CORES + (o % CORES + m) % CORES for o in in_owner for m in range(1, CORES)
    ]
    out_owner = [
        (x + m) % nx * CORES + (c + k) % CORES for k in [*range(1, CORES), 0] for m in range(nx)
    ]
    owners = jnp.stack(in_owner + out_owner + [z]).astype(jnp.int32)
    count = n_head * capacity
    returning = [None] * experts
    arrived = None
    gots, fars = [], []
    for group in range(ny):
        sends = [outgoing[k * ny + group] for k in range(nz)]
        if group:
            sends = lax.optimization_barrier((sends, arrived))[0]
        arrived = [
            permute_seq(sends[k], lambda q, d=k * ny + group: q ^ d) if k + group else sends[k]
            for k in reversed(range(nz))
        ]
        arrived = lax.optimization_barrier(arrived)[::-1]
        got = local_call(
            pack_kernel,
            "pack",
            struct((capacity, model_width), BF16),
            count * part,
            z.astype(jnp.int32).reshape(1),
            norm_gain.reshape(1, model_width),
            *arrived,
            scalars=1,
        )
        gots.append(got)
        fars.append(
            [permute_head(got, lambda q, m=m: (q - m * CORES) % n_head) for m in range(1, nx)]
        )
    for group in range(ny):
        got, far = gots[group], fars[group]
        if group + 1 < ny:
            far = lax.optimization_barrier((far, gots[group + 1]))[0]
        pieces = [got, *far]
        for piece in [got, *far]:
            for m in range(1, CORES):
                pieces.append(
                    permute_head(
                        piece, lambda q, m=m: q // CORES * CORES + (q % CORES - m) % CORES
                    )
                )
        first = [blocks, middle] if group else None
        if group + 1 < ny:
            first = (first, fars[group + 1])
        if group:
            pieces = lax.optimization_barrier((pieces, crossing))[0]
        sent, kept = expert_call(owners, pieces, gate_weight, up_weight, down_weight, first)
        if group == 0:
            middle = crossed(lax.optimization_barrier((middle_there, sent))[0])

        near = permute_head(sent, lambda q: q // CORES * CORES + (q % CORES + 1) % CORES)
        near_sum = kept.astype(F32) + near.astype(F32)
        crossing = [near_sum[m].astype(BF16) for m in range(1, nx)]
        parts = [near_sum[0]]
        for m in range(1, nx):
            parts.append(permute_head(crossing[m - 1], lambda q, m=m: (q + m * CORES) % n_head))
        blocks = local_call(
            functools.partial(sum_kernel, nz),
            "total",
            [struct((capacity, part), BF16)] * nz,
            count * part * nx,
            z.astype(jnp.int32).reshape(1),
            *parts,
            scratch=[pltpu.VMEM((count, part), BF16)],
            scalars=1,
        )
        for k in range(nz):
            returning[k * ny + group] = blocks[k]
    return local_call(
        mix_kernel,
        "mix",
        block,
        4 * tokens * experts * capacity * part,
        middle,
        mix,
        *swap_seq(returning),
        scratch=[pltpu.VMEM((experts * capacity, part), BF16)],
    )


def solution(mesh):
    placed = (
        P("seq", "head"),
        P("seq", "head"),
        P("seq", "head"),
        P("seq", "head"),
        P("seq"),
        P("head"),
        P("head", "seq"),
        P("seq", "head"),
        P(),
        P("seq", None),
        P("seq", None),
        P("seq", None, "head"),
        P("seq", None, "head"),
        P("seq", "head", None),
    )
    return jax.shard_map(
        shards, mesh=mesh, in_specs=placed, out_specs=P("seq", "head"), check_vma=False
    )
```
